32 devices in a mesh: dp: 8 (over z, y), tensor: 4 (over x, core).
Axes of the slice: x: 2, y: 2, z: 4, core: 2. Of those that a mesh axis runs over, the one named last changes fastest.
Arguments:
- tokens: bfloat16 [8192, 2560], P(('dp', 'tensor')), may hold values from -6 to 6
- cotangent: bfloat16 [8192, 2560], P(('dp', 'tensor')), may hold values from -6 to 6
- doc_lengths: int32 [8, 4], P('dp'), may hold values from 1 to 800, 1024 in all within a row
- query_weight: float32 [2560, 2560], P('dp', 'tensor'), may hold values from -0.125 to 0.125
- keyvalue_weight_full: float32 [2560, 2, 640], P('dp', None, 'tensor'), may hold values from -0.125 to 0.125
- output_weight: float32 [2560, 2560], P('dp', 'tensor'), may hold values from -0.625 to 0.625
- gating_weight: float32 [2560, 2, 7168], P('dp', None, 'tensor'), may hold values from -0.125 to 0.125
- down_weight: float32 [2560, 7168], P('dp', 'tensor'), may hold values from -0.125 to 0.125
- norm_gains: float32 [2, 2560], P(None, 'dp'), may hold values from 0.5 to 1.5
- first_query: float32 [4, 2560, 2560], P(None, 'dp', 'tensor'), may hold values from -64 to 64
- keyvalue_first_moment: float32 [4, 2560, 2, 640], P(None, 'dp', None, 'tensor'), may hold values from -80 to 80
- first_output: float32 [4, 2560, 2560], P(None, 'dp', 'tensor'), may hold values from -8 to 8
- first_gating: float32 [4, 2560, 2, 7168], P(None, 'dp', None, 'tensor'), may hold values from -16 to 16
- first_down: float32 [4, 2560, 7168], P(None, 'dp', 'tensor'), may hold values from -16 to 16
- first_gains: float32 [4, 2, 2560], P(None, None, 'dp'), may hold values from -48 to 48
- second_query: float32 [4, 2560, 2560], P(None, 'dp', 'tensor'), may hold values from 245.76 to 3276.8
- keyvalue_second_moment: float32 [4, 2560, 2, 640], P(None, 'dp', None, 'tensor'), may hold values from 389.12 to 5120
- second_output: float32 [4, 2560, 2560], P(None, 'dp', 'tensor'), may hold values from 3.8912 to 51.2
- second_gating: float32 [4, 2560, 2, 7168], P(None, 'dp', None, 'tensor'), may hold values from 22.528 to 294.912
- second_down: float32 [4, 2560, 7168], P(None, 'dp', 'tensor'), may hold values from 22.528 to 294.912
- second_gains: float32 [4, 2, 2560], P(None, None, 'dp'), may hold values from 139.264 to 1843.2
- moment_query: float32 [2560, 2560], P('dp', 'tensor'), may hold values from -0.015625 to 0.015625
- keyvalue_outer_momentum: float32 [2560, 2, 640], P('dp', None, 'tensor'), may hold values from -0.015625 to 0.015625
- moment_output: float32 [2560, 2560], P('dp', 'tensor'), may hold values from -0.0625 to 0.0625
- moment_gating: float32 [2560, 2, 7168], P('dp', None, 'tensor'), may hold values from -0.015625 to 0.015625
- moment_down: float32 [2560, 7168], P('dp', 'tensor'), may hold values from -0.015625 to 0.015625
- moment_gains: float32 [2, 2560], P(None, 'dp'), may hold values from -0.1875 to 0.1875
Outputs:
- block_output: bfloat16 [8192, 2560], P(('dp', 'tensor'))
- token_grad: bfloat16 [8192, 2560], P(('dp', 'tensor'))
- query_first: float32 [4, 2560, 2560], P(None, 'dp', 'tensor')
- query_second: float32 [4, 2560, 2560], P(None, 'dp', 'tensor')
- query_delta: float32 [2560, 2560], P('dp', 'tensor')
- query_moment: float32 [2560, 2560], P('dp', 'tensor')
- query_master: float32 [2560, 2560], P('dp', 'tensor')
- query_copy: bfloat16 [2560, 2560], P('dp', 'tensor')
- keyvalue_first: float32 [4, 2560, 2, 640], P(None, 'dp', None, 'tensor')
- keyvalue_second: float32 [4, 2560, 2, 640], P(None, 'dp', None, 'tensor')
- keyvalue_delta: float32 [2560, 2, 640], P('dp', None, 'tensor')
- keyvalue_moment: float32 [2560, 2, 640], P('dp', None, 'tensor')
- keyvalue_master: float32 [2560, 2, 640], P('dp', None, 'tensor')
- keyvalue_copy: bfloat16 [2560, 2, 640], P('dp', None, 'tensor')
- output_first: float32 [4, 2560, 2560], P(None, 'dp', 'tensor')
- output_second: float32 [4, 2560, 2560], P(None, 'dp', 'tensor')
- output_delta: float32 [2560, 2560], P('dp', 'tensor')
- output_moment: float32 [2560, 2560], P('dp', 'tensor')
- output_master: float32 [2560, 2560], P('dp', 'tensor')
- output_copy: bfloat16 [2560, 2560], P('dp', 'tensor')
- gating_first: float32 [4, 2560, 2, 7168], P(None, 'dp', None, 'tensor')
- gating_second: float32 [4, 2560, 2, 7168], P(None, 'dp', None, 'tensor')
- gating_delta: float32 [2560, 2, 7168], P('dp', None, 'tensor')
- gating_moment: float32 [2560, 2, 7168], P('dp', None, 'tensor')
- gating_master: float32 [2560, 2, 7168], P('dp', None, 'tensor')
- gating_copy: bfloat16 [2560, 2, 7168], P('dp', None, 'tensor')
- down_first: float32 [4, 2560, 7168], P(None, 'dp', 'tensor')
- down_second: float32 [4, 2560, 7168], P(None, 'dp', 'tensor')
- down_delta: float32 [2560, 7168], P('dp', 'tensor')
- down_moment: float32 [2560, 7168], P('dp', 'tensor')
- down_master: float32 [2560, 7168], P('dp', 'tensor')
- down_copy: bfloat16 [2560, 7168], P('dp', 'tensor')
- gains_first: float32 [4, 2, 2560], P(None, None, 'dp')
- gains_second: float32 [4, 2, 2560], P(None, None, 'dp')
- gains_delta: float32 [2, 2560], P(None, 'dp')
- gains_moment: float32 [2, 2560], P(None, 'dp')
- gains_master: float32 [2, 2560], P(None, 'dp')
- gains_copy: bfloat16 [2, 2560], P(None, 'dp')
The draws below stay inside these ranges and needn't reach their ends.
Inputs may be any that keep to these rules, and one draw needn't show every extreme that they name: `doc_lengths`: each row holds the lengths of the 4 documents packed in order into one sequence; they sum to 1024, and the longest of each row is exactly 800.
All inputs are finite; a program needn't handle non-finite values.
Results may differ from the reference program's by a relative error of at most 0.023.
Values may be sent and summed in bfloat16 or wider, within the bound.
No kernel may reach another device: no remote copies, remote signals or barrier semaphores. Data moves between devices by JAX's collectives and lax.ppermute only.
A program may use at most 384 MiB of HBM per device.

```python
import math
import jax
import jax.numpy as jnp
import numpy as np
from jax import lax

MODEL_WIDTH = 2560
QUERY_HEADS = 32
KEYVALUE_HEADS = 8
HEAD_WIDTH = 80
FF = 7168
SEQ = 1024
DOCS = 4
REPLICA_GROUPS = 4
STEP = 8
SEQS = 8
TOKENS = 8192
GROUP_TOKENS = 2048
DOC_MOST = 800
N_DP = 8


def block_scale(key, extent, split, low, top_value):
    def one(dim, shards_of):
        steps = jax.random.uniform(jax.random.fold_in(jax.random.fold_in(key, 6), dim), (shards_of,), jnp.float32, low / len(split), top_value / len(split))
        return jnp.repeat(jnp.exp(steps), extent[dim] // shards_of).reshape((-1,) + (1,) * (len(extent) - dim - 1))

    loudness = one(*split[0])
    for cut in split[1:]:
        loudness = loudness * one(*cut)
    return loudness


def profile(amount, total, reach, slope):
    portions = [(1 << 20) // math.isqrt(standing ** slope) + 1 for standing in range(2, amount + 1)]
    rest, counts = total - reach - (amount - 1), [1] * (amount - 1)
    while rest > 0:
        movable = [i for i in range(amount - 1) if counts[i] < reach]
        whole, budget = sum([portions[i] for i in movable]), rest
        for i in movable:
            more = min(reach - counts[i], max(1, budget * portions[i] // whole), rest)
            counts[i] = counts[i] + more
            rest = rest - more
    return np.array([reach] + counts)


def ragged_sizes(stream_key, count, total, reach, skew):
    if count == 2:
        one = jax.random.randint(stream_key, (), max(1, total - reach), min(reach, total - 1) + 1)
        return jnp.stack([one, total - one])
    tallies = jnp.asarray(profile(count, total, reach, skew), jnp.int32)
    pairs = (count - 1) // 2
    source_of, taker = tallies[1:1 + 2 * pairs:2], tallies[2:2 + 2 * pairs:2]
    room = jnp.minimum(source_of - 1, reach - taker)
    passed = jax.random.randint(jax.random.fold_in(stream_key, 1), (pairs,), 0, 1 << 20) % (room + 1)
    tallies = tallies.at[1:1 + 2 * pairs:2].set(source_of - passed).at[2:2 + 2 * pairs:2].set(taker + passed)
    return tallies[jax.random.permutation(jax.random.fold_in(stream_key, 2), count)]


def bell_draw(stream_key, extent, spread, bound, shards=(), kind=jnp.bfloat16):
    level = block_scale(stream_key, extent, shards, -0.22, 0.18) if shards else 1.0
    entries = jax.random.normal(stream_key, extent, jnp.float32) * spread * level
    return jnp.minimum(jnp.maximum(entries, -bound), bound).astype(kind)


def setup_inputs(seed: int = 0) -> dict:
    key_of = jax.random.split(jax.random.key(seed), 28)
    return {
        "tokens": bell_draw(key_of[0], (TOKENS, MODEL_WIDTH), 1.0, 6.0, ((0, 32),)),
        "cotangent": bell_draw(key_of[1], (TOKENS, MODEL_WIDTH), 1.0, 6.0, ((0, 32),)),
        "doc_lengths": jax.vmap(lambda own: ragged_sizes(own, DOCS, SEQ, DOC_MOST, 0))(jax.random.split(key_of[2], SEQS)).reshape((SEQS, DOCS)).astype(jnp.int32),
        "query_weight": bell_draw(key_of[3], (MODEL_WIDTH, QUERY_HEADS * HEAD_WIDTH), MODEL_WIDTH ** -0.5, 0.125, ((0, 8), (1, 4)), jnp.float32),
        "keyvalue_weight_full": bell_draw(key_of[4], (MODEL_WIDTH, 2, KEYVALUE_HEADS * HEAD_WIDTH), MODEL_WIDTH ** -0.5, 0.125, ((0, 8), (2, 4)), jnp.float32),
        "output_weight": bell_draw(key_of[5], (MODEL_WIDTH, QUERY_HEADS * HEAD_WIDTH), (QUERY_HEADS * HEAD_WIDTH // 32) ** -0.5, 0.625, ((0, 8), (1, 4)), jnp.float32),
        "gating_weight": bell_draw(key_of[6], (MODEL_WIDTH, 2, FF), MODEL_WIDTH ** -0.5, 0.125, ((0, 8), (2, 4)), jnp.float32),
        "down_weight": bell_draw(key_of[7], (MODEL_WIDTH, FF), (FF // 3) ** -0.5, 0.125, ((0, 8), (1, 4)), jnp.float32),
        "norm_gains": jnp.clip(1.0 + 0.1 * jax.random.normal(key_of[8], (2, MODEL_WIDTH), jnp.float32), 0.5, 1.5),
        "first_query": bell_draw(key_of[9], (REPLICA_GROUPS, MODEL_WIDTH, QUERY_HEADS * HEAD_WIDTH), (0.22 * GROUP_TOKENS ** 0.5), 64.0, ((1, 8), (2, 4)), jnp.float32),
        "keyvalue_first_moment": bell_draw(key_of[10], (REPLICA_GROUPS, MODEL_WIDTH, 2, KEYVALUE_HEADS * HEAD_WIDTH), (0.28 * GROUP_TOKENS ** 0.5), 80.0, ((1, 8), (3, 4)), jnp.float32),
        "first_output": bell_draw(key_of[11], (REPLICA_GROUPS, MODEL_WIDTH, QUERY_HEADS * HEAD_WIDTH), (0.028 * GROUP_TOKENS ** 0.5), 8.0, ((1, 8), (2, 4)), jnp.float32),
        "first_gating": bell_draw(key_of[12], (REPLICA_GROUPS, MODEL_WIDTH, 2, FF), (0.066 * GROUP_TOKENS ** 0.5), 16.0, ((1, 8), (3, 4)), jnp.float32),
        "first_down": bell_draw(key_of[13], (REPLICA_GROUPS, MODEL_WIDTH, FF), (0.066 * GROUP_TOKENS ** 0.5), 16.0, ((1, 8), (2, 4)), jnp.float32),
        "first_gains": bell_draw(key_of[14], (REPLICA_GROUPS, 2, MODEL_WIDTH), (0.165 * GROUP_TOKENS ** 0.5), 48.0, ((2, 8),), jnp.float32),
        "second_query": jnp.clip(jnp.exp(math.log(3276.8) - 2.5902672 * jax.random.uniform(key_of[15], (REPLICA_GROUPS, MODEL_WIDTH, QUERY_HEADS * HEAD_WIDTH), jnp.float32) ** block_scale(key_of[15], (REPLICA_GROUPS, MODEL_WIDTH, QUERY_HEADS * HEAD_WIDTH), ((1, 8), (2, 4)), -0.2, 0.2)), 245.76, 3276.8),
        "keyvalue_second_moment": jnp.clip(jnp.exp(math.log(5120.0) - 2.57702195 * jax.random.uniform(key_of[16], (REPLICA_GROUPS, MODEL_WIDTH, 2, KEYVALUE_HEADS * HEAD_WIDTH), jnp.float32) ** block_scale(key_of[16], (REPLICA_GROUPS, MODEL_WIDTH, 2, KEYVALUE_HEADS * HEAD_WIDTH), ((1, 8), (3, 4)), -0.2, 0.2)), 389.12, 5120.0),
        "second_output": jnp.clip(jnp.exp(math.log(51.2) - 2.5770219 * jax.random.uniform(key_of[17], (REPLICA_GROUPS, MODEL_WIDTH, QUERY_HEADS * HEAD_WIDTH), jnp.float32) ** block_scale(key_of[17], (REPLICA_GROUPS, MODEL_WIDTH, QUERY_HEADS * HEAD_WIDTH), ((1, 8), (2, 4)), -0.2, 0.2)), 3.8912, 51.2),
        "second_gating": jnp.clip(jnp.exp(math.log(294.912) - 2.571918 * jax.random.uniform(key_of[18], (REPLICA_GROUPS, MODEL_WIDTH, 2, FF), jnp.float32) ** block_scale(key_of[18], (REPLICA_GROUPS, MODEL_WIDTH, 2, FF), ((1, 8), (3, 4)), -0.2, 0.2)), 22.528, 294.912),
        "second_down": jnp.clip(jnp.exp(math.log(294.912) - 2.571918 * jax.random.uniform(key_of[19], (REPLICA_GROUPS, MODEL_WIDTH, FF), jnp.float32) ** block_scale(key_of[19], (REPLICA_GROUPS, MODEL_WIDTH, FF), ((1, 8), (2, 4)), -0.2, 0.2)), 22.528, 294.912),
        "second_gains": jnp.clip(jnp.exp(math.log(1843.2) - 2.582887 * jax.random.uniform(key_of[20], (REPLICA_GROUPS, 2, MODEL_WIDTH), jnp.float32) ** block_scale(key_of[20], (REPLICA_GROUPS, 2, MODEL_WIDTH), ((2, 8),), -0.2, 0.2)), 139.264, 1843.2),
        "moment_query": bell_draw(key_of[21], (MODEL_WIDTH, QUERY_HEADS * HEAD_WIDTH), 0.003, 0.015625, ((0, 8), (1, 4)), jnp.float32),
        "keyvalue_outer_momentum": bell_draw(key_of[22], (MODEL_WIDTH, 2, KEYVALUE_HEADS * HEAD_WIDTH), 0.003, 0.015625, ((0, 8), (2, 4)), jnp.float32),
        "moment_output": bell_draw(key_of[23], (MODEL_WIDTH, QUERY_HEADS * HEAD_WIDTH), 0.012, 0.0625, ((0, 8), (1, 4)), jnp.float32),
        "moment_gating": bell_draw(key_of[24], (MODEL_WIDTH, 2, FF), 0.003, 0.015625, ((0, 8), (2, 4)), jnp.float32),
        "moment_down": bell_draw(key_of[25], (MODEL_WIDTH, FF), 0.003, 0.015625, ((0, 8), (1, 4)), jnp.float32),
        "moment_gains": bell_draw(key_of[26], (2, MODEL_WIDTH), 0.03, 0.1875, ((1, 8),), jnp.float32),
    }


@jax.custom_vjp
def low(v):
    return lax.optimization_barrier(v.astype(jnp.bfloat16)).astype(jnp.float32)

@jax.custom_vjp
def reduced_backward(v):
    return v

def low_keep(v):
    return (low(v), None)

def low_pass(kept, grad):
    return (grad,)

def back_keep(v):
    return (v, None)

def back_low(kept, grad):
    return (low(grad),)
low.defvjp(low_keep, low_pass)
reduced_backward.defvjp(back_keep, back_low)
epsilon = 1e-05
rope_base = 1000000.0
precise = lax.Precision.HIGHEST
beta_one = 0.9
beta_two = 0.95
adam_epsilon = 1e-08
outer_mu = 0.9
outer_rate = 0.7
inner_rates = (0.05, 0.05, 0.2, 0.05, 0.05, 0.5)
inner_decays = (0.1, 0.1, 0.1, 0.1, 0.1, 0.0)

def product_highest(left, right):
    return jnp.dot(left, right, precision=precise, preferred_element_type=jnp.float32)

def matmul_right_t(left, right):
    return lax.dot_general(left, right, (((1,), (1,)), ((), ())), precision=precise, preferred_element_type=jnp.float32)

def doc_layout(lengths, token_length):
    ends = jnp.cumsum(lengths).astype(jnp.int32)
    starts = ends - lengths
    places = jnp.arange(token_length, dtype=jnp.int32)
    segment = lax.optimization_barrier(jnp.sum((places[:, None] >= ends[None, :]).astype(jnp.int32), axis=1)).astype(jnp.int32)
    member = (segment[:, None] == jnp.arange(lengths.shape[0], dtype=jnp.int32)[None, :]).astype(jnp.int32)
    offset = lax.optimization_barrier(jnp.sum(member * starts[None, :], axis=1)).astype(jnp.int32)
    return (segment, places - offset)

def rope_tables(position, head_size):
    half_size = head_size // 2
    frequency = rope_base ** (-2.0 * jnp.arange(half_size, dtype=jnp.float32) / head_size)
    angle = position.astype(jnp.float32)[:, None] * frequency[None, :]
    return (jnp.cos(angle), jnp.sin(angle))

def rotate(value, cosine, sine):
    half_size = value.shape[-1] // 2
    first = value[..., :half_size]
    second = value[..., half_size:]
    cos_wide = cosine[:, None, :]
    sin_wide = sine[:, None, :]
    return jnp.concatenate([first * cos_wide - second * sin_wide, second * cos_wide + first * sin_wide], axis=-1)

def rms_norm(value, gain):
    inverse = lax.rsqrt(lax.optimization_barrier(jnp.mean(value * value, axis=-1, keepdims=True)) + epsilon)
    return value * inverse * gain

def forward(hidden, weights, segment, position):
    query_weight, keyvalue_weight_full, output_weight, gating_weight, down_weight, norm_gains = [low(weight) for weight in weights]
    token_length = hidden.shape[0]
    cosine, sine = rope_tables(position, HEAD_WIDTH)
    first_normalized = low(rms_norm(hidden, norm_gains[0]))
    query = reduced_backward(product_highest(first_normalized, query_weight)).reshape(token_length, QUERY_HEADS, HEAD_WIDTH)
    keyvalue_proj = reduced_backward(product_highest(first_normalized, keyvalue_weight_full.reshape(MODEL_WIDTH, 2 * KEYVALUE_HEADS * HEAD_WIDTH))).reshape(token_length, 2, KEYVALUE_HEADS, HEAD_WIDTH)
    query_rot = low(rotate(query, cosine, sine))
    key_rot = low(rotate(keyvalue_proj[:, 0], cosine, sine))
    values = low(keyvalue_proj[:, 1])
    replica_group_size = QUERY_HEADS // KEYVALUE_HEADS
    key_wide = jnp.repeat(key_rot, replica_group_size, axis=1)
    value_wide = jnp.repeat(values, replica_group_size, axis=1)
    block = min(512, token_length)
    places = jnp.arange(token_length, dtype=jnp.int32)
    scale = 1.0 / math.sqrt(HEAD_WIDTH)

    def attend(inputs):
        row_index, query_block = inputs
        scores = jnp.einsum('qhd,khd->hqk', query_block, key_wide, precision=precise) * scale
        scores = reduced_backward(scores)
        row_segment = jnp.take(segment, row_index)
        allowed = (row_segment[:, None] == segment[None, :]) & (row_index[:, None] >= places[None, :])
        scores = jnp.where(allowed[None], scores, -1e+30)
        top = lax.optimization_barrier(jnp.max(scores, axis=-1, keepdims=True))
        expo = jnp.exp(scores - top)
        probability = low(expo / lax.optimization_barrier(jnp.sum(expo, axis=-1, keepdims=True)))
        return jnp.einsum('hqk,khd->qhd', probability, value_wide, precision=precise)
    mixed = lax.map(jax.checkpoint(attend), (places.reshape(token_length // block, block), query_rot.reshape(token_length // block, block, QUERY_HEADS, HEAD_WIDTH)))
    mixed = reduced_backward(low(mixed.reshape(token_length, QUERY_HEADS * HEAD_WIDTH)))
    attention = reduced_backward(matmul_right_t(mixed, output_weight))
    hidden_one = hidden + attention
    normed_two = low(rms_norm(hidden_one, norm_gains[1]))
    gating = reduced_backward(product_highest(normed_two, gating_weight.reshape(MODEL_WIDTH, 2 * FF))).reshape(token_length, 2, FF)
    activated = low(jax.nn.silu(gating[:, 0]) * gating[:, 1])
    return hidden_one + reduced_backward(matmul_right_t(activated, down_weight))

def optimize(weight, grad, first, second, moment, rate, decay):
    first_new = beta_one * first + (1.0 - beta_one) * grad
    second_new = beta_two * second + (1.0 - beta_two) * grad * grad
    correct_one = 1.0 - beta_one ** STEP
    correct_two = 1.0 - beta_two ** STEP
    direction = first_new / correct_one / (jnp.sqrt(second_new / correct_two) + adam_epsilon) + decay * weight[None]
    delta = lax.optimization_barrier(jnp.mean(rate * direction, axis=0))
    moment_new = outer_mu * moment + delta
    weight_new = weight - outer_rate * (delta + outer_mu * moment_new)
    return (first_new, second_new, delta, moment_new, weight_new, weight_new.astype(jnp.bfloat16))

def reference(tokens, cotangent, doc_lengths, query_weight, keyvalue_weight_full, output_weight, gating_weight, down_weight, norm_gains, first_query, keyvalue_first_moment, first_output, first_gating, first_down, first_gains, second_query, keyvalue_second_moment, second_output, second_gating, second_down, second_gains, moment_query, keyvalue_outer_momentum, moment_output, moment_gating, moment_down, moment_gains):
    masters = (query_weight, keyvalue_weight_full, output_weight, gating_weight, down_weight, norm_gains)
    per_group = N_DP // REPLICA_GROUPS
    inputs_all = tokens.astype(jnp.float32).reshape(REPLICA_GROUPS, per_group, SEQ, MODEL_WIDTH)
    cotangent_all = cotangent.astype(jnp.float32).reshape(REPLICA_GROUPS, per_group, SEQ, MODEL_WIDTH)
    lengths_all = doc_lengths.reshape(REPLICA_GROUPS, per_group, DOCS)

    def group_pass(inputs):
        group_tokens, group_cotangent, group_lengths = inputs
        zeros = tuple((jnp.zeros_like(weight) for weight in masters))

        def one_sequence(totals, item):
            sequence_tokens, sequence_cotangent, sequence_lengths = item
            segment, position = doc_layout(sequence_lengths, SEQ)

            def apply(hidden, *weights):
                return forward(hidden, weights, segment, position)
            result, pullback = jax.vjp(apply, sequence_tokens, *masters)
            grads = pullback(sequence_cotangent)
            totals = tuple((total + grad for total, grad in zip(totals, grads[1:])))
            return (totals, (result, grads[0]))
        return lax.scan(one_sequence, zeros, (group_tokens, group_cotangent, group_lengths))
    grads, (results, input_grads) = lax.map(group_pass, (inputs_all, cotangent_all, lengths_all))
    block_output = results.reshape(TOKENS, MODEL_WIDTH).astype(jnp.bfloat16)
    token_grad = input_grads.reshape(TOKENS, MODEL_WIDTH).astype(jnp.bfloat16)
    firsts = (first_query, keyvalue_first_moment, first_output, first_gating, first_down, first_gains)
    seconds = (second_query, keyvalue_second_moment, second_output, second_gating, second_down, second_gains)
    moments = (moment_query, keyvalue_outer_momentum, moment_output, moment_gating, moment_down, moment_gains)
    updated = [optimize(masters[kind], grads[kind], firsts[kind], seconds[kind], moments[kind], inner_rates[kind], inner_decays[kind]) for kind in range(6)]
    qry, kvl, out, gat, dwn, gns = updated
    return (block_output, token_grad, qry[0], qry[1], qry[2], qry[3], qry[4], qry[5], kvl[0], kvl[1], kvl[2], kvl[3], kvl[4], kvl[5], out[0], out[1], out[2], out[3], out[4], out[5], gat[0], gat[1], gat[2], gat[3], gat[4], gat[5], dwn[0], dwn[1], dwn[2], dwn[3], dwn[4], dwn[5], gns[0], gns[1], gns[2], gns[3], gns[4], gns[5])
```

```python
import functools
import math

import jax
import jax.numpy as jnp
import numpy as np
from jax import lax
from jax.experimental import pallas as pl
from jax.experimental.pallas import tpu as pltpu
from jax.sharding import Mesh, PartitionSpec as P

HEAD_WIDTH = 80
REPLICA_GROUPS = 4
STEP = 8
LANES = 128
HEADS = 4
TILE = 256
PACK = 512
WIDE = 768
HALF = 64
VMEM_BYTES = 58 * 2**20

epsilon = 1e-05
rope_base = 1000000.0
beta_one = 0.9
beta_two = 0.95
adam_epsilon = 1e-08
outer_mu = 0.9
outer_rate = 0.7
inner_rates = (0.05, 0.05, 0.2, 0.05, 0.05, 0.5)
inner_decays = (0.1, 0.1, 0.1, 0.1, 0.1, 0.0)
correct_one = 1.0 - beta_one**STEP
correct_two = 1.0 - beta_two**STEP

low_type = jnp.bfloat16
f32 = jnp.float32

NN = (((1,), (0,)), ((), ()))
NT = (((1,), (1,)), ((), ()))
TN = (((0,), (0,)), ((), ()))

CHUNKS = ((0, 3), (3, 7))


def after(value, *earlier):
    return lax.optimization_barrier((value, earlier))[0]


def dot(left, right, dims=NN):
    return lax.dot_general(left, right, dims, preferred_element_type=f32)


def params(**kwargs):
    return pltpu.CompilerParams(vmem_limit_bytes=VMEM_BYTES, **kwargs)


def cost(flops, size):
    return pl.CostEstimate(flops=int(flops), bytes_accessed=int(size), transcendentals=0)


SHORT = pl.CostEstimate(flops=1, bytes_accessed=1, transcendentals=0)


def resident(shape):
    zeros = (0,) * len(shape)
    return pl.BlockSpec(shape, lambda *_: zeros, pipeline_mode=pl.Buffered(1))


def projection_selector():
    table = np.zeros((PACK, WIDE), np.float32)
    for head in range(HEADS + 1):
        for place in range(HEAD_WIDTH):
            half, rest = divmod(place, HEAD_WIDTH // 2)
            table[head * HEAD_WIDTH + place, head * LANES + half * HALF + rest] = 1.0
    for place in range(HEAD_WIDTH):
        table[(HEADS + 1) * HEAD_WIDTH + place, (HEADS + 1) * LANES + place] = 1.0
    return table


def output_selector():
    table = np.zeros((HEADS * HEAD_WIDTH, HEADS * LANES), np.float32)
    for head in range(HEADS):
        for place in range(HEAD_WIDTH):
            table[head * HEAD_WIDTH + place, head * LANES + place] = 1.0
    return table


def gains_selector():
    table = np.zeros((8, PACK), np.float32)
    table[0, (HEADS + 2) * HEAD_WIDTH] = 1.0
    table[1, (HEADS + 2) * HEAD_WIDTH + 1] = 1.0
    return table


def seen_from(place_ref, piece):
    return lax.bitwise_xor(piece, place_ref[3])


def piece_specs(width, piece):
    return [pl.BlockSpec((TILE, width), lambda *at: (lax.shift_right_logical(piece(*at), 1), 0))] * 2


def piece_shapes(total, width):
    return [jax.ShapeDtypeStruct((total // 2, width), low_type)] * 2


def write_piece(piece, kept, sent, value):
    odd = lax.bitwise_and(piece, 1)

    @pl.when(odd == 0)
    def _():
        kept[...] = value

    @pl.when(odd == 1)
    def _():
        sent[...] = value


def first_row(place, step, blocks, rows):
    return pl.multiple_of(lax.rem(place - step + blocks, blocks) * rows, LANES if blocks > 1 else rows)


def assemble(place, blocks, target):
    rows = blocks[0].shape[0]
    for step, block in enumerate(blocks):
        target[pl.ds(first_row(place, step, len(blocks), rows), rows), :] = block[...]


def projection_kernel(count, place_ref, tokens, *refs):
    blocks, (select, pick, cosine, sine, normed, heads, gains, wide) = refs[:count], refs[count:]

    @pl.when(pl.program_id(0) == 0)
    def _():
        rows = blocks[0].shape[0]
        for step, block in enumerate(blocks):
            start = first_row(place_ref[0], step, count, rows)
            value = block[...]
            wide[pl.ds(start, rows), :] = dot(value, select[...]).astype(low_type)
            gains[:, pl.ds(start, rows)] = dot(pick[...], value, NT)

    value = tokens[...].astype(f32)
    inverse = lax.rsqrt(jnp.mean(value * value, axis=-1, keepdims=True) + epsilon)
    low = (value * inverse * gains[0:1, :]).astype(low_type)
    normed[...] = low
    result = dot(low, wide[...])
    cos_tile = cosine[...]
    sin_tile = sine[...]
    for head in range(HEADS + 1):
        part = result[:, head * LANES : (head + 1) * LANES]
        turned = part * cos_tile + pltpu.roll(part, HALF, 1) * sin_tile
        heads[:, head * LANES : (head + 1) * LANES] = turned.astype(low_type)
    heads[:, (HEADS + 1) * LANES :] = result[:, (HEADS + 1) * LANES :].astype(low_type)


def project(place, tokens, blocks, cosine, sine):
    total, width = tokens.shape
    tile = lambda columns: pl.BlockSpec((TILE, columns), lambda i, p: (i, 0))
    return pl.pallas_call(
        functools.partial(projection_kernel, len(blocks)),
        grid_spec=pltpu.PrefetchScalarGridSpec(
            num_scalar_prefetch=1,
            grid=(total // TILE,),
            in_specs=[tile(width)]
            + [resident((block.shape[0], PACK)) for block in blocks]
            + [
                resident((PACK, WIDE)),
                resident((8, PACK)),
                tile(LANES),
                tile(LANES),
            ],
            out_specs=[
                tile(width),
                tile(WIDE),
                pl.BlockSpec((8, width), lambda *_: (0, 0)),
                pl.BlockSpec((width, WIDE), lambda *_: (0, 0)),
            ],
        ),
        out_shape=[
            jax.ShapeDtypeStruct((total, width), low_type),
            jax.ShapeDtypeStruct((total, WIDE), low_type),
            jax.ShapeDtypeStruct((8, width), f32),
            jax.ShapeDtypeStruct((width, WIDE), low_type),
        ],
        compiler_params=params(),
        cost_estimate=cost(2 * total * width * WIDE, 4 * total * width + 3 * width * WIDE * 2),
        name="projection",
    )(
        place,
        tokens,
        *blocks,
        jnp.asarray(projection_selector(), low_type),
        jnp.asarray(gains_selector(), low_type),
        cosine,
        sine,
    )


SCORE_SCALE = math.log2(math.e) / math.sqrt(HEAD_WIDTH)
GRAD_SCALE = 1.0 / math.sqrt(HEAD_WIDTH)


def allowed_pairs(block, width, starts):
    key_index = lax.broadcasted_iota(jnp.int32, (width, TILE), 0)
    row_index = block * TILE + lax.broadcasted_iota(jnp.int32, (1, TILE), 1)
    return (key_index >= starts) & (key_index <= row_index)


def widen_output(place_ref, blocks, select, wide):
    @pl.when((pl.program_id(0) == 0) & (pl.program_id(1) == 0))
    def _():
        rows = blocks[0].shape[0]
        for step, block in enumerate(blocks):
            start = first_row(place_ref[0], step, len(blocks), rows)
            value = block[:, PACK:]
            wide[pl.ds(start, rows), :] = dot(value, select[...]).astype(low_type)


def attention_kernel(count, blocks_per, place_ref, query, key, value, starts, *refs):
    blocks, (select, mixed, totals, kept, sent, wide) = refs[:count], refs[count:]
    widen_output(place_ref, blocks, select, wide)

    for block in range(blocks_per):

        @pl.when(pl.program_id(1) == block)
        def _(block=block):
            width = (block + 1) * TILE
            allowed = allowed_pairs(block, width, starts[0:1, :])
            keys = key[0:width, :]
            values = value[0:width, :]
            for head in range(HEADS):
                lanes = slice(head * LANES, (head + 1) * LANES)
                scores = dot(keys, query[:, lanes], NT) * SCORE_SCALE
                scores = jnp.where(allowed, scores, -1e30)
                top = jnp.max(scores, axis=0, keepdims=True)
                expo = jnp.exp2(scores - top)
                total = jnp.sum(expo, axis=0, keepdims=True)
                out = dot(values, expo.astype(low_type), TN) * (1.0 / total)
                mixed[:, lanes] = out.T.astype(low_type)
                totals[head : head + 1, :] = top + jnp.log2(total)

    piece = pl.program_id(0) * blocks_per + pl.program_id(1)
    value = dot(mixed[...], wide[...], NT).astype(low_type)
    write_piece(seen_from(place_ref, piece), kept, sent, value)


def attend(place, heads, starts, blocks, sequence):
    total = heads.shape[0]
    width = blocks[0].shape[0] * len(blocks)
    per = sequence // TILE
    tile = lambda size, column: pl.BlockSpec((TILE, size), lambda s, i, *_: (s * per + i, column))
    full = lambda column: pl.BlockSpec((sequence, LANES), lambda s, i, *_: (s, column))
    line = pl.BlockSpec((8, TILE), lambda s, i, *_: (0, s * per + i))
    return pl.pallas_call(
        functools.partial(attention_kernel, len(blocks), per),
        grid_spec=pltpu.PrefetchScalarGridSpec(
            num_scalar_prefetch=1,
            grid=(total // sequence, per),
            in_specs=[
                tile(HEADS * LANES, 0),
                full(HEADS),
                full(HEADS + 1),
                line,
            ]
            + [resident(block.shape) for block in blocks]
            + [resident((HEADS * HEAD_WIDTH, HEADS * LANES))],
            out_specs=[tile(HEADS * LANES, 0), line]
            + piece_specs(width, lambda s, i, p: seen_from(p, s * per + i)),
            scratch_shapes=[pltpu.VMEM((width, HEADS * LANES), low_type)],
        ),
        out_shape=[
            jax.ShapeDtypeStruct((total, HEADS * LANES), low_type),
            jax.ShapeDtypeStruct((8, total), f32),
        ]
        + piece_shapes(total, width),
        compiler_params=params(),
        cost_estimate=cost(20e9, 4 * total * width),
        name="attention",
    )(place, heads, heads, heads, starts, *blocks, jnp.asarray(output_selector(), low_type))


def attention_grad_kernel(
    count,
    blocks_per,
    place_ref,
    grad_hidden,
    query,
    key,
    value,
    totals,
    starts,
    cosine,
    sine,
    cos_all,
    sin_all,
    *refs,
):
    blocks, (select, grad_query, grad_pair, wide, key_sum, value_sum) = refs[:count], refs[count:]
    widen_output(place_ref, blocks, select, wide)

    @pl.when(pl.program_id(1) == 0)
    def _():
        key_sum[...] = jnp.zeros_like(key_sum)
        value_sum[...] = jnp.zeros_like(value_sum)

    grad_mixed = dot(grad_hidden[...], wide[...]).astype(low_type)
    cos_tile = cosine[...]
    sin_tile = sine[...]
    for block in range(blocks_per):

        @pl.when(pl.program_id(1) == block)
        def _(block=block):
            width = (block + 1) * TILE
            allowed = allowed_pairs(block, width, starts[0:1, :])
            keys = key[0:width, :]
            values = value[0:width, :]
            key_part = jnp.zeros((width, LANES), f32)
            value_part = jnp.zeros((width, LANES), f32)
            for head in range(HEADS):
                lanes = slice(head * LANES, (head + 1) * LANES)
                queries = query[:, lanes]
                grads = grad_mixed[:, lanes]
                scores = dot(keys, queries, NT) * SCORE_SCALE
                scores = jnp.where(allowed, scores, -1e30)
                prob = jnp.exp2(scores - totals[head : head + 1, :])
                grad_prob = dot(values, grads, NT)
                inner = jnp.sum(prob * grad_prob, axis=0, keepdims=True)
                grad_scores = (prob * (grad_prob - inner)).astype(low_type)
                key_part = key_part + dot(grad_scores, queries)
                value_part = value_part + dot(prob.astype(low_type), grads)
                turned = dot(keys, grad_scores, TN).T * GRAD_SCALE
                turned = turned * cos_tile - pltpu.roll(turned, HALF, 1) * sin_tile
                grad_query[:, lanes] = turned.astype(low_type)
            key_sum[0:width, :] += key_part
            value_sum[0:width, :] += value_part

    @pl.when(pl.program_id(1) == blocks_per - 1)
    def _():
        grad_key = key_sum[...] * GRAD_SCALE
        grad_key = grad_key * cos_all[...] - pltpu.roll(grad_key, HALF, 1) * sin_all[...]
        grad_pair[:, :LANES] = grad_key.astype(low_type)
        grad_pair[:, LANES:] = value_sum[...].astype(low_type)


def attend_grad(place, grad_hidden, heads, totals, starts, cosine, sine, blocks, sequence):
    total, width = grad_hidden.shape
    per = sequence // TILE
    tile = lambda size, column: pl.BlockSpec((TILE, size), lambda s, i, p: (s * per + i, column))
    full = lambda size, column: pl.BlockSpec((sequence, size), lambda s, i, p: (s, column))
    line = pl.BlockSpec((8, TILE), lambda s, i, p: (0, s * per + i))
    return pl.pallas_call(
        functools.partial(attention_grad_kernel, len(blocks), per),
        grid_spec=pltpu.PrefetchScalarGridSpec(
            num_scalar_prefetch=1,
            grid=(total // sequence, per),
            in_specs=[
                tile(width, 0),
                tile(HEADS * LANES, 0),
                full(LANES, HEADS),
                full(LANES, HEADS + 1),
                line,
                line,
                tile(LANES, 0),
                tile(LANES, 0),
                full(LANES, 0),
                full(LANES, 0),
            ]
            + [resident(block.shape) for block in blocks]
            + [resident((HEADS * HEAD_WIDTH, HEADS * LANES))],
            out_specs=[tile(HEADS * LANES, 0), full(2 * LANES, 0)],
            scratch_shapes=[
                pltpu.VMEM((width, HEADS * LANES), low_type),
                pltpu.VMEM((sequence, LANES), f32),
                pltpu.VMEM((sequence, LANES), f32),
            ],
        ),
        out_shape=[
            jax.ShapeDtypeStruct((total, HEADS * LANES), low_type),
            jax.ShapeDtypeStruct((total, 2 * LANES), low_type),
        ],
        compiler_params=params(),
        cost_estimate=cost(30e9, 4 * total * width),
        name="attention_grad",
    )(
        place,
        grad_hidden,
        heads,
        heads,
        heads,
        totals,
        starts,
        cosine,
        sine,
        cosine,
        sine,
        *blocks,
        jnp.asarray(output_selector(), low_type),
    )


def projection_grad_kernel(place_ref, grad_query, grad_pair, tokens, wide, kept, sent, gain_sums):
    grad = dot(grad_query[...], wide[:, : HEADS * LANES], NT)
    grad = grad + dot(grad_pair[...], wide[:, HEADS * LANES :], NT)
    write_piece(seen_from(place_ref, pl.program_id(0)), kept, sent, grad.astype(low_type))
    value = tokens[...].astype(f32)
    inverse = lax.rsqrt(jnp.mean(value * value, axis=-1, keepdims=True) + epsilon)
    product = grad * (value * inverse)
    sums = jnp.sum(product.reshape(TILE // 8, 8, product.shape[1]), axis=0)

    @pl.when(pl.program_id(0) == 0)
    def _():
        gain_sums[...] = sums

    @pl.when(pl.program_id(0) != 0)
    def _():
        gain_sums[...] += sums


def project_grad(place, grad_query, grad_pair, tokens, wide):
    total, width = tokens.shape
    tile = lambda columns: pl.BlockSpec((TILE, columns), lambda i, *_: (i, 0))
    return pl.pallas_call(
        projection_grad_kernel,
        grid_spec=pltpu.PrefetchScalarGridSpec(
            num_scalar_prefetch=1,
            grid=(total // TILE,),
            in_specs=[
                tile(HEADS * LANES),
                tile(2 * LANES),
                tile(width),
                resident((width, WIDE)),
            ],
            out_specs=piece_specs(width, lambda i, p: seen_from(p, i)) + [pl.BlockSpec((8, width), lambda i, *_: (0, 0))],
        ),
        out_shape=piece_shapes(total, width) + [jax.ShapeDtypeStruct((8, width), f32)],
        compiler_params=params(),
        cost_estimate=SHORT,
        name="projection_grad",
    )(place, grad_query, grad_pair, tokens, wide)


def pack_kernel(place_ref, gating, down, *outs):
    kept, sent = outs[: len(CHUNKS)], outs[len(CHUNKS) :]

    def write(targets):
        for (first, last), target in zip(CHUNKS, targets):
            count = last - first
            for tile in range(first, last):
                lanes = slice(tile * LANES, (tile + 1) * LANES)
                place = (tile - first) * 2 * LANES
                target[:, place : place + LANES] = gating[:, 0, lanes].astype(low_type)
                target[:, place + LANES : place + 2 * LANES] = gating[:, 1, lanes].astype(low_type)
                place = (2 * count + tile - first) * LANES
                target[:, place : place + LANES] = down[:, lanes].astype(low_type)

    @pl.when(pl.program_id(0) == 0)
    def _():
        write(sent)

    @pl.when(pl.program_id(0) == 1)
    def _():
        write(kept)


def pack_feed(place, gating, down):
    rows, _, hidden = gating.shape
    half = hidden // 2
    side = lambda i, place_ref: jnp.where(i == 0, 1 - place_ref[1], place_ref[1])
    shapes = [(rows, 3 * LANES * (last - first)) for first, last in CHUNKS] * 2
    return pl.pallas_call(
        pack_kernel,
        grid_spec=pltpu.PrefetchScalarGridSpec(
            num_scalar_prefetch=1,
            grid=(2,),
            in_specs=[
                pl.BlockSpec((rows, 2, half), lambda i, p: (0, 0, side(i, p))),
                pl.BlockSpec((rows, half), lambda i, p: (0, side(i, p))),
            ],
            out_specs=[pl.BlockSpec(shape, lambda *_: (0, 0)) for shape in shapes],
        ),
        out_shape=[jax.ShapeDtypeStruct(shape, low_type) for shape in shapes],
        compiler_params=params(),
        cost_estimate=cost(0, 18 * rows * hidden),
        name="pack_feed",
    )(place, gating, down)


def feed_kernel(count, tiles, place_ref, normed, grad_out, *refs):
    blocks, (hidden, grad_pair, weights) = refs[:count], refs[count:]

    @pl.when(pl.program_id(0) == 0)
    def _():
        assemble(place_ref[0], blocks, weights)

    pair = dot(normed[...], weights[:, : 2 * tiles * LANES])
    grad_hidden = dot(grad_out[...], weights[:, 2 * tiles * LANES :])
    for tile in range(tiles):
        place = 2 * tile * LANES
        gate = pair[:, place : place + LANES]
        up = pair[:, place + LANES : place + 2 * LANES]
        grad = grad_hidden[:, tile * LANES : (tile + 1) * LANES]
        sigma = 1.0 / (1.0 + jnp.exp(-gate))
        silu = gate * sigma
        hidden[:, tile * LANES : (tile + 1) * LANES] = (silu * up).astype(low_type)
        grad_gate = grad * up * sigma * (1.0 + gate * (1.0 - sigma))
        grad_pair[:, place : place + LANES] = grad_gate.astype(low_type)
        grad_pair[:, place + LANES : place + 2 * LANES] = (grad * silu).astype(low_type)


def feed(place, normed, grad_out, blocks):
    total, width = normed.shape
    rows, columns = blocks[0].shape
    tiles = columns // (3 * LANES)
    tile = lambda size: pl.BlockSpec((TILE, size), lambda i, p: (i, 0))
    return pl.pallas_call(
        functools.partial(feed_kernel, len(blocks), tiles),
        grid_spec=pltpu.PrefetchScalarGridSpec(
            num_scalar_prefetch=1,
            grid=(total // TILE,),
            in_specs=[tile(width), tile(width)] + [resident(block.shape) for block in blocks],
            out_specs=[tile(tiles * LANES), tile(2 * tiles * LANES)],
            scratch_shapes=[pltpu.VMEM((width, columns), low_type)],
        ),
        out_shape=[
            jax.ShapeDtypeStruct((total, tiles * LANES), low_type),
            jax.ShapeDtypeStruct((total, 2 * tiles * LANES), low_type),
        ],
        compiler_params=params(),
        cost_estimate=cost(2 * total * width * columns, 4 * total * width + 2 * width * columns),
        name="feed",
    )(place, normed, grad_out, *blocks)


def spread_kernel(counts, place_ref, *refs):
    parts = len(counts)
    values, rest = refs[:parts], refs[parts:]
    chunks = []
    for count in counts:
        chunks.append(rest[:count])
        rest = rest[count:]
    kept, sent, wholes = rest[0], rest[1], rest[2:]

    @pl.when(pl.program_id(0) == 0)
    def _():
        for blocks, whole in zip(chunks, wholes):
            assemble(place_ref[0], blocks, whole)

    total = dot(values[0][...], wholes[0][...], NT)
    for value, whole in zip(values[1:], wholes[1:]):
        total = total + dot(value[...], whole[...], NT)
    write_piece(pl.program_id(0), kept, sent, total.astype(low_type))


def spread(place, values, chunks, column):
    total = values[0].shape[0]
    width = chunks[0][0].shape[0] * len(chunks[0])
    tile = lambda size: pl.BlockSpec((TILE, size), lambda i, p: (i, 0))
    return pl.pallas_call(
        functools.partial(spread_kernel, tuple(len(blocks) for blocks in chunks)),
        grid_spec=pltpu.PrefetchScalarGridSpec(
            num_scalar_prefetch=1,
            grid=(total // TILE,),
            in_specs=[tile(value.shape[1]) for value in values]
            + [
                pl.BlockSpec(
                    (block.shape[0], value.shape[1]), lambda *_: (0, column), pipeline_mode=pl.Buffered(1)
                )
                for value, blocks in zip(values, chunks)
                for block in blocks
            ],
            out_specs=piece_specs(width, lambda i, p: i),
            scratch_shapes=[pltpu.VMEM((width, value.shape[1]), low_type) for value in values],
        ),
        out_shape=piece_shapes(total, width),
        compiler_params=params(),
        cost_estimate=SHORT,
        name="spread",
    )(place, *values, *[block for blocks in chunks for block in blocks])


ROW_TILE = 640


def weight_grad_kernel(parts, select_count, split, place_ref, *refs):
    lefts, rights, rest = refs[:parts], refs[parts : 2 * parts], refs[2 * parts :]
    select, outs = rest[:select_count], rest[select_count:]

    def compute(left, right, offset):
        value = dot(left[...], right[...], TN).astype(low_type)
        if select_count:
            return dot(value, select[0][:, offset : offset + right.shape[1]], NT)
        return value

    def write(targets, value, columns, again):
        size = targets[0].shape[0]
        for place, target in enumerate(targets):
            rows = value[place * size : (place + 1) * size]
            if again:
                rows = rows + target[:, columns].astype(f32)
            target[:, columns] = rows.astype(low_type)

    for block in range(len(outs) // split):
        targets = outs[block * split : (block + 1) * split]

        @pl.when(pl.program_id(0) == block)
        def _(targets=targets):
            offset = 0
            for left, right in zip(lefts, rights):
                value = compute(left, right, offset)
                columns = slice(None) if select_count else slice(offset, offset + right.shape[1])
                again = select_count and offset
                offset += right.shape[1]
                if split == 1:
                    write(targets, value, columns, again)
                    continue

                @pl.when(place_ref[1] == 0)
                def _(value=value, columns=columns, again=again):
                    write(targets, value, columns, again)

                @pl.when(place_ref[1] != 0)
                def _(value=value, columns=columns, again=again):
                    write(targets[::-1], value, columns, again)


def weight_grad(place, blocks, pairs, select=None):
    total, width = pairs[0][0].shape
    rows = width // blocks
    split = 1 if blocks == 1 else 2
    row_tile = math.gcd(rows, ROW_TILE)
    row_tiles = rows // row_tile
    columns = sum(right.shape[1] for _, right in pairs)
    out_columns = columns if select is None else select.shape[0]
    first = lambda b, r, p: lax.rem(p[0] - b + blocks, blocks) * row_tiles + r
    extra = [] if select is None else [jnp.asarray(select, low_type)]
    return pl.pallas_call(
        functools.partial(weight_grad_kernel, len(pairs), len(extra), split),
        grid_spec=pltpu.PrefetchScalarGridSpec(
            num_scalar_prefetch=1,
            grid=(blocks, row_tiles),
            in_specs=[pl.BlockSpec((total, row_tile), lambda b, r, p: (0, first(b, r, p))) for _ in pairs]
            + [resident(right.shape) for _, right in pairs]
            + [resident(value.shape) for value in extra],
            out_specs=[pl.BlockSpec((row_tile // split, out_columns), lambda b, r, p: (r, 0))] * (blocks * split),
        ),
        out_shape=[jax.ShapeDtypeStruct((rows // split, out_columns), low_type)] * (blocks * split),
        compiler_params=params(),
        cost_estimate=cost(2 * total * width * columns, 2 * total * (columns + width * len(pairs))),
        name="weight_grad",
    )(place, *[left for left, _ in pairs], *[right for _, right in pairs], *extra)


ROOT_TWO = math.sqrt(correct_two)


def adam_step(grad, first, second, reciprocal):
    first_new = beta_one * first + (1.0 - beta_one) * grad
    second_new = beta_two * second + ((1.0 - beta_two) * grad) * grad
    root = second_new * lax.rsqrt(jnp.maximum(second_new, 1e-30)) + adam_epsilon * ROOT_TWO
    return first_new, second_new, first_new * reciprocal(root)


def mean_step(total, weight, rate, decay):
    return (rate * ROOT_TWO / correct_one / REPLICA_GROUPS) * total + (rate * decay) * weight


def outer_step(weight, delta, moment):
    moment_new = outer_mu * moment + delta
    return moment_new, weight - outer_rate * (delta + outer_mu * moment_new)


PAIR_ROWS = 4


def feed_update_kernel(place_ref, *refs):
    slots = REPLICA_GROUPS * len(CHUNKS)
    own, other, rest = refs[:slots], refs[slots : 2 * slots], refs[2 * slots :]
    (
        gate_first,
        gate_second,
        gate_weight,
        gate_moment,
        down_first,
        down_second,
        down_weight,
        down_moment,
        gate_first_new,
        gate_second_new,
        gate_delta,
        gate_moment_new,
        gate_master,
        gate_copy,
        down_first_new,
        down_second_new,
        down_delta,
        down_moment_new,
        down_master,
        down_copy,
        gate_grads,
    ) = rest
    near = place_ref[1] == 0
    quick = lambda value: pl.reciprocal(value, approx=True)
    half = down_weight.shape[1] // 2
    groups = [lax.rem(place_ref[2] + k, REPLICA_GROUPS) for k in range(REPLICA_GROUPS)]

    def update(grads, at, first, second, weight, moment, outs, rate, decay):
        first_new, second_new, delta_out, moment_new, master, copy = outs
        start = weight[at]
        total = None
        for group, grad in zip(groups, grads):
            here = (group,) + at
            one, two, step = adam_step(grad, first[here], second[here], quick)
            first_new[here] = one
            second_new[here] = two
            total = step if total is None else total + step
        delta = mean_step(total, start, rate, decay)
        new_moment, new_weight = outer_step(start, delta, moment[at])
        delta_out[at] = delta
        moment_new[at] = new_moment
        master[at] = new_weight
        copy[at] = new_weight.astype(low_type)

    every = slice(None)
    for chunk, (begin, end) in enumerate(CHUNKS):
        for tile in range(begin, end):
            for kind in range(3):
                place = (2 * (tile - begin) + kind) if kind < 2 else (2 * (end - begin) + tile - begin)
                lanes = slice(place * LANES, (place + 1) * LANES)
                mine = [own[chunk * REPLICA_GROUPS + k][:, lanes] for k in range(REPLICA_GROUPS)]
                theirs = [other[chunk * REPLICA_GROUPS + k][:, lanes] for k in range(REPLICA_GROUPS)]
                for side in range(2):
                    grads = [
                        (jnp.where(near, a, b) if side == 0 else jnp.where(near, b, a)).astype(f32)
                        for a, b in zip(mine, theirs)
                    ]
                    at = slice(side * half + tile * LANES, side * half + (tile + 1) * LANES)
                    if kind < 2:
                        for k, grad in enumerate(grads):
                            gate_grads[k, :, kind, at] = grad
                    else:
                        update(
                            grads,
                            (every, at),
                            down_first,
                            down_second,
                            down_weight,
                            down_moment,
                            (down_first_new, down_second_new, down_delta, down_moment_new, down_master, down_copy),
                            inner_rates[4],
                            inner_decays[4],
                        )

    def some_rows(step, _):
        at = (pl.ds(step * PAIR_ROWS, PAIR_ROWS),)
        update(
            [gate_grads[(k,) + at] for k in range(REPLICA_GROUPS)],
            at,
            gate_first,
            gate_second,
            gate_weight,
            gate_moment,
            (gate_first_new, gate_second_new, gate_delta, gate_moment_new, gate_master, gate_copy),
            inner_rates[3],
            inner_decays[3],
        )
        return 0

    lax.fori_loop(0, down_weight.shape[0] // PAIR_ROWS, some_rows, 0)


def feed_update(place, own, other, gating, down):
    rows, _, hidden = gating[2].shape
    size = 32 if rows % 32 == 0 else 16
    steps = rows // size
    own_list = [value for chunk in own for value in chunk]
    other_list = [value for chunk in other for value in chunk]
    plane = pl.BlockSpec((size, hidden), lambda i, p: (i, 0))
    pair = pl.BlockSpec((size, 2, hidden), lambda i, p: (i, 0, 0))
    stack = pl.BlockSpec((REPLICA_GROUPS, size, hidden), lambda i, p: (0, i, 0))
    stack_pair = pl.BlockSpec((REPLICA_GROUPS, size, 2, hidden), lambda i, p: (0, i, 0, 0))
    shape = lambda value, dtype=f32: jax.ShapeDtypeStruct(value.shape, dtype)
    return pl.pallas_call(
        feed_update_kernel,
        grid_spec=pltpu.PrefetchScalarGridSpec(
            num_scalar_prefetch=1,
            grid=(steps,),
            in_specs=[
                pl.BlockSpec((size, value.shape[1]), lambda i, p: (i, 0)) for value in own_list + other_list
            ]
            + [stack_pair, stack_pair, pair, pair, stack, stack, plane, plane],
            out_specs=[stack_pair, stack_pair, pair, pair, pair, pair, stack, stack, plane, plane, plane, plane],
            scratch_shapes=[pltpu.VMEM((REPLICA_GROUPS, size, 2, hidden), f32)],
        ),
        out_shape=[
            shape(gating[0]),
            shape(gating[1]),
            shape(gating[2]),
            shape(gating[2]),
            shape(gating[2]),
            shape(gating[2], low_type),
            shape(down[0]),
            shape(down[1]),
            shape(down[2]),
            shape(down[2]),
            shape(down[2]),
            shape(down[2], low_type),
        ],
        compiler_params=params(),
        cost_estimate=cost(0, rows * hidden * 3 * 90),
        name="feed_update",
    )(place, *own_list, *other_list, *gating, *down)


def optimize(weight, grad, first, second, moment, rate, decay):
    first_new, second_new, step = adam_step(grad, first, second, lambda value: 1.0 / value)
    delta = mean_step(jnp.sum(step, axis=0), weight, rate, decay)
    moment_new, weight_new = outer_step(weight, delta, moment)
    return (first_new, second_new, delta, moment_new, weight_new, weight_new.astype(low_type))


def doc_layout(lengths, token_length):
    ends = jnp.cumsum(lengths)
    starts = ends - lengths
    places = jnp.arange(token_length, dtype=jnp.int32)
    segment = jnp.sum((places[:, None] >= ends[None, :]).astype(jnp.int32), axis=1)
    member = (segment[:, None] == jnp.arange(lengths.shape[0], dtype=jnp.int32)[None, :]).astype(
        jnp.int32
    )
    offset = jnp.sum(member * starts[None, :], axis=1)
    return offset, places - offset


def rope_tables(position):
    half = HEAD_WIDTH // 2
    frequency = rope_base ** (-2.0 * jnp.arange(half, dtype=f32) / HEAD_WIDTH)
    angle = position.astype(f32)[:, None] * frequency[None, :]
    cosine, sine = jnp.cos(angle), jnp.sin(angle)
    gap = jnp.zeros((angle.shape[0], HALF - half), f32)
    return (
        jnp.concatenate([cosine, gap, cosine, gap], axis=1),
        jnp.concatenate([-sine, gap, sine, gap], axis=1),
    )


def norm_inverse(value):
    return lax.rsqrt(jnp.mean(value * value, axis=-1, keepdims=True) + epsilon)


def norm_backward(value, inverse, gain, grad_normed):
    scaled = gain * grad_normed
    return inverse * scaled - value * inverse**3 * jnp.mean(scaled * value, axis=-1, keepdims=True)


def per_device(
    tokens,
    cotangent,
    doc_lengths,
    query_weight,
    keyvalue_weight_full,
    output_weight,
    gating_weight,
    down_weight,
    norm_gains,
    first_query,
    keyvalue_first_moment,
    first_output,
    first_gating,
    first_down,
    first_gains,
    second_query,
    keyvalue_second_moment,
    second_output,
    second_gating,
    second_down,
    second_gains,
    moment_query,
    keyvalue_outer_momentum,
    moment_output,
    moment_gating,
    moment_down,
    moment_gains,
):
    ring = lax.axis_size("ring")
    spot = lax.axis_index("ring")
    side = lax.axis_index("pair")
    near = side == 0
    rows = query_weight.shape[0]
    width = tokens.shape[1]
    local_rows = tokens.shape[0]
    sequence = local_rows * lax.axis_size("tensor")
    plane = ("pair", "tensor")
    per_group = ring // REPLICA_GROUPS
    direct = per_group == 1 and (2 * rows) % LANES == 0
    zero = jnp.zeros_like(spot)
    mine = side * lax.axis_size("tensor") + lax.axis_index("tensor")
    place = jnp.stack([spot if direct else zero, side, spot if direct else zero, mine])
    blocks = ring if direct else 1
    hops = [1, 3, 2]

    def swap(value):
        return lax.ppermute(value, "pair", [(0, 1), (1, 0)])

    def across(value, bit):
        count = lax.axis_size("tensor")
        return lax.ppermute(value, "tensor", [(i, i ^ bit) for i in range(count)])

    def add(left, right):
        return (left.astype(f32) + right.astype(f32)).astype(low_type)

    def core_stage(kept, sent):
        shape = (2, 2, local_rows, width)
        kept, other = kept.reshape(shape), across(sent, 1).reshape(shape)
        cut = local_rows // 2
        spans = [
            (slice(None), 0, slice(None, cut)),
            (slice(None), 1, slice(None, cut)),
            (0, slice(None), slice(cut, None)),
            (1, slice(None), slice(cut, None)),
        ]
        return [add(kept[span], other[span]) for span in spans]

    def chip_stage(parts, *earlier):
        by_x, by_y = after((across(parts[1], 2), swap(parts[3])), *earlier)
        return add(parts[0], by_x), add(parts[2], by_y)

    def last_stage(parts, *earlier):
        one, two = parts
        by_y, by_x = after((swap(one[1]), across(two[1], 2)), *earlier)
        return jnp.concatenate(
            [one[0].astype(f32) + by_y.astype(f32), two[0].astype(f32) + by_x.astype(f32)], axis=0
        )

    def hop(value, step):
        return lax.ppermute(value, "ring", [(i, (i + step) % ring) for i in range(ring)])

    def halves(kept, sent):
        other = swap(sent)
        return jnp.concatenate([jnp.where(near, kept, other), jnp.where(near, other, kept)], axis=0)

    def gather(shard):
        return lax.all_gather(shard, "ring", axis=0, tiled=True)

    def gather_hops(shard):
        if not direct:
            return [gather(shard)]
        found = [shard] + [None] * (ring - 1)
        for step in hops:
            found[step] = hop(shard, step)
        return found

    def relay(found):
        if not direct:
            return [gather(found[0])] if len(found) == 1 and found[0].shape[0] == 2 * rows else found
        return found + [hop(found[-1], 1)]

    def gather_first(value):
        cut = local_rows // 2
        return value, across(value[:cut], 2), swap(value[cut:])

    def gather_second(parts):
        value, by_x, by_y = parts
        cut = local_rows // 2
        one = jnp.stack([value[:cut], by_x])
        two = jnp.stack([value[cut:], by_y])
        return one, two, swap(one), across(two, 2)

    def gather_last(parts):
        one, two, one_y, two_x = parts
        ones = [one[0], one[1], one_y[0], one_y[1]]
        twos = [two[0], two_x[0], two[1], two_x[1]]
        mine = jnp.concatenate([half for pair in zip(ones, twos) for half in pair], axis=0)
        other = across(mine, 1)
        found = []
        for start in range(0, mine.shape[0], local_rows):
            found += [mine[start : start + local_rows], other[start : start + local_rows]]
        return jnp.concatenate(found, axis=0)

    def sides(grads):
        if direct:
            return grads[1::2], grads[0::2]
        whole = grads[0].reshape(ring, 2, rows, -1)
        return (lax.dynamic_index_in_dim(whole, 1 - side, 1, False), lax.dynamic_index_in_dim(whole, side, 1, False))

    def deliver(grads):
        if not direct:
            whole = lax.all_to_all(grads, "ring", split_axis=0, concat_axis=0, tiled=True).astype(f32)
            whole = whole.reshape((REPLICA_GROUPS, per_group) + whole.shape[1:])
            whole = jnp.sum(whole, axis=1).astype(low_type)
            return [whole[k] for k in range(REPLICA_GROUPS)]
        found = [grads[0]] + [None] * (ring - 1)
        for step in hops:
            found[step] = hop(grads[step], -step)
        return found

    def plane_sum(value):
        count = lax.axis_size("tensor")
        bit = 1
        while bit < count:
            value = value + across(value, bit)
            bit *= 2
        return value + swap(value)

    tokens_all = lax.all_gather(tokens, plane, axis=0, tiled=True)

    flat = HEADS * HEAD_WIDTH
    query_halves = [query_weight[:, :flat], query_weight[:, flat:]]
    pair_halves = [
        keyvalue_weight_full[:, :, :HEAD_WIDTH].reshape(rows, 2 * HEAD_WIDTH),
        keyvalue_weight_full[:, :, HEAD_WIDTH:].reshape(rows, 2 * HEAD_WIDTH),
    ]
    gain_columns = jnp.concatenate(
        [norm_gains.T, jnp.zeros((rows, PACK - flat - 2 * HEAD_WIDTH - 2), f32)], axis=1
    )
    packed = [
        jnp.concatenate([q, p, gain_columns, o], axis=1).astype(low_type)
        for q, p, o in zip(query_halves, pair_halves, [output_weight[:, :flat], output_weight[:, flat:]])
    ]
    kept, sent = (jnp.where(near, packed[0], packed[1]), jnp.where(near, packed[1], packed[0]))
    attention_shard = halves(kept, sent)
    attention_blocks = gather_hops(attention_shard)

    feed_parts = pack_feed(after(place, attention_shard), gating_weight, down_weight)
    kept, sent = feed_parts[: len(CHUNKS)], feed_parts[len(CHUNKS) :]
    feed_shards = []
    last = tokens_all
    for a, b in zip(kept, sent):
        last = halves(a, after(b, last))
        feed_shards.append(last)
    one = relay([after(feed_shards[0], attention_blocks)])
    cotangent_parts = gather_first(after(cotangent, tokens_all))

    other_lengths = swap(doc_lengths)
    lengths = [jnp.where(near, doc_lengths[0], other_lengths[0]), jnp.where(near, other_lengths[0], doc_lengths[0])]
    layouts = [doc_layout(value, sequence) for value in lengths]
    starts = jnp.broadcast_to(
        jnp.concatenate([value[0] for value in layouts])[None, :], (8, 2 * sequence)
    ).astype(jnp.int32)
    cosine, sine = rope_tables(jnp.concatenate([value[1] for value in layouts]))

    tokens_late = after(tokens_all, feed_parts)
    normed_one, heads, gains, wide = project(place, tokens_late, attention_blocks, cosine, sine)
    gain_one, gain_two = gains[0], gains[1]
    heads = after(heads, cotangent_parts, feed_shards[0])
    mixed, totals, *partial = attend(place, heads, starts, attention_blocks, sequence)
    cotangent_parts = gather_second(cotangent_parts)
    partial = after(partial, cotangent_parts, feed_shards[1:], one)
    parts = core_stage(*partial)
    one = relay(one)
    cotangent_all = gather_last(after(cotangent_parts, parts))
    parts = chip_stage(parts, cotangent_all, one)
    one = relay(one)
    attention = last_stage(parts, one)

    hidden = tokens.astype(f32)
    inverse_one = norm_inverse(hidden)
    hidden_one = hidden + attention
    inverse_two = norm_inverse(hidden_one)
    normed_two = (hidden_one * inverse_two * gain_two).astype(low_type)
    two = relay([after(feed_shards[1], one)])
    normed_parts = gather_second(after(gather_first(normed_two)))
    normed_two_all = gather_last(after(normed_parts, two))
    hid, grad_pair = feed(place, normed_two_all, cotangent_all, one)
    two = relay(two)
    grad_pair = after(grad_pair, two)
    two = relay(two)
    theirs, mine = sides(weight_grad(place, blocks, [(normed_two_all, grad_pair), (cotangent_all, hid)]))
    theirs_one = deliver(theirs)
    others_one = [swap(theirs_one[0])]
    normed_late = after(normed_two_all, theirs[0])
    hid_two, grad_pair_two = feed(place, normed_late, cotangent_all, two)
    partial = spread(place, after([grad_pair, grad_pair_two], others_one), [one, two], 0)
    partial = after(partial, theirs_one)
    others_one += [swap(after(value, partial)) for value in theirs_one[1:]]
    mine_one = deliver(after(mine, theirs_one))
    parts = core_stage(*partial)
    theirs, mine = sides(
        weight_grad(place, blocks, [(normed_two_all, after(grad_pair_two, *parts)), (cotangent_all, hid_two)])
    )
    parts = chip_stage(parts, theirs[0], mine_one[1::2])
    theirs_two = deliver(after(theirs, mine_one[1:]))
    feed_partial = spread(place, after([hid, hid_two], *parts), [one, two], 2)
    grad_normed_two = last_stage(parts, *feed_partial)
    grad_normed_two = after(grad_normed_two, mine_one, others_one[1])

    grad_hidden_one = cotangent.astype(f32) + norm_backward(
        hidden_one, inverse_two, gain_two, grad_normed_two
    )
    grad_gain_two = jnp.sum(grad_normed_two * hidden_one * inverse_two, axis=0)
    grad_hidden_all = lax.all_gather(grad_hidden_one.astype(low_type), plane, axis=0, tiled=True)
    grad_hidden_all = after(grad_hidden_all, theirs_two, others_one)
    mine_two = deliver(after(mine, grad_hidden_all))
    others_two = [swap(after(value, grad_hidden_all)) for value in theirs_two]

    grad_query, grad_pair = attend_grad(
        place, grad_hidden_all, heads, totals, starts, cosine, sine, attention_blocks, sequence
    )
    *partial, gain_sums = project_grad(place, grad_query, grad_pair, tokens_all, wide)
    partial = after(partial, others_two[:3], mine_two)
    parts = core_stage(*partial)
    project_theirs, project_mine = sides(
        weight_grad(
            place,
            blocks,
            [(normed_one, after(grad_query, *parts)), (normed_one, grad_pair)],
            projection_selector(),
        )
    )
    parts = chip_stage(parts, project_theirs[0])
    project_theirs = deliver(project_theirs)
    project_mine = deliver(project_mine)
    output_theirs, output_mine = sides(
        weight_grad(place, blocks, [(grad_hidden_all, after(mixed, *parts))], output_selector())
    )
    feed_parts = core_stage(*after(feed_partial, output_theirs[0]))
    grad_normed_one = last_stage(parts, output_theirs[0], feed_parts)
    output_theirs, output_mine = deliver(output_theirs), deliver(output_mine)

    token_grad = (
        grad_hidden_one + norm_backward(hidden, inverse_one, gain_one, grad_normed_one)
    ).astype(low_type)

    grad_gains = jnp.stack([jnp.sum(gain_sums, axis=0), grad_gain_two], axis=0)
    grad_gains = plane_sum(grad_gains)
    start = (2 * spot + side) * rows
    if direct:
        found = [grad_gains] + [hop(grad_gains, -step) for step in range(1, ring)]
        found = [lax.dynamic_slice_in_dim(value, start, rows, 1) for value in found]
        gains_total = jnp.roll(jnp.stack(found), spot, axis=0)
    else:
        gains_all = lax.all_gather(grad_gains, "ring", axis=0, tiled=False)
        gains_all = jnp.sum(gains_all.reshape(REPLICA_GROUPS, per_group, 2, width), axis=1)
        gains_total = lax.dynamic_slice_in_dim(gains_all, start, rows, 2)

    updated = feed_update(
        after(place, grad_normed_one, project_theirs, gains_total, others_two),
        [mine_one, mine_two],
        [others_one, others_two],
        (first_gating, second_gating, gating_weight, moment_gating),
        (first_down, second_down, down_weight, moment_down),
    )
    project_other = [swap(value) for value in project_theirs]
    output_other = [swap(after(value, updated[0])) for value in output_theirs]
    feed_parts = chip_stage(feed_parts, updated[0])
    feed_out = last_stage(feed_parts)
    block_output = (hidden_one + feed_out).astype(low_type)

    def slots_to_groups(own, other):
        both = [jnp.stack(own), jnp.stack(other)]
        both = [jnp.where(near, both[0], both[1]), jnp.where(near, both[1], both[0])]
        if direct:
            both = [jnp.roll(value, spot, axis=0) for value in both]
        return [value.astype(f32) for value in both]

    project_totals = slots_to_groups(project_mine, project_other)
    output_totals = slots_to_groups(output_mine, output_other)
    query_total = jnp.concatenate([value[..., :flat] for value in project_totals], axis=-1)
    pair_total = jnp.concatenate(
        [
            value[..., flat : flat + 2 * HEAD_WIDTH].reshape(REPLICA_GROUPS, rows, 2, HEAD_WIDTH)
            for value in project_totals
        ],
        axis=-1,
    )
    output_total = jnp.concatenate(output_totals, axis=-1)

    qry = optimize(
        query_weight, query_total, first_query, second_query, moment_query, inner_rates[0], inner_decays[0]
    )
    kvl = optimize(
        keyvalue_weight_full,
        pair_total,
        keyvalue_first_moment,
        keyvalue_second_moment,
        keyvalue_outer_momentum,
        inner_rates[1],
        inner_decays[1],
    )
    out = optimize(
        output_weight, output_total, first_output, second_output, moment_output, inner_rates[2], inner_decays[2]
    )
    gns = optimize(
        norm_gains, gains_total, first_gains, second_gains, moment_gains, inner_rates[5], inner_decays[5]
    )
    gat = updated[:6]
    dwn = updated[6:]
    return (block_output, token_grad, *qry, *kvl, *out, *gat, *dwn, *gns)


def solution(mesh):
    shape = (mesh.shape["dp"] // 2, 2, mesh.shape["tensor"])
    mesh = Mesh(mesh.devices.reshape(shape), ("ring", "pair", "tensor"))
    dp = ("ring", "pair")
    matrix = P(dp, "tensor")
    pair = P(dp, None, "tensor")
    stack = P(None, dp, "tensor")
    stack_pair = P(None, dp, None, "tensor")
    tokens = P(("ring", "pair", "tensor"), None)
    gains = P(None, dp)
    stack_gains = P(None, None, dp)
    weights = (matrix, pair, matrix, pair, matrix, gains)
    states = (stack, stack_pair, stack, stack_pair, stack, stack_gains)
    outs = []
    for weight, state in zip(weights, states):
        outs += [state, state, weight, weight, weight, weight]
    return jax.shard_map(
        per_device,
        mesh=mesh,
        in_specs=(tokens, tokens, P(dp, None), *weights, *states, *states, *weights),
        out_specs=(tokens, tokens, *outs),
        check_vma=False,
    )
```

```python
import functools
import math

import jax
import jax.numpy as jnp
import numpy as np
from jax import lax
from jax.experimental import pallas as pl
from jax.experimental.pallas import tpu as pltpu
from jax.sharding import Mesh, PartitionSpec as P

HEAD_WIDTH = 80
REPLICA_GROUPS = 4
STEP = 8
LANES = 128
HEADS = 4
TILE = 256
PACK = 512
WIDE = 768
HALF = 64
VMEM_BYTES = 58 * 2**20

epsilon = 1e-05
rope_base = 1000000.0
beta_one = 0.9
beta_two = 0.95
adam_epsilon = 1e-08
outer_mu = 0.9
outer_rate = 0.7
inner_rates = (0.05, 0.05, 0.2, 0.05, 0.05, 0.5)
inner_decays = (0.1, 0.1, 0.1, 0.1, 0.1, 0.0)
correct_one = 1.0 - beta_one**STEP
correct_two = 1.0 - beta_two**STEP

low_type = jnp.bfloat16
f32 = jnp.float32

NN = (((1,), (0,)), ((), ()))
NT = (((1,), (1,)), ((), ()))
TN = (((0,), (0,)), ((), ()))

CHUNKS = ((0, 3), (3, 7))


def after(value, *earlier):
    return lax.optimization_barrier((value, earlier))[0]


def dot(left, right, dims=NN):
    return lax.dot_general(left, right, dims, preferred_element_type=f32)


def params(**kwargs):
    return pltpu.CompilerParams(vmem_limit_bytes=VMEM_BYTES, **kwargs)


COST_SHARE = 1.0


def cost(flops, size):
    return pl.CostEstimate(
        flops=int(COST_SHARE * flops), bytes_accessed=int(COST_SHARE * size), transcendentals=0
    )


SHORT = pl.CostEstimate(flops=1, bytes_accessed=1, transcendentals=0)


def resident(shape):
    zeros = (0,) * len(shape)
    return pl.BlockSpec(shape, lambda *_: zeros, pipeline_mode=pl.Buffered(1))


def projection_selector():
    table = np.zeros((PACK, WIDE), np.float32)
    for head in range(HEADS + 1):
        for place in range(HEAD_WIDTH):
            half, rest = divmod(place, HEAD_WIDTH // 2)
            table[head * HEAD_WIDTH + place, head * LANES + half * HALF + rest] = 1.0
    for place in range(HEAD_WIDTH):
        table[(HEADS + 1) * HEAD_WIDTH + place, (HEADS + 1) * LANES + place] = 1.0
    return table


def output_selector():
    table = np.zeros((HEADS * HEAD_WIDTH, HEADS * LANES), np.float32)
    for head in range(HEADS):
        for place in range(HEAD_WIDTH):
            table[head * HEAD_WIDTH + place, head * LANES + place] = 1.0
    return table


OUTPUT_PACK = 384


def gradient_selectors():
    project, output = projection_selector(), output_selector()
    padded = np.zeros((OUTPUT_PACK, HEADS * LANES), np.float32)
    padded[: output.shape[0]] = output
    return ((0, project[:, : HEADS * LANES]), (0, project[:, HEADS * LANES :]), (0, None), (1, padded))


def gains_selector():
    table = np.zeros((8, PACK), np.float32)
    table[0, (HEADS + 2) * HEAD_WIDTH] = 1.0
    table[1, (HEADS + 2) * HEAD_WIDTH + 1] = 1.0
    return table


def seen_from(place_ref, piece):
    return lax.bitwise_xor(piece, place_ref[3])


def piece_specs(width, piece):
    return [pl.BlockSpec((TILE, width), lambda *at: (lax.shift_right_logical(piece(*at), 1), 0))] * 2


def piece_shapes(total, width):
    return [jax.ShapeDtypeStruct((total // 2, width), low_type)] * 2


def write_piece(piece, kept, sent, value):
    odd = lax.bitwise_and(piece, 1)

    @pl.when(odd == 0)
    def _():
        kept[...] = value

    @pl.when(odd == 1)
    def _():
        sent[...] = value


def first_row(place, step, blocks, rows):
    return pl.multiple_of(lax.rem(place - step + blocks, blocks) * rows, LANES if blocks > 1 else rows)


def assemble(place, blocks, target):
    rows = blocks[0].shape[0]
    for step, block in enumerate(blocks):
        target[pl.ds(first_row(place, step, len(blocks), rows), rows), :] = block[...]


def projection_kernel(count, place_ref, tokens, *refs):
    blocks, (select, pick, cosine, sine, normed, heads, gains, wide) = refs[:count], refs[count:]

    @pl.when(pl.program_id(0) == 0)
    def _():
        rows = blocks[0].shape[0]
        for step, block in enumerate(blocks):
            start = first_row(place_ref[0], step, count, rows)
            value = block[...]
            wide[pl.ds(start, rows), :] = dot(value, select[...]).astype(low_type)
            gains[:, pl.ds(start, rows)] = dot(pick[...], value, NT)

    value = tokens[...].astype(f32)
    inverse = lax.rsqrt(jnp.mean(value * value, axis=-1, keepdims=True) + epsilon)
    low = (value * inverse * gains[0:1, :]).astype(low_type)
    normed[...] = low
    result = dot(low, wide[...])
    cos_tile = cosine[...]
    sin_tile = sine[...]
    for head in range(HEADS + 1):
        part = result[:, head * LANES : (head + 1) * LANES]
        turned = part * cos_tile + pltpu.roll(part, HALF, 1) * sin_tile
        heads[:, head * LANES : (head + 1) * LANES] = turned.astype(low_type)
    heads[:, (HEADS + 1) * LANES :] = result[:, (HEADS + 1) * LANES :].astype(low_type)


def project(place, tokens, blocks, cosine, sine):
    total, width = tokens.shape
    tile = lambda columns: pl.BlockSpec((TILE, columns), lambda i, p: (i, 0))
    return pl.pallas_call(
        functools.partial(projection_kernel, len(blocks)),
        grid_spec=pltpu.PrefetchScalarGridSpec(
            num_scalar_prefetch=1,
            grid=(total // TILE,),
            in_specs=[tile(width)]
            + [resident(block.shape) for block in blocks]
            + [
                resident((PACK, WIDE)),
                resident((8, PACK)),
                tile(LANES),
                tile(LANES),
            ],
            out_specs=[
                tile(width),
                tile(WIDE),
                pl.BlockSpec((8, width), lambda *_: (0, 0)),
                pl.BlockSpec((width, WIDE), lambda *_: (0, 0)),
            ],
        ),
        out_shape=[
            jax.ShapeDtypeStruct((total, width), low_type),
            jax.ShapeDtypeStruct((total, WIDE), low_type),
            jax.ShapeDtypeStruct((8, width), f32),
            jax.ShapeDtypeStruct((width, WIDE), low_type),
        ],
        compiler_params=params(),
        cost_estimate=cost(2 * total * width * WIDE, 4 * total * width + 3 * width * WIDE * 2),
        name="projection",
    )(
        place,
        tokens,
        *blocks,
        jnp.asarray(projection_selector(), low_type),
        jnp.asarray(gains_selector(), low_type),
        cosine,
        sine,
    )


SCORE_SCALE = math.log2(math.e) / math.sqrt(HEAD_WIDTH)
GRAD_SCALE = 1.0 / math.sqrt(HEAD_WIDTH)


def allowed_pairs(block, width, starts):
    key_index = lax.broadcasted_iota(jnp.int32, (width, TILE), 0)
    row_index = block * TILE + lax.broadcasted_iota(jnp.int32, (1, TILE), 1)
    return (key_index >= starts) & (key_index <= row_index)


def widen_output(place_ref, blocks, select, wide):
    @pl.when((pl.program_id(0) == 0) & (pl.program_id(1) == 0))
    def _():
        rows = blocks[0].shape[0]
        for step, block in enumerate(blocks):
            start = first_row(place_ref[0], step, len(blocks), rows)
            wide[pl.ds(start, rows), :] = dot(block[...], select[...]).astype(low_type)


def attention_kernel(count, blocks_per, place_ref, query, key, value, starts, *refs):
    blocks, (select, mixed, totals, kept, sent, wide) = refs[:count], refs[count:]
    widen_output(place_ref, blocks, select, wide)

    for block in range(blocks_per):

        @pl.when(pl.program_id(1) == block)
        def _(block=block):
            width = (block + 1) * TILE
            allowed = allowed_pairs(block, width, starts[0:1, :])
            keys = key[0:width, :]
            values = value[0:width, :]
            for head in range(HEADS):
                lanes = slice(head * LANES, (head + 1) * LANES)
                scores = dot(keys, query[:, lanes], NT) * SCORE_SCALE
                scores = jnp.where(allowed, scores, -1e30)
                top = jnp.max(scores, axis=0, keepdims=True)
                expo = jnp.exp2(scores - top)
                total = jnp.sum(expo, axis=0, keepdims=True)
                out = dot(values, expo.astype(low_type), TN) * (1.0 / total)
                mixed[:, lanes] = out.T.astype(low_type)
                totals[head : head + 1, :] = top + jnp.log2(total)

    piece = pl.program_id(0) * blocks_per + pl.program_id(1)
    value = dot(mixed[...], wide[...], NT).astype(low_type)
    write_piece(seen_from(place_ref, piece), kept, sent, value)


def attend(place, heads, starts, blocks, sequence):
    total = heads.shape[0]
    width = blocks[0].shape[0] * len(blocks)
    per = sequence // TILE
    tile = lambda size, column: pl.BlockSpec((TILE, size), lambda s, i, *_: (s * per + i, column))
    full = lambda column: pl.BlockSpec((sequence, LANES), lambda s, i, *_: (s, column))
    line = pl.BlockSpec((8, TILE), lambda s, i, *_: (0, s * per + i))
    return pl.pallas_call(
        functools.partial(attention_kernel, len(blocks), per),
        grid_spec=pltpu.PrefetchScalarGridSpec(
            num_scalar_prefetch=1,
            grid=(total // sequence, per),
            in_specs=[
                tile(HEADS * LANES, 0),
                full(HEADS),
                full(HEADS + 1),
                line,
            ]
            + [resident(block.shape) for block in blocks]
            + [resident((HEADS * HEAD_WIDTH, HEADS * LANES))],
            out_specs=[tile(HEADS * LANES, 0), line]
            + piece_specs(width, lambda s, i, p: seen_from(p, s * per + i)),
            scratch_shapes=[pltpu.VMEM((width, HEADS * LANES), low_type)],
        ),
        out_shape=[
            jax.ShapeDtypeStruct((total, HEADS * LANES), low_type),
            jax.ShapeDtypeStruct((8, total), f32),
        ]
        + piece_shapes(total, width),
        compiler_params=params(),
        cost_estimate=cost(20e9, 4 * total * width),
        name="attention",
    )(place, heads, heads, heads, starts, *blocks, jnp.asarray(output_selector(), low_type))


def attention_grad_kernel(
    count,
    blocks_per,
    place_ref,
    grad_hidden,
    query,
    key,
    value,
    totals,
    starts,
    cosine,
    sine,
    cos_all,
    sin_all,
    *refs,
):
    blocks, (select, grad_query, grad_pair, wide, key_sum, value_sum) = refs[:count], refs[count:]
    widen_output(place_ref, blocks, select, wide)

    @pl.when(pl.program_id(1) == 0)
    def _():
        key_sum[...] = jnp.zeros_like(key_sum)
        value_sum[...] = jnp.zeros_like(value_sum)

    grad_mixed = dot(grad_hidden[...], wide[...]).astype(low_type)
    cos_tile = cosine[...]
    sin_tile = sine[...]
    for block in range(blocks_per):

        @pl.when(pl.program_id(1) == block)
        def _(block=block):
            width = (block + 1) * TILE
            allowed = allowed_pairs(block, width, starts[0:1, :])
            keys = key[0:width, :]
            values = value[0:width, :]
            key_part = jnp.zeros((width, LANES), f32)
            value_part = jnp.zeros((width, LANES), f32)
            for head in range(HEADS):
                lanes = slice(head * LANES, (head + 1) * LANES)
                queries = query[:, lanes]
                grads = grad_mixed[:, lanes]
                scores = dot(keys, queries, NT) * SCORE_SCALE
                scores = jnp.where(allowed, scores, -1e30)
                prob = jnp.exp2(scores - totals[head : head + 1, :])
                grad_prob = dot(values, grads, NT)
                inner = jnp.sum(prob * grad_prob, axis=0, keepdims=True)
                grad_scores = (prob * (grad_prob - inner)).astype(low_type)
                key_part = key_part + dot(grad_scores, queries)
                value_part = value_part + dot(prob.astype(low_type), grads)
                turned = dot(keys, grad_scores, TN).T * GRAD_SCALE
                turned = turned * cos_tile - pltpu.roll(turned, HALF, 1) * sin_tile
                grad_query[:, lanes] = turned.astype(low_type)
            key_sum[0:width, :] += key_part
            value_sum[0:width, :] += value_part

    @pl.when(pl.program_id(1) == blocks_per - 1)
    def _():
        grad_key = key_sum[...] * GRAD_SCALE
        grad_key = grad_key * cos_all[...] - pltpu.roll(grad_key, HALF, 1) * sin_all[...]
        grad_pair[:, :LANES] = grad_key.astype(low_type)
        grad_pair[:, LANES:] = value_sum[...].astype(low_type)


def attend_grad(place, grad_hidden, heads, totals, starts, cosine, sine, blocks, sequence):
    total, width = grad_hidden.shape
    per = sequence // TILE
    tile = lambda size, column: pl.BlockSpec((TILE, size), lambda s, i, p: (s * per + i, column))
    full = lambda size, column: pl.BlockSpec((sequence, size), lambda s, i, p: (s, column))
    line = pl.BlockSpec((8, TILE), lambda s, i, p: (0, s * per + i))
    return pl.pallas_call(
        functools.partial(attention_grad_kernel, len(blocks), per),
        grid_spec=pltpu.PrefetchScalarGridSpec(
            num_scalar_prefetch=1,
            grid=(total // sequence, per),
            in_specs=[
                tile(width, 0),
                tile(HEADS * LANES, 0),
                full(LANES, HEADS),
                full(LANES, HEADS + 1),
                line,
                line,
                tile(LANES, 0),
                tile(LANES, 0),
                full(LANES, 0),
                full(LANES, 0),
            ]
            + [resident(block.shape) for block in blocks]
            + [resident((HEADS * HEAD_WIDTH, HEADS * LANES))],
            out_specs=[tile(HEADS * LANES, 0), full(2 * LANES, 0)],
            scratch_shapes=[
                pltpu.VMEM((width, HEADS * LANES), low_type),
                pltpu.VMEM((sequence, LANES), f32),
                pltpu.VMEM((sequence, LANES), f32),
            ],
        ),
        out_shape=[
            jax.ShapeDtypeStruct((total, HEADS * LANES), low_type),
            jax.ShapeDtypeStruct((total, 2 * LANES), low_type),
        ],
        compiler_params=params(),
        cost_estimate=cost(30e9, 4 * total * width),
        name="attention_grad",
    )(
        place,
        grad_hidden,
        heads,
        heads,
        heads,
        totals,
        starts,
        cosine,
        sine,
        cosine,
        sine,
        *blocks,
        jnp.asarray(output_selector(), low_type),
    )


def projection_grad_kernel(place_ref, grad_query, grad_pair, tokens, wide, kept, sent, gain_sums):
    grad = dot(grad_query[...], wide[:, : HEADS * LANES], NT)
    grad = grad + dot(grad_pair[...], wide[:, HEADS * LANES :], NT)
    write_piece(seen_from(place_ref, pl.program_id(0)), kept, sent, grad.astype(low_type))
    value = tokens[...].astype(f32)
    inverse = lax.rsqrt(jnp.mean(value * value, axis=-1, keepdims=True) + epsilon)
    product = grad * (value * inverse)
    sums = jnp.sum(product.reshape(TILE // 8, 8, product.shape[1]), axis=0)

    @pl.when(pl.program_id(0) == 0)
    def _():
        gain_sums[...] = sums

    @pl.when(pl.program_id(0) != 0)
    def _():
        gain_sums[...] += sums


def project_grad(place, grad_query, grad_pair, tokens, wide):
    total, width = tokens.shape
    tile = lambda columns: pl.BlockSpec((TILE, columns), lambda i, *_: (i, 0))
    return pl.pallas_call(
        projection_grad_kernel,
        grid_spec=pltpu.PrefetchScalarGridSpec(
            num_scalar_prefetch=1,
            grid=(total // TILE,),
            in_specs=[
                tile(HEADS * LANES),
                tile(2 * LANES),
                tile(width),
                resident((width, WIDE)),
            ],
            out_specs=piece_specs(width, lambda i, p: seen_from(p, i)) + [pl.BlockSpec((8, width), lambda i, *_: (0, 0))],
        ),
        out_shape=piece_shapes(total, width) + [jax.ShapeDtypeStruct((8, width), f32)],
        compiler_params=params(),
        cost_estimate=SHORT,
        name="projection_grad",
    )(place, grad_query, grad_pair, tokens, wide)


def pack_kernel(place_ref, gating, down, *outs):
    kept, sent = outs[: len(CHUNKS)], outs[len(CHUNKS) :]

    def write(targets):
        for (first, last), target in zip(CHUNKS, targets):
            count = last - first
            for tile in range(first, last):
                lanes = slice(tile * LANES, (tile + 1) * LANES)
                place = (tile - first) * 2 * LANES
                target[:, place : place + LANES] = gating[:, 0, lanes].astype(low_type)
                target[:, place + LANES : place + 2 * LANES] = gating[:, 1, lanes].astype(low_type)
                place = (2 * count + tile - first) * LANES
                target[:, place : place + LANES] = down[:, lanes].astype(low_type)

    @pl.when(pl.program_id(0) == 0)
    def _():
        write(sent)

    @pl.when(pl.program_id(0) == 1)
    def _():
        write(kept)


def pack_feed(place, gating, down):
    rows, _, hidden = gating.shape
    half = hidden // 2
    side = lambda i, place_ref: jnp.where(i == 0, 1 - place_ref[1], place_ref[1])
    shapes = [(rows, 3 * LANES * (last - first)) for first, last in CHUNKS] * 2
    return pl.pallas_call(
        pack_kernel,
        grid_spec=pltpu.PrefetchScalarGridSpec(
            num_scalar_prefetch=1,
            grid=(2,),
            in_specs=[
                pl.BlockSpec((rows, 2, half), lambda i, p: (0, 0, side(i, p))),
                pl.BlockSpec((rows, half), lambda i, p: (0, side(i, p))),
            ],
            out_specs=[pl.BlockSpec(shape, lambda *_: (0, 0)) for shape in shapes],
        ),
        out_shape=[jax.ShapeDtypeStruct(shape, low_type) for shape in shapes],
        compiler_params=params(),
        cost_estimate=cost(0, 18 * rows * hidden),
        name="pack_feed",
    )(place, gating, down)


def feed_kernel(count, tiles, place_ref, normed, grad_out, *refs):
    blocks, (hidden, grad_pair, weights) = refs[:count], refs[count:]

    @pl.when(pl.program_id(0) == 0)
    def _():
        assemble(place_ref[0], blocks, weights)

    pair = dot(normed[...], weights[:, : 2 * tiles * LANES])
    grad_hidden = dot(grad_out[...], weights[:, 2 * tiles * LANES :])
    for tile in range(tiles):
        place = 2 * tile * LANES
        gate = pair[:, place : place + LANES]
        up = pair[:, place + LANES : place + 2 * LANES]
        grad = grad_hidden[:, tile * LANES : (tile + 1) * LANES]
        sigma = 1.0 / (1.0 + jnp.exp(-gate))
        silu = gate * sigma
        hidden[:, tile * LANES : (tile + 1) * LANES] = (silu * up).astype(low_type)
        grad_gate = grad * up * sigma * (1.0 + gate * (1.0 - sigma))
        grad_pair[:, place : place + LANES] = grad_gate.astype(low_type)
        grad_pair[:, place + LANES : place + 2 * LANES] = (grad * silu).astype(low_type)


def feed(place, normed, grad_out, blocks):
    total, width = normed.shape
    rows, columns = blocks[0].shape
    tiles = columns // (3 * LANES)
    tile = lambda size: pl.BlockSpec((TILE, size), lambda i, p: (i, 0))
    return pl.pallas_call(
        functools.partial(feed_kernel, len(blocks), tiles),
        grid_spec=pltpu.PrefetchScalarGridSpec(
            num_scalar_prefetch=1,
            grid=(total // TILE,),
            in_specs=[tile(width), tile(width)] + [resident(block.shape) for block in blocks],
            out_specs=[tile(tiles * LANES), tile(2 * tiles * LANES)],
            scratch_shapes=[pltpu.VMEM((width, columns), low_type)],
        ),
        out_shape=[
            jax.ShapeDtypeStruct((total, tiles * LANES), low_type),
            jax.ShapeDtypeStruct((total, 2 * tiles * LANES), low_type),
        ],
        compiler_params=params(),
        cost_estimate=cost(2 * total * width * columns, 4 * total * width + 2 * width * columns),
        name="feed",
    )(place, normed, grad_out, *blocks)


def spread_kernel(counts, place_ref, *refs):
    parts = len(counts)
    values, rest = refs[:parts], refs[parts:]
    chunks = []
    for count in counts:
        chunks.append(rest[:count])
        rest = rest[count:]
    kept, sent, wholes = rest[0], rest[1], rest[2:]

    @pl.when(pl.program_id(0) == 0)
    def _():
        for blocks, whole in zip(chunks, wholes):
            assemble(place_ref[0], blocks, whole)

    total = dot(values[0][...], wholes[0][...], NT)
    for value, whole in zip(values[1:], wholes[1:]):
        total = total + dot(value[...], whole[...], NT)
    write_piece(pl.program_id(0), kept, sent, total.astype(low_type))


def spread(place, values, chunks, column):
    total = values[0].shape[0]
    width = chunks[0][0].shape[0] * len(chunks[0])
    tile = lambda size: pl.BlockSpec((TILE, size), lambda i, p: (i, 0))
    return pl.pallas_call(
        functools.partial(spread_kernel, tuple(len(blocks) for blocks in chunks)),
        grid_spec=pltpu.PrefetchScalarGridSpec(
            num_scalar_prefetch=1,
            grid=(total // TILE,),
            in_specs=[tile(value.shape[1]) for value in values]
            + [
                pl.BlockSpec(
                    (block.shape[0], value.shape[1]), lambda *_: (0, column), pipeline_mode=pl.Buffered(1)
                )
                for value, blocks in zip(values, chunks)
                for block in blocks
            ],
            out_specs=piece_specs(width, lambda i, p: i),
            scratch_shapes=[pltpu.VMEM((width, value.shape[1]), low_type) for value in values],
        ),
        out_shape=piece_shapes(total, width),
        compiler_params=params(),
        cost_estimate=SHORT,
        name="spread",
    )(place, *values, *[block for blocks in chunks for block in blocks])


ROW_TILE = 640


def weight_grad_kernel(spans, selected, split, place_ref, *refs):
    parts = len(spans)
    lefts, rights, rest = refs[:parts], refs[parts : 2 * parts], refs[2 * parts :]
    outs = rest[sum(selected) :]
    selects = [rest[sum(selected[:place])] if chosen else None for place, chosen in enumerate(selected)]

    def write(targets, value, columns, again):
        size = targets[0].shape[0]
        for place, target in enumerate(targets):
            rows = value[place * size : (place + 1) * size]
            if again:
                rows = rows + target[:, columns].astype(f32)
            target[:, columns] = rows.astype(low_type)

    for block in range(len(outs) // split):
        targets = outs[block * split : (block + 1) * split]

        @pl.when(pl.program_id(0) == block)
        def _(targets=targets):
            for place, (left, right) in enumerate(zip(lefts, rights)):
                value = dot(left[...], right[...], TN).astype(low_type)
                if selects[place] is not None:
                    value = dot(value, selects[place][...], NT)
                columns = slice(*spans[place])
                again = place and spans[place] == spans[place - 1]
                if split == 1:
                    write(targets, value, columns, again)
                    continue

                @pl.when(place_ref[1] == 0)
                def _(value=value, columns=columns, again=again):
                    write(targets, value, columns, again)

                @pl.when(place_ref[1] != 0)
                def _(value=value, columns=columns, again=again):
                    write(targets[::-1], value, columns, again)


def weight_grad(place, blocks, pairs, selects=()):
    total, width = pairs[0][0].shape
    rows = width // blocks
    split = 1 if blocks == 1 else 2
    row_tile = math.gcd(rows, ROW_TILE)
    row_tiles = rows // row_tile
    spans, end = [], 0
    for index, (_, right) in enumerate(pairs):
        if selects and index and selects[index][0] == selects[index - 1][0]:
            spans.append(spans[-1])
            continue
        size = selects[index][1].shape[0] if selects else right.shape[1]
        spans.append((end, end + size))
        end += size
    first = lambda b, r, p: lax.rem(p[0] - b + blocks, blocks) * row_tiles + r
    selected = [table is not None for _, table in selects] or [False] * len(pairs)
    extra = [jnp.asarray(table, low_type) for _, table in selects if table is not None]
    return pl.pallas_call(
        functools.partial(weight_grad_kernel, spans, selected, split),
        grid_spec=pltpu.PrefetchScalarGridSpec(
            num_scalar_prefetch=1,
            grid=(blocks, row_tiles),
            in_specs=[
                pl.BlockSpec((left.shape[0], row_tile), lambda b, r, p: (0, first(b, r, p))) for left, _ in pairs
            ]
            + [resident(right.shape) for _, right in pairs]
            + [resident(value.shape) for value in extra],
            out_specs=[pl.BlockSpec((row_tile // split, end), lambda b, r, p: (r, 0))] * (blocks * split),
        ),
        out_shape=[jax.ShapeDtypeStruct((rows // split, end), low_type)] * (blocks * split),
        compiler_params=params(),
        cost_estimate=cost(2 * total * width * end, 2 * total * (end + width * len(pairs))),
        name="weight_grad",
    )(place, *[left for left, _ in pairs], *[right for _, right in pairs], *extra)


ROOT_TWO = math.sqrt(correct_two)


def adam_step(grad, first, second, reciprocal):
    first_new = beta_one * first + (1.0 - beta_one) * grad
    second_new = beta_two * second + ((1.0 - beta_two) * grad) * grad
    root = second_new * lax.rsqrt(jnp.maximum(second_new, 1e-30)) + adam_epsilon * ROOT_TWO
    return first_new, second_new, first_new * reciprocal(root)


def mean_step(total, weight, rate, decay):
    return (rate * ROOT_TWO / correct_one / REPLICA_GROUPS) * total + (rate * decay) * weight


def outer_step(weight, delta, moment):
    moment_new = outer_mu * moment + delta
    return moment_new, weight - outer_rate * (delta + outer_mu * moment_new)


PAIR_ROWS = 4


def feed_update_kernel(place_ref, *refs):
    slots = REPLICA_GROUPS * len(CHUNKS)
    own, other, rest = refs[:slots], refs[slots : 2 * slots], refs[2 * slots :]
    (
        gate_first,
        gate_second,
        gate_weight,
        gate_moment,
        down_first,
        down_second,
        down_weight,
        down_moment,
        gate_first_new,
        gate_second_new,
        gate_delta,
        gate_moment_new,
        gate_master,
        gate_copy,
        down_first_new,
        down_second_new,
        down_delta,
        down_moment_new,
        down_master,
        down_copy,
        gate_grads,
    ) = rest
    near = place_ref[1] == 0
    quick = lambda value: pl.reciprocal(value, approx=True)
    half = down_weight.shape[1] // 2
    groups = [lax.rem(place_ref[2] + k, REPLICA_GROUPS) for k in range(REPLICA_GROUPS)]

    def update(grads, at, first, second, weight, moment, outs, rate, decay):
        first_new, second_new, delta_out, moment_new, master, copy = outs
        start = weight[at]
        total = None
        for group, grad in zip(groups, grads):
            here = (group,) + at
            one, two, step = adam_step(grad, first[here], second[here], quick)
            first_new[here] = one
            second_new[here] = two
            total = step if total is None else total + step
        delta = mean_step(total, start, rate, decay)
        new_moment, new_weight = outer_step(start, delta, moment[at])
        delta_out[at] = delta
        moment_new[at] = new_moment
        master[at] = new_weight
        copy[at] = new_weight.astype(low_type)

    every = slice(None)
    for chunk, (begin, end) in enumerate(CHUNKS):
        for tile in range(begin, end):
            for kind in range(3):
                place = (2 * (tile - begin) + kind) if kind < 2 else (2 * (end - begin) + tile - begin)
                lanes = slice(place * LANES, (place + 1) * LANES)
                mine = [own[chunk * REPLICA_GROUPS + k][:, lanes] for k in range(REPLICA_GROUPS)]
                theirs = [other[chunk * REPLICA_GROUPS + k][:, lanes] for k in range(REPLICA_GROUPS)]
                for side in range(2):
                    grads = [
                        (jnp.where(near, a, b) if side == 0 else jnp.where(near, b, a)).astype(f32)
                        for a, b in zip(mine, theirs)
                    ]
                    at = slice(side * half + tile * LANES, side * half + (tile + 1) * LANES)
                    if kind < 2:
                        for k, grad in enumerate(grads):
                            gate_grads[k, :, kind, at] = grad
                    else:
                        update(
                            grads,
                            (every, at),
                            down_first,
                            down_second,
                            down_weight,
                            down_moment,
                            (down_first_new, down_second_new, down_delta, down_moment_new, down_master, down_copy),
                            inner_rates[4],
                            inner_decays[4],
                        )

    def some_rows(step, _):
        at = (pl.ds(step * PAIR_ROWS, PAIR_ROWS),)
        update(
            [gate_grads[(k,) + at] for k in range(REPLICA_GROUPS)],
            at,
            gate_first,
            gate_second,
            gate_weight,
            gate_moment,
            (gate_first_new, gate_second_new, gate_delta, gate_moment_new, gate_master, gate_copy),
            inner_rates[3],
            inner_decays[3],
        )
        return 0

    lax.fori_loop(0, down_weight.shape[0] // PAIR_ROWS, some_rows, 0)


def feed_update(place, own, other, gating, down):
    rows, _, hidden = gating[2].shape
    size = 32 if rows % 32 == 0 else 16
    steps = rows // size
    own_list = [value for chunk in own for value in chunk]
    other_list = [value for chunk in other for value in chunk]
    plane = pl.BlockSpec((size, hidden), lambda i, p: (i, 0))
    pair = pl.BlockSpec((size, 2, hidden), lambda i, p: (i, 0, 0))
    stack = pl.BlockSpec((REPLICA_GROUPS, size, hidden), lambda i, p: (0, i, 0))
    stack_pair = pl.BlockSpec((REPLICA_GROUPS, size, 2, hidden), lambda i, p: (0, i, 0, 0))
    shape = lambda value, dtype=f32: jax.ShapeDtypeStruct(value.shape, dtype)
    return pl.pallas_call(
        feed_update_kernel,
        grid_spec=pltpu.PrefetchScalarGridSpec(
            num_scalar_prefetch=1,
            grid=(steps,),
            in_specs=[
                pl.BlockSpec((size, value.shape[1]), lambda i, p: (i, 0)) for value in own_list + other_list
            ]
            + [stack_pair, stack_pair, pair, pair, stack, stack, plane, plane],
            out_specs=[stack_pair, stack_pair, pair, pair, pair, pair, stack, stack, plane, plane, plane, plane],
            scratch_shapes=[pltpu.VMEM((REPLICA_GROUPS, size, 2, hidden), f32)],
        ),
        out_shape=[
            shape(gating[0]),
            shape(gating[1]),
            shape(gating[2]),
            shape(gating[2]),
            shape(gating[2]),
            shape(gating[2], low_type),
            shape(down[0]),
            shape(down[1]),
            shape(down[2]),
            shape(down[2]),
            shape(down[2]),
            shape(down[2], low_type),
        ],
        compiler_params=params(),
        cost_estimate=cost(0, rows * hidden * 3 * 90),
        name="feed_update",
    )(place, *own_list, *other_list, *gating, *down)


def attention_update_kernel(place_ref, *refs):
    own, other, rest = refs[:REPLICA_GROUPS], refs[REPLICA_GROUPS : 2 * REPLICA_GROUPS], refs[2 * REPLICA_GROUPS :]
    left, right, states, outs = rest[0], rest[1], rest[2:10], rest[10:]
    near = place_ref[1] == 0
    flat = HEADS * HEAD_WIDTH
    for kind, (start, size) in enumerate(((0, PACK), (PACK, OUTPUT_PACK))):
        first, second, weight, moment = states[4 * kind : 4 * kind + 4]
        first_new, second_new, delta_out, moment_new, master, copy = outs[6 * kind : 6 * kind + 6]
        value = weight[...]
        total = None
        for slot in range(REPLICA_GROUPS):
            group = lax.rem(place_ref[2] + slot, REPLICA_GROUPS)
            mine, theirs = own[slot][:, start : start + size], other[slot][:, start : start + size]
            low, high = jnp.where(near, mine, theirs), jnp.where(near, theirs, mine)
            grad = dot(low, left[:size, :]) + dot(high, right[:size, :])
            one, two, step = adam_step(
                grad, first[group], second[group], lambda item: pl.reciprocal(item, approx=True)
            )
            first_new[group] = one
            second_new[group] = two
            total = step if total is None else total + step
        delta = mean_step(total, value, inner_rates[2 * kind], inner_decays[2 * kind])
        new_moment, new_weight = outer_step(value, delta, moment[...])
        delta_out[...] = delta
        moment_new[...] = new_moment
        master[...] = new_weight
        copy[...] = new_weight.astype(low_type)


def attention_update(place, own, other, query, output):
    rows, columns = query[2].shape
    flat = HEADS * HEAD_WIDTH
    size = math.gcd(rows, 160)
    table = np.zeros((2, PACK, columns), np.float32)
    for place_of in range(flat):
        table[0, place_of, place_of] = 1.0
        table[1, place_of, flat + place_of] = 1.0
    plane = pl.BlockSpec((size, columns), lambda i, p: (i, 0))
    stack = pl.BlockSpec((REPLICA_GROUPS, size, columns), lambda i, p: (0, i, 0))
    shape = lambda value, dtype=f32: jax.ShapeDtypeStruct(value.shape, dtype)
    shapes = []
    for state in (query, output):
        shapes += [shape(state[0]), shape(state[1])] + [shape(state[2])] * 3 + [shape(state[2], low_type)]
    return pl.pallas_call(
        attention_update_kernel,
        grid_spec=pltpu.PrefetchScalarGridSpec(
            num_scalar_prefetch=1,
            grid=(rows // size,),
            in_specs=[
                pl.BlockSpec((size, value.shape[1]), lambda i, p: (i, 0)) for value in (*own, *other)
            ]
            + [resident((PACK, columns))] * 2
            + [stack, stack, plane, plane] * 2,
            out_specs=[stack, stack, plane, plane, plane, plane] * 2,
        ),
        out_shape=shapes,
        compiler_params=params(),
        cost_estimate=cost(0, rows * columns * 2 * 90),
        name="attention_update",
    )(place, *own, *other, jnp.asarray(table[0], low_type), jnp.asarray(table[1], low_type), *query, *output)


def optimize(weight, grad, first, second, moment, rate, decay):
    first_new, second_new, step = adam_step(grad, first, second, lambda value: 1.0 / value)
    delta = mean_step(jnp.sum(step, axis=0), weight, rate, decay)
    moment_new, weight_new = outer_step(weight, delta, moment)
    return (first_new, second_new, delta, moment_new, weight_new, weight_new.astype(low_type))


def doc_layout(lengths, token_length):
    ends = jnp.cumsum(lengths)
    starts = ends - lengths
    places = jnp.arange(token_length, dtype=jnp.int32)
    segment = jnp.sum((places[:, None] >= ends[None, :]).astype(jnp.int32), axis=1)
    member = (segment[:, None] == jnp.arange(lengths.shape[0], dtype=jnp.int32)[None, :]).astype(
        jnp.int32
    )
    offset = jnp.sum(member * starts[None, :], axis=1)
    return offset, places - offset


def rope_tables(position):
    half = HEAD_WIDTH // 2
    frequency = rope_base ** (-2.0 * jnp.arange(half, dtype=f32) / HEAD_WIDTH)
    angle = position.astype(f32)[:, None] * frequency[None, :]
    cosine, sine = jnp.cos(angle), jnp.sin(angle)
    gap = jnp.zeros((angle.shape[0], HALF - half), f32)
    return (
        jnp.concatenate([cosine, gap, cosine, gap], axis=1),
        jnp.concatenate([-sine, gap, sine, gap], axis=1),
    )


def norm_inverse(value):
    return lax.rsqrt(jnp.mean(value * value, axis=-1, keepdims=True) + epsilon)


def norm_backward(value, inverse, gain, grad_normed):
    scaled = gain * grad_normed
    return inverse * scaled - value * inverse**3 * jnp.mean(scaled * value, axis=-1, keepdims=True)


def per_device(
    tokens,
    cotangent,
    doc_lengths,
    query_weight,
    keyvalue_weight_full,
    output_weight,
    gating_weight,
    down_weight,
    norm_gains,
    first_query,
    keyvalue_first_moment,
    first_output,
    first_gating,
    first_down,
    first_gains,
    second_query,
    keyvalue_second_moment,
    second_output,
    second_gating,
    second_down,
    second_gains,
    moment_query,
    keyvalue_outer_momentum,
    moment_output,
    moment_gating,
    moment_down,
    moment_gains,
):
    ring = lax.axis_size("ring")
    spot = lax.axis_index("ring")
    side = lax.axis_index("pair")
    near = side == 0
    rows = query_weight.shape[0]
    width = tokens.shape[1]
    local_rows = tokens.shape[0]
    sequence = local_rows * lax.axis_size("tensor")
    plane = ("pair", "tensor")
    per_group = ring // REPLICA_GROUPS
    direct = per_group == 1 and (2 * rows) % LANES == 0
    zero = jnp.zeros_like(spot)
    mine = side * lax.axis_size("tensor") + lax.axis_index("tensor")
    place = jnp.stack([spot if direct else zero, side, spot if direct else zero, mine])
    blocks = ring if direct else 1
    hops = [1, 3, 2]

    def swap(value):
        return lax.ppermute(value, "pair", [(0, 1), (1, 0)])

    def across(value, bit):
        count = lax.axis_size("tensor")
        return lax.ppermute(value, "tensor", [(i, i ^ bit) for i in range(count)])

    def add(left, right):
        return (left.astype(f32) + right.astype(f32)).astype(low_type)

    def core_stage(kept, sent):
        shape = (2, 2, local_rows, width)
        kept, other = kept.reshape(shape), across(sent, 1).reshape(shape)
        cut = local_rows // 2
        spans = [
            (slice(None), 0, slice(None, cut)),
            (slice(None), 1, slice(None, cut)),
            (0, slice(None), slice(cut, None)),
            (1, slice(None), slice(cut, None)),
        ]
        return [add(kept[span], other[span]) for span in spans]

    def chip_send(parts):
        return across(parts[1], 2), swap(parts[3])

    def chip_stage(parts, *earlier, came=None):
        by_x, by_y = after(came or chip_send(parts), *earlier)
        return add(parts[0], by_x), add(parts[2], by_y)

    def last_send(parts):
        return swap(parts[0][1]), across(parts[1][1], 2)

    def last_stage(parts, *earlier, came=None):
        one, two = parts
        by_y, by_x = after(came or last_send(parts), *earlier)
        return jnp.concatenate(
            [one[0].astype(f32) + by_y.astype(f32), two[0].astype(f32) + by_x.astype(f32)], axis=0
        )

    def hop(value, step):
        return lax.ppermute(value, "ring", [(i, (i + step) % ring) for i in range(ring)])

    def halves(kept, sent, other=None):
        other = swap(sent) if other is None else other
        return jnp.concatenate([jnp.where(near, kept, other), jnp.where(near, other, kept)], axis=0)

    def gather(shard):
        return lax.all_gather(shard, "ring", axis=0, tiled=True)

    def gather_hops(shard):
        if not direct:
            return [gather(shard)]
        found = [shard] + [None] * (ring - 1)
        for step in hops:
            found[step] = hop(shard, step)
        return found

    def relay(found):
        if not direct:
            return [gather(found[0])] if found[0].shape[0] == 2 * rows else found
        return found + [hop(found[-1], 1)]

    def gather_first(value):
        cut = local_rows // 2
        return value, across(value[:cut], 2), swap(value[cut:])

    def gather_second(parts):
        value, by_x, by_y = parts
        cut = local_rows // 2
        one = jnp.stack([value[:cut], by_x])
        two = jnp.stack([value[cut:], by_y])
        return one, two, swap(one), across(two, 2)

    def gather_last(parts):
        one, two, one_y, two_x = parts
        ones = [one[0], one[1], one_y[0], one_y[1]]
        twos = [two[0], two_x[0], two[1], two_x[1]]
        mine = jnp.concatenate([half for pair in zip(ones, twos) for half in pair], axis=0)
        other = across(mine, 1)
        found = []
        for start in range(0, mine.shape[0], local_rows):
            found += [mine[start : start + local_rows], other[start : start + local_rows]]
        return jnp.concatenate(found, axis=0)

    def sides(grads):
        if direct:
            return grads[1::2], grads[0::2]
        whole = grads[0].reshape(ring, 2, rows, -1)
        return (lax.dynamic_index_in_dim(whole, 1 - side, 1, False), lax.dynamic_index_in_dim(whole, side, 1, False))

    def deliver(grads):
        if not direct:
            whole = lax.all_to_all(grads, "ring", split_axis=0, concat_axis=0, tiled=True).astype(f32)
            whole = whole.reshape((REPLICA_GROUPS, per_group) + whole.shape[1:])
            whole = jnp.sum(whole, axis=1).astype(low_type)
            return [whole[k] for k in range(REPLICA_GROUPS)]
        found = [grads[0]] + [None] * (ring - 1)
        for step in hops:
            found[step] = hop(grads[step], -step)
        return found

    def tensor_sum(value):
        count = lax.axis_size("tensor")
        bit = 1
        while bit < count:
            value = value + across(value, bit)
            bit *= 2
        return value

    tokens_all = lax.all_gather(tokens, plane, axis=0, tiled=True)

    flat = HEADS * HEAD_WIDTH
    query_halves = [query_weight[:, :flat], query_weight[:, flat:]]
    pair_halves = [
        keyvalue_weight_full[:, :, :HEAD_WIDTH].reshape(rows, 2 * HEAD_WIDTH),
        keyvalue_weight_full[:, :, HEAD_WIDTH:].reshape(rows, 2 * HEAD_WIDTH),
    ]
    gain_columns = jnp.concatenate(
        [norm_gains.T, jnp.zeros((rows, PACK - flat - 2 * HEAD_WIDTH - 2), f32)], axis=1
    )
    packed = [
        jnp.concatenate([q, p, gain_columns], axis=1).astype(low_type)
        for q, p in zip(query_halves, pair_halves)
    ]
    output_low = output_weight.astype(low_type)
    output_parts = [output_low[:, :flat], output_low[:, flat:]]
    pick = lambda parts: (jnp.where(near, parts[0], parts[1]), jnp.where(near, parts[1], parts[0]))
    attention_shard = halves(*pick(packed))
    attention_blocks = gather_hops(attention_shard)
    output_kept, output_sent = pick(output_parts)
    output_shard = halves(output_kept, after(output_sent, attention_shard))
    output_blocks = gather_hops(after(output_shard, attention_blocks[1:2]))

    feed_parts = pack_feed(after(place, attention_shard), gating_weight, down_weight)
    tokens_all = after(tokens_all, feed_parts)
    kept, sent = feed_parts[: len(CHUNKS)], feed_parts[len(CHUNKS) :]
    feed_shards, came = [], []
    last = attention_shard
    for a, b in zip(kept, sent):
        came.append(swap(after(b, last)))
        last = halves(a, b, came[-1])
        feed_shards.append(last)
    one = relay([after(feed_shards[0], attention_blocks)])
    cotangent_parts = gather_first(after(cotangent, tokens_all))

    other_lengths = swap(doc_lengths)
    lengths = [jnp.where(near, doc_lengths[0], other_lengths[0]), jnp.where(near, other_lengths[0], doc_lengths[0])]
    layouts = [doc_layout(value, sequence) for value in lengths]
    starts = jnp.broadcast_to(
        jnp.concatenate([value[0] for value in layouts])[None, :], (8, 2 * sequence)
    ).astype(jnp.int32)
    cosine, sine = rope_tables(jnp.concatenate([value[1] for value in layouts]))

    cosine = after(cosine, came[0])
    normed_one, heads, gains, wide = project(place, tokens_all, attention_blocks, cosine, sine)
    gain_one, gain_two = gains[0], gains[1]
    heads = after(heads, cotangent_parts)
    mixed, totals, *partial = attend(place, heads, starts, output_blocks, sequence)
    cotangent_parts = gather_second(cotangent_parts)
    partial = after(partial, cotangent_parts, one)
    one = relay(one)
    parts = after(core_stage(*partial), one)
    one = relay(one)
    cotangent_all = gather_last(after(cotangent_parts, parts))
    parts = after(chip_stage(parts, one), cotangent_all)
    two = relay([after(feed_shards[1], one)])
    attention = last_stage(parts, two)

    hidden = tokens.astype(f32)
    inverse_one = norm_inverse(hidden)
    hidden_one = hidden + attention
    inverse_two = norm_inverse(hidden_one)
    normed_two = (hidden_one * inverse_two * gain_two).astype(low_type)
    two = relay(two)
    normed_parts = after(gather_second(gather_first(normed_two)), two)
    two = relay(two)
    normed_two_all = gather_last(normed_parts)
    hid, grad_pair = feed(place, normed_two_all, cotangent_all, one)
    theirs, mine = sides(weight_grad(place, blocks, [(normed_two_all, grad_pair), (cotangent_all, hid)]))
    theirs_one = deliver(theirs)
    others_one = [swap(theirs_one[0])]
    normed_late = after(normed_two_all, theirs[0])
    hid_two, grad_pair_two = feed(place, normed_late, cotangent_all, two)
    partial = spread(place, after([grad_pair, grad_pair_two], others_one), [one, two], 0)
    partial = after(partial, theirs_one)
    others_one += [swap(after(value, partial)) for value in theirs_one[1:3]]
    parts = core_stage(*partial)
    mine_one = deliver(after(mine, partial))
    theirs, mine_later = sides(
        weight_grad(place, blocks, [(normed_two_all, after(grad_pair_two, *parts)), (cotangent_all, hid_two)])
    )
    parts = after(chip_stage(parts, theirs[0]), others_one, mine_one[1:2])
    theirs_two = deliver(theirs)
    feed_partial = spread(place, after([hid, hid_two], *parts), [one, two], 2)
    grad_normed_two = last_stage(parts, *feed_partial, theirs_two[1:2], theirs_two[3:])

    grad_hidden_one = cotangent.astype(f32) + norm_backward(
        hidden_one, inverse_two, gain_two, grad_normed_two
    )
    grad_gain_two = jnp.sum(grad_normed_two * hidden_one * inverse_two, axis=0)
    grad_hidden_all = lax.all_gather(grad_hidden_one.astype(low_type), plane, axis=0, tiled=True)
    feed_parts = chip_stage(core_stage(*after(feed_partial, grad_hidden_one)))
    feed_came = last_send(feed_parts)
    grad_hidden_all = after(grad_hidden_all, theirs_two, mine_one[3:], feed_came)
    mine_two = deliver(after(mine_later, grad_hidden_all))
    others_one.append(swap(after(theirs_one[3], grad_hidden_all)))
    others_two = [swap(after(value, grad_hidden_all)) for value in theirs_two[:2]]

    grad_query, grad_pair = attend_grad(
        place, grad_hidden_all, heads, totals, starts, cosine, sine, output_blocks, sequence
    )
    *partial, gain_sums = project_grad(place, grad_query, grad_pair, tokens_all, wide)
    grad_gains = jnp.stack([jnp.sum(gain_sums, axis=0), grad_gain_two], axis=0)
    grad_gains = jnp.concatenate([grad_gains, jnp.zeros((6, width), f32)], axis=0).astype(low_type)
    partial = after(partial, mine_one, others_one, others_two, mine_two[1:2])
    parts = core_stage(*partial)
    others_two += [swap(after(value, partial)) for value in theirs_two[2:]]
    theirs, mine = sides(
        weight_grad(
            place,
            blocks,
            [
                (normed_one, after(grad_query, *parts)),
                (normed_one, grad_pair),
                (grad_gains, jnp.asarray(gains_selector(), low_type)),
                (grad_hidden_all, mixed),
            ],
            gradient_selectors(),
        )
    )
    parts = after(chip_stage(parts, theirs[0]), mine_two, others_two[:3])
    theirs_last = deliver(theirs)
    came = last_send(parts)
    grad_normed_one = last_stage(parts, came=came)
    mine_one, others_one, mine_two, others_two, theirs_last = after(
        (mine_one, others_one, mine_two, others_two, theirs_last), came
    )
    mine_last = deliver(after(mine, theirs_last))
    others_last = [swap(theirs_last[0]), swap(jnp.stack(theirs_last[1:]))]
    block_output = (hidden_one + last_stage(feed_parts, came=feed_came)).astype(low_type)

    token_grad = (
        grad_hidden_one + norm_backward(hidden, inverse_one, gain_one, grad_normed_one)
    ).astype(low_type)

    updated = feed_update(
        place,
        [mine_one, mine_two],
        [others_one, others_two],
        (first_gating, second_gating, gating_weight, moment_gating),
        (first_down, second_down, down_weight, moment_down),
    )
    mine_last = after(mine_last, updated[0])
    others_last = [others_last[0]] + [others_last[1][k] for k in range(REPLICA_GROUPS - 1)]
    attention_updated = attention_update(
        place,
        mine_last,
        others_last,
        (first_query, second_query, query_weight, moment_query),
        (first_output, second_output, output_weight, moment_output),
    )
    qry, out = attention_updated[:6], attention_updated[6:]
    columns = slice(flat, flat + 2 * HEAD_WIDTH + 2)
    both = [jnp.stack([value[:, columns] for value in part]) for part in (mine_last, others_last)]
    both = [jnp.where(near, both[0], both[1]), jnp.where(near, both[1], both[0])]
    if direct:
        both = [jnp.roll(value, spot, axis=0) for value in both]
    both = [value.astype(f32) for value in both]
    pair_total = jnp.concatenate(
        [value[..., : 2 * HEAD_WIDTH].reshape(REPLICA_GROUPS, rows, 2, HEAD_WIDTH) for value in both], axis=-1
    )
    gains_total = jnp.swapaxes(both[0][..., 2 * HEAD_WIDTH :] + both[1][..., 2 * HEAD_WIDTH :], 1, 2)
    gains_total = tensor_sum(gains_total)
    kvl = optimize(
        keyvalue_weight_full,
        pair_total,
        keyvalue_first_moment,
        keyvalue_second_moment,
        keyvalue_outer_momentum,
        inner_rates[1],
        inner_decays[1],
    )
    gns = optimize(
        norm_gains, gains_total, first_gains, second_gains, moment_gains, inner_rates[5], inner_decays[5]
    )
    gat = updated[:6]
    dwn = updated[6:]
    return (block_output, token_grad, *qry, *kvl, *out, *gat, *dwn, *gns)


def solution(mesh):
    shape = (mesh.shape["dp"] // 2, 2, mesh.shape["tensor"])
    mesh = Mesh(mesh.devices.reshape(shape), ("ring", "pair", "tensor"))
    dp = ("ring", "pair")
    matrix = P(dp, "tensor")
    pair = P(dp, None, "tensor")
    stack = P(None, dp, "tensor")
    stack_pair = P(None, dp, None, "tensor")
    tokens = P(("ring", "pair", "tensor"), None)
    gains = P(None, dp)
    stack_gains = P(None, None, dp)
    weights = (matrix, pair, matrix, pair, matrix, gains)
    states = (stack, stack_pair, stack, stack_pair, stack, stack_gains)
    outs = []
    for weight, state in zip(weights, states):
        outs += [state, state, weight, weight, weight, weight]
    return jax.shard_map(
        per_device,
        mesh=mesh,
        in_specs=(tokens, tokens, P(dp, None), *weights, *states, *states, *weights),
        out_specs=(tokens, tokens, *outs),
        check_vma=False,
    )
```

```python
import functools
import math

import jax
import jax.numpy as jnp
import numpy as np
from jax import lax
from jax.experimental import pallas as pl
from jax.experimental.pallas import tpu as pltpu
from jax.sharding import Mesh, PartitionSpec as P

HEAD_WIDTH = 80
REPLICA_GROUPS = 4
STEP = 8
LANES = 128
HEADS = 4
TILE = 256
PACK = 512
WIDE = 768
HALF = 64
VMEM_BYTES = 58 * 2**20

epsilon = 1e-05
rope_base = 1000000.0
beta_one = 0.9
beta_two = 0.95
adam_epsilon = 1e-08
outer_mu = 0.9
outer_rate = 0.7
inner_rates = (0.05, 0.05, 0.2, 0.05, 0.05, 0.5)
inner_decays = (0.1, 0.1, 0.1, 0.1, 0.1, 0.0)
correct_one = 1.0 - beta_one**STEP
correct_two = 1.0 - beta_two**STEP

low_type = jnp.bfloat16
f32 = jnp.float32

NN = (((1,), (0,)), ((), ()))
NT = (((1,), (1,)), ((), ()))
TN = (((0,), (0,)), ((), ()))

CHUNKS = ((0, 3), (3, 7))


def after(value, *earlier):
    return lax.optimization_barrier((value, earlier))[0]


def dot(left, right, dims=NN):
    return lax.dot_general(left, right, dims, preferred_element_type=f32)


def params(**kwargs):
    return pltpu.CompilerParams(vmem_limit_bytes=VMEM_BYTES, **kwargs)


COST_SHARE = 1.0


def cost(flops, size):
    return pl.CostEstimate(
        flops=int(COST_SHARE * flops), bytes_accessed=int(COST_SHARE * size), transcendentals=0
    )


SHORT = pl.CostEstimate(flops=1, bytes_accessed=1, transcendentals=0)


def resident(shape):
    zeros = (0,) * len(shape)
    return pl.BlockSpec(shape, lambda *_: zeros, pipeline_mode=pl.Buffered(1))


def projection_selector():
    table = np.zeros((PACK, WIDE), np.float32)
    for head in range(HEADS + 1):
        for place in range(HEAD_WIDTH):
            half, rest = divmod(place, HEAD_WIDTH // 2)
            table[head * HEAD_WIDTH + place, head * LANES + half * HALF + rest] = 1.0
    for place in range(HEAD_WIDTH):
        table[(HEADS + 1) * HEAD_WIDTH + place, (HEADS + 1) * LANES + place] = 1.0
    return table


def output_selector():
    table = np.zeros((HEADS * HEAD_WIDTH, HEADS * LANES), np.float32)
    for head in range(HEADS):
        for place in range(HEAD_WIDTH):
            table[head * HEAD_WIDTH + place, head * LANES + place] = 1.0
    return table


OUTPUT_PACK = 384


def gradient_selectors():
    project, output = projection_selector(), output_selector()
    padded = np.zeros((OUTPUT_PACK, HEADS * LANES), np.float32)
    padded[: output.shape[0]] = output
    return ((0, project), (0, None), (1, padded))


def gains_selector():
    table = np.zeros((8, PACK), np.float32)
    table[0, (HEADS + 2) * HEAD_WIDTH] = 1.0
    table[1, (HEADS + 2) * HEAD_WIDTH + 1] = 1.0
    return table


def seen_from(place_ref, piece):
    return lax.bitwise_xor(piece, place_ref[3])


def piece_specs(width, piece):
    return [pl.BlockSpec((TILE, width), lambda *at: (lax.shift_right_logical(piece(*at), 1), 0))] * 2


def piece_shapes(total, width):
    return [jax.ShapeDtypeStruct((total // 2, width), low_type)] * 2


def write_piece(piece, kept, sent, value):
    odd = lax.bitwise_and(piece, 1)

    @pl.when(odd == 0)
    def _():
        kept[...] = value

    @pl.when(odd == 1)
    def _():
        sent[...] = value


def first_row(place, step, blocks, rows):
    return pl.multiple_of(lax.rem(place - step + blocks, blocks) * rows, LANES if blocks > 1 else rows)


def assemble(place, blocks, target):
    rows = blocks[0].shape[0]
    for step, block in enumerate(blocks):
        target[pl.ds(first_row(place, step, len(blocks), rows), rows), :] = block[...]


def projection_kernel(count, place_ref, tokens, *refs):
    blocks, (select, pick, cosine, sine, normed, heads, gains, wide) = refs[:count], refs[count:]

    @pl.when(pl.program_id(0) == 0)
    def _():
        rows = blocks[0].shape[0]
        for step, block in enumerate(blocks):
            start = first_row(place_ref[0], step, count, rows)
            value = block[...]
            wide[pl.ds(start, rows), :] = dot(value, select[...]).astype(low_type)
            gains[:, pl.ds(start, rows)] = dot(pick[...], value, NT)

    value = tokens[...].astype(f32)
    inverse = lax.rsqrt(jnp.mean(value * value, axis=-1, keepdims=True) + epsilon)
    low = (value * inverse * gains[0:1, :]).astype(low_type)
    normed[...] = low
    result = dot(low, wide[...])
    cos_tile = cosine[...]
    sin_tile = sine[...]
    for head in range(HEADS + 1):
        part = result[:, head * LANES : (head + 1) * LANES]
        turned = part * cos_tile + pltpu.roll(part, HALF, 1) * sin_tile
        heads[:, head * LANES : (head + 1) * LANES] = turned.astype(low_type)
    heads[:, (HEADS + 1) * LANES :] = result[:, (HEADS + 1) * LANES :].astype(low_type)


def project(place, tokens, blocks, cosine, sine):
    total, width = tokens.shape
    tile = lambda columns: pl.BlockSpec((TILE, columns), lambda i, p: (i, 0))
    return pl.pallas_call(
        functools.partial(projection_kernel, len(blocks)),
        grid_spec=pltpu.PrefetchScalarGridSpec(
            num_scalar_prefetch=1,
            grid=(total // TILE,),
            in_specs=[tile(width)]
            + [resident(block.shape) for block in blocks]
            + [
                resident((PACK, WIDE)),
                resident((8, PACK)),
                tile(LANES),
                tile(LANES),
            ],
            out_specs=[
                tile(width),
                tile(WIDE),
                pl.BlockSpec((8, width), lambda *_: (0, 0)),
                pl.BlockSpec((width, WIDE), lambda *_: (0, 0)),
            ],
        ),
        out_shape=[
            jax.ShapeDtypeStruct((total, width), low_type),
            jax.ShapeDtypeStruct((total, WIDE), low_type),
            jax.ShapeDtypeStruct((8, width), f32),
            jax.ShapeDtypeStruct((width, WIDE), low_type),
        ],
        compiler_params=params(),
        cost_estimate=cost(2 * total * width * WIDE, 4 * total * width + 3 * width * WIDE * 2),
        name="projection",
    )(
        place,
        tokens,
        *blocks,
        jnp.asarray(projection_selector(), low_type),
        jnp.asarray(gains_selector(), low_type),
        cosine,
        sine,
    )


SCORE_SCALE = math.log2(math.e) / math.sqrt(HEAD_WIDTH)
GRAD_SCALE = 1.0 / math.sqrt(HEAD_WIDTH)


def allowed_pairs(block, width, starts):
    key_index = lax.broadcasted_iota(jnp.int32, (width, TILE), 0)
    row_index = block * TILE + lax.broadcasted_iota(jnp.int32, (1, TILE), 1)
    return (key_index >= starts) & (key_index <= row_index)


def widen_output(place_ref, blocks, select, wide):
    @pl.when((pl.program_id(0) == 0) & (pl.program_id(1) == 0))
    def _():
        rows = blocks[0].shape[0]
        for step, block in enumerate(blocks):
            start = first_row(place_ref[0], step, len(blocks), rows)
            wide[pl.ds(start, rows), :] = dot(block[...], select[...]).astype(low_type)


def attention_kernel(count, blocks_per, place_ref, query, key, value, starts, *refs):
    blocks, (select, mixed, totals, kept, sent, wide) = refs[:count], refs[count:]
    widen_output(place_ref, blocks, select, wide)

    for block in range(blocks_per):

        @pl.when(pl.program_id(1) == block)
        def _(block=block):
            width = (block + 1) * TILE
            allowed = allowed_pairs(block, width, starts[0:1, :])
            keys = key[0:width, :]
            values = value[0:width, :]
            for head in range(HEADS):
                lanes = slice(head * LANES, (head + 1) * LANES)
                scores = dot(keys, query[:, lanes], NT) * SCORE_SCALE
                scores = jnp.where(allowed, scores, -1e30)
                top = jnp.max(scores, axis=0, keepdims=True)
                expo = jnp.exp2(scores - top)
                total = jnp.sum(expo, axis=0, keepdims=True)
                out = dot(values, expo.astype(low_type), TN) * (1.0 / total)
                mixed[:, lanes] = out.T.astype(low_type)
                totals[head : head + 1, :] = top + jnp.log2(total)

    piece = pl.program_id(0) * blocks_per + pl.program_id(1)
    value = dot(mixed[...], wide[...], NT).astype(low_type)
    write_piece(seen_from(place_ref, piece), kept, sent, value)


def attend(place, heads, starts, blocks, sequence):
    total = heads.shape[0]
    width = blocks[0].shape[0] * len(blocks)
    per = sequence // TILE
    tile = lambda size, column: pl.BlockSpec((TILE, size), lambda s, i, *_: (s * per + i, column))
    full = lambda column: pl.BlockSpec((sequence, LANES), lambda s, i, *_: (s, column))
    line = pl.BlockSpec((8, TILE), lambda s, i, *_: (0, s * per + i))
    return pl.pallas_call(
        functools.partial(attention_kernel, len(blocks), per),
        grid_spec=pltpu.PrefetchScalarGridSpec(
            num_scalar_prefetch=1,
            grid=(total // sequence, per),
            in_specs=[
                tile(HEADS * LANES, 0),
                full(HEADS),
                full(HEADS + 1),
                line,
            ]
            + [resident(block.shape) for block in blocks]
            + [resident((HEADS * HEAD_WIDTH, HEADS * LANES))],
            out_specs=[tile(HEADS * LANES, 0), line]
            + piece_specs(width, lambda s, i, p: seen_from(p, s * per + i)),
            scratch_shapes=[pltpu.VMEM((width, HEADS * LANES), low_type)],
        ),
        out_shape=[
            jax.ShapeDtypeStruct((total, HEADS * LANES), low_type),
            jax.ShapeDtypeStruct((8, total), f32),
        ]
        + piece_shapes(total, width),
        compiler_params=params(),
        cost_estimate=cost(20e9, 4 * total * width),
        name="attention",
    )(place, heads, heads, heads, starts, *blocks, jnp.asarray(output_selector(), low_type))


def attention_grad_kernel(
    count,
    blocks_per,
    place_ref,
    grad_hidden,
    query,
    key,
    value,
    totals,
    starts,
    cosine,
    sine,
    cos_all,
    sin_all,
    *refs,
):
    blocks, (select, grad_query, grad_pair, wide, key_sum, value_sum) = refs[:count], refs[count:]
    widen_output(place_ref, blocks, select, wide)

    @pl.when(pl.program_id(1) == 0)
    def _():
        key_sum[...] = jnp.zeros_like(key_sum)
        value_sum[...] = jnp.zeros_like(value_sum)

    grad_mixed = dot(grad_hidden[...], wide[...]).astype(low_type)
    cos_tile = cosine[...]
    sin_tile = sine[...]
    for block in range(blocks_per):

        @pl.when(pl.program_id(1) == block)
        def _(block=block):
            width = (block + 1) * TILE
            allowed = allowed_pairs(block, width, starts[0:1, :])
            keys = key[0:width, :]
            values = value[0:width, :]
            key_part = jnp.zeros((width, LANES), f32)
            value_part = jnp.zeros((width, LANES), f32)
            for head in range(HEADS):
                lanes = slice(head * LANES, (head + 1) * LANES)
                queries = query[:, lanes]
                grads = grad_mixed[:, lanes]
                scores = dot(keys, queries, NT) * SCORE_SCALE
                scores = jnp.where(allowed, scores, -1e30)
                prob = jnp.exp2(scores - totals[head : head + 1, :])
                grad_prob = dot(values, grads, NT)
                inner = jnp.sum(prob * grad_prob, axis=0, keepdims=True)
                grad_scores = (prob * (grad_prob - inner)).astype(low_type)
                key_part = key_part + dot(grad_scores, queries)
                value_part = value_part + dot(prob.astype(low_type), grads)
                turned = dot(keys, grad_scores, TN).T * GRAD_SCALE
                turned = turned * cos_tile - pltpu.roll(turned, HALF, 1) * sin_tile
                grad_query[:, lanes] = turned.astype(low_type)
            key_sum[0:width, :] += key_part
            value_sum[0:width, :] += value_part

    @pl.when(pl.program_id(1) == blocks_per - 1)
    def _():
        grad_key = key_sum[...] * GRAD_SCALE
        grad_key = grad_key * cos_all[...] - pltpu.roll(grad_key, HALF, 1) * sin_all[...]
        grad_pair[:, :LANES] = grad_key.astype(low_type)
        grad_pair[:, LANES:] = value_sum[...].astype(low_type)


def attend_grad(place, grad_hidden, heads, totals, starts, cosine, sine, blocks, sequence):
    total, width = grad_hidden.shape
    per = sequence // TILE
    tile = lambda size, column: pl.BlockSpec((TILE, size), lambda s, i, p: (s * per + i, column))
    full = lambda size, column: pl.BlockSpec((sequence, size), lambda s, i, p: (s, column))
    line = pl.BlockSpec((8, TILE), lambda s, i, p: (0, s * per + i))
    return pl.pallas_call(
        functools.partial(attention_grad_kernel, len(blocks), per),
        grid_spec=pltpu.PrefetchScalarGridSpec(
            num_scalar_prefetch=1,
            grid=(total // sequence, per),
            in_specs=[
                tile(width, 0),
                tile(HEADS * LANES, 0),
                full(LANES, HEADS),
                full(LANES, HEADS + 1),
                line,
                line,
                tile(LANES, 0),
                tile(LANES, 0),
                full(LANES, 0),
                full(LANES, 0),
            ]
            + [resident(block.shape) for block in blocks]
            + [resident((HEADS * HEAD_WIDTH, HEADS * LANES))],
            out_specs=[tile(HEADS * LANES, 0), full(2 * LANES, 0)],
            scratch_shapes=[
                pltpu.VMEM((width, HEADS * LANES), low_type),
                pltpu.VMEM((sequence, LANES), f32),
                pltpu.VMEM((sequence, LANES), f32),
            ],
        ),
        out_shape=[
            jax.ShapeDtypeStruct((total, HEADS * LANES), low_type),
            jax.ShapeDtypeStruct((total, 2 * LANES), low_type),
        ],
        compiler_params=params(),
        cost_estimate=cost(30e9, 4 * total * width),
        name="attention_grad",
    )(
        place,
        grad_hidden,
        heads,
        heads,
        heads,
        totals,
        starts,
        cosine,
        sine,
        cosine,
        sine,
        *blocks,
        jnp.asarray(output_selector(), low_type),
    )


def projection_grad_kernel(place_ref, grad_heads, tokens, wide, kept, sent, gain_sums):
    grad = dot(grad_heads[...], wide[...], NT)
    write_piece(seen_from(place_ref, pl.program_id(0)), kept, sent, grad.astype(low_type))
    value = tokens[...].astype(f32)
    inverse = lax.rsqrt(jnp.mean(value * value, axis=-1, keepdims=True) + epsilon)
    product = grad * (value * inverse)
    sums = jnp.sum(product.reshape(TILE // 8, 8, product.shape[1]), axis=0)

    @pl.when(pl.program_id(0) == 0)
    def _():
        gain_sums[...] = sums

    @pl.when(pl.program_id(0) != 0)
    def _():
        gain_sums[...] += sums


def project_grad(place, grad_heads, tokens, wide):
    total, width = tokens.shape
    tile = lambda columns: pl.BlockSpec((TILE, columns), lambda i, *_: (i, 0))
    return pl.pallas_call(
        projection_grad_kernel,
        grid_spec=pltpu.PrefetchScalarGridSpec(
            num_scalar_prefetch=1,
            grid=(total // TILE,),
            in_specs=[
                tile(WIDE),
                tile(width),
                resident((width, WIDE)),
            ],
            out_specs=piece_specs(width, lambda i, p: seen_from(p, i)) + [pl.BlockSpec((8, width), lambda i, *_: (0, 0))],
        ),
        out_shape=piece_shapes(total, width) + [jax.ShapeDtypeStruct((8, width), f32)],
        compiler_params=params(),
        cost_estimate=SHORT,
        name="projection_grad",
    )(place, grad_heads, tokens, wide)


def pack_kernel(place_ref, gating, down, *outs):
    kept, sent = outs[: len(CHUNKS)], outs[len(CHUNKS) :]

    def write(targets):
        for (first, last), target in zip(CHUNKS, targets):
            count = last - first
            for tile in range(first, last):
                lanes = slice(tile * LANES, (tile + 1) * LANES)
                place = (tile - first) * 2 * LANES
                target[:, place : place + LANES] = gating[:, 0, lanes].astype(low_type)
                target[:, place + LANES : place + 2 * LANES] = gating[:, 1, lanes].astype(low_type)
                place = (2 * count + tile - first) * LANES
                target[:, place : place + LANES] = down[:, lanes].astype(low_type)

    @pl.when(pl.program_id(0) == 0)
    def _():
        write(sent)

    @pl.when(pl.program_id(0) == 1)
    def _():
        write(kept)


def pack_feed(place, gating, down):
    rows, _, hidden = gating.shape
    half = hidden // 2
    side = lambda i, place_ref: jnp.where(i == 0, 1 - place_ref[1], place_ref[1])
    shapes = [(rows, 3 * LANES * (last - first)) for first, last in CHUNKS] * 2
    return pl.pallas_call(
        pack_kernel,
        grid_spec=pltpu.PrefetchScalarGridSpec(
            num_scalar_prefetch=1,
            grid=(2,),
            in_specs=[
                pl.BlockSpec((rows, 2, half), lambda i, p: (0, 0, side(i, p))),
                pl.BlockSpec((rows, half), lambda i, p: (0, side(i, p))),
            ],
            out_specs=[pl.BlockSpec(shape, lambda *_: (0, 0)) for shape in shapes],
        ),
        out_shape=[jax.ShapeDtypeStruct(shape, low_type) for shape in shapes],
        compiler_params=params(),
        cost_estimate=cost(0, 18 * rows * hidden),
        name="pack_feed",
    )(place, gating, down)


def feed_kernel(count, tiles, place_ref, normed, grad_out, *refs):
    blocks, (hidden, grad_pair, weights) = refs[:count], refs[count:]

    @pl.when(pl.program_id(0) == 0)
    def _():
        assemble(place_ref[0], blocks, weights)

    pair = dot(normed[...], weights[:, : 2 * tiles * LANES])
    grad_hidden = dot(grad_out[...], weights[:, 2 * tiles * LANES :])
    for tile in range(tiles):
        place = 2 * tile * LANES
        gate = pair[:, place : place + LANES]
        up = pair[:, place + LANES : place + 2 * LANES]
        grad = grad_hidden[:, tile * LANES : (tile + 1) * LANES]
        sigma = 1.0 / (1.0 + jnp.exp(-gate))
        silu = gate * sigma
        hidden[:, tile * LANES : (tile + 1) * LANES] = (silu * up).astype(low_type)
        grad_gate = grad * up * sigma * (1.0 + gate * (1.0 - sigma))
        grad_pair[:, place : place + LANES] = grad_gate.astype(low_type)
        grad_pair[:, place + LANES : place + 2 * LANES] = (grad * silu).astype(low_type)


def feed(place, normed, grad_out, blocks):
    total, width = normed.shape
    rows, columns = blocks[0].shape
    tiles = columns // (3 * LANES)
    tile = lambda size: pl.BlockSpec((TILE, size), lambda i, p: (i, 0))
    return pl.pallas_call(
        functools.partial(feed_kernel, len(blocks), tiles),
        grid_spec=pltpu.PrefetchScalarGridSpec(
            num_scalar_prefetch=1,
            grid=(total // TILE,),
            in_specs=[tile(width), tile(width)] + [resident(block.shape) for block in blocks],
            out_specs=[tile(tiles * LANES), tile(2 * tiles * LANES)],
            scratch_shapes=[pltpu.VMEM((width, columns), low_type)],
        ),
        out_shape=[
            jax.ShapeDtypeStruct((total, tiles * LANES), low_type),
            jax.ShapeDtypeStruct((total, 2 * tiles * LANES), low_type),
        ],
        compiler_params=params(),
        cost_estimate=cost(2 * total * width * columns, 4 * total * width + 2 * width * columns),
        name="feed",
    )(place, normed, grad_out, *blocks)


def spread_kernel(counts, place_ref, *refs):
    parts = len(counts)
    values, rest = refs[:parts], refs[parts:]
    chunks = []
    for count in counts:
        chunks.append(rest[:count])
        rest = rest[count:]
    kept, sent, wholes = rest[0], rest[1], rest[2:]

    @pl.when(pl.program_id(0) == 0)
    def _():
        for blocks, whole in zip(chunks, wholes):
            assemble(place_ref[0], blocks, whole)

    total = dot(values[0][...], wholes[0][...], NT)
    for value, whole in zip(values[1:], wholes[1:]):
        total = total + dot(value[...], whole[...], NT)
    write_piece(pl.program_id(0), kept, sent, total.astype(low_type))


def spread(place, values, chunks, column):
    total = values[0].shape[0]
    width = chunks[0][0].shape[0] * len(chunks[0])
    tile = lambda size: pl.BlockSpec((TILE, size), lambda i, p: (i, 0))
    return pl.pallas_call(
        functools.partial(spread_kernel, tuple(len(blocks) for blocks in chunks)),
        grid_spec=pltpu.PrefetchScalarGridSpec(
            num_scalar_prefetch=1,
            grid=(total // TILE,),
            in_specs=[tile(value.shape[1]) for value in values]
            + [
                pl.BlockSpec(
                    (block.shape[0], value.shape[1]), lambda *_: (0, column), pipeline_mode=pl.Buffered(1)
                )
                for value, blocks in zip(values, chunks)
                for block in blocks
            ],
            out_specs=piece_specs(width, lambda i, p: i),
            scratch_shapes=[pltpu.VMEM((width, value.shape[1]), low_type) for value in values],
        ),
        out_shape=piece_shapes(total, width),
        compiler_params=params(),
        cost_estimate=SHORT,
        name="spread",
    )(place, *values, *[block for blocks in chunks for block in blocks])


ROW_TILE = 640


def weight_grad_kernel(spans, selected, split, place_ref, *refs):
    parts = len(spans)
    lefts, rights, rest = refs[:parts], refs[parts : 2 * parts], refs[2 * parts :]
    outs = rest[sum(selected) :]
    selects = [rest[sum(selected[:place])] if chosen else None for place, chosen in enumerate(selected)]

    def write(targets, value, columns, again):
        size = targets[0].shape[0]
        for place, target in enumerate(targets):
            rows = value[place * size : (place + 1) * size]
            if again:
                rows = rows + target[:, columns].astype(f32)
            target[:, columns] = rows.astype(low_type)

    for block in range(len(outs) // split):
        targets = outs[block * split : (block + 1) * split]

        @pl.when(pl.program_id(0) == block)
        def _(targets=targets):
            for place, (left, right) in enumerate(zip(lefts, rights)):
                value = dot(left[...], right[...], TN).astype(low_type)
                if selects[place] is not None:
                    value = dot(value, selects[place][...], NT)
                columns = slice(*spans[place])
                again = place and spans[place] == spans[place - 1]
                if split == 1:
                    write(targets, value, columns, again)
                    continue

                @pl.when(place_ref[1] == 0)
                def _(value=value, columns=columns, again=again):
                    write(targets, value, columns, again)

                @pl.when(place_ref[1] != 0)
                def _(value=value, columns=columns, again=again):
                    write(targets[::-1], value, columns, again)


def weight_grad(place, blocks, pairs, selects=()):
    total, width = pairs[0][0].shape
    rows = width // blocks
    split = 1 if blocks == 1 else 2
    row_tile = math.gcd(rows, ROW_TILE)
    row_tiles = rows // row_tile
    spans, end = [], 0
    for index, (_, right) in enumerate(pairs):
        if selects and index and selects[index][0] == selects[index - 1][0]:
            spans.append(spans[-1])
            continue
        size = selects[index][1].shape[0] if selects else right.shape[1]
        spans.append((end, end + size))
        end += size
    first = lambda b, r, p: lax.rem(p[0] - b + blocks, blocks) * row_tiles + r
    selected = [table is not None for _, table in selects] or [False] * len(pairs)
    extra = [jnp.asarray(table, low_type) for _, table in selects if table is not None]
    return pl.pallas_call(
        functools.partial(weight_grad_kernel, spans, selected, split),
        grid_spec=pltpu.PrefetchScalarGridSpec(
            num_scalar_prefetch=1,
            grid=(blocks, row_tiles),
            in_specs=[
                pl.BlockSpec((left.shape[0], row_tile), lambda b, r, p: (0, first(b, r, p))) for left, _ in pairs
            ]
            + [resident(right.shape) for _, right in pairs]
            + [resident(value.shape) for value in extra],
            out_specs=[pl.BlockSpec((row_tile // split, end), lambda b, r, p: (r, 0))] * (blocks * split),
        ),
        out_shape=[jax.ShapeDtypeStruct((rows // split, end), low_type)] * (blocks * split),
        compiler_params=params(),
        cost_estimate=cost(2 * total * width * end, 2 * total * (end + width * len(pairs))),
        name="weight_grad",
    )(place, *[left for left, _ in pairs], *[right for _, right in pairs], *extra)


ROOT_TWO = math.sqrt(correct_two)


def adam_step(grad, first, second, reciprocal):
    first_new = beta_one * first + (1.0 - beta_one) * grad
    second_new = beta_two * second + ((1.0 - beta_two) * grad) * grad
    root = second_new * lax.rsqrt(jnp.maximum(second_new, 1e-30)) + adam_epsilon * ROOT_TWO
    return first_new, second_new, first_new * reciprocal(root)


def mean_step(total, weight, rate, decay):
    return (rate * ROOT_TWO / correct_one / REPLICA_GROUPS) * total + (rate * decay) * weight


def outer_step(weight, delta, moment):
    moment_new = outer_mu * moment + delta
    return moment_new, weight - outer_rate * (delta + outer_mu * moment_new)


PAIR_ROWS = 4


def feed_update_kernel(place_ref, *refs):
    slots = REPLICA_GROUPS * len(CHUNKS)
    own, other, rest = refs[:slots], refs[slots : 2 * slots], refs[2 * slots :]
    (
        gate_first,
        gate_second,
        gate_weight,
        gate_moment,
        down_first,
        down_second,
        down_weight,
        down_moment,
        gate_first_new,
        gate_second_new,
        gate_delta,
        gate_moment_new,
        gate_master,
        gate_copy,
        down_first_new,
        down_second_new,
        down_delta,
        down_moment_new,
        down_master,
        down_copy,
        gate_grads,
    ) = rest
    near = place_ref[1] == 0
    quick = lambda value: pl.reciprocal(value, approx=True)
    half = down_weight.shape[1] // 2
    groups = [lax.rem(place_ref[2] + k, REPLICA_GROUPS) for k in range(REPLICA_GROUPS)]

    def update(grads, at, first, second, weight, moment, outs, rate, decay):
        first_new, second_new, delta_out, moment_new, master, copy = outs
        start = weight[at]
        total = None
        for group, grad in zip(groups, grads):
            here = (group,) + at
            one, two, step = adam_step(grad, first[here], second[here], quick)
            first_new[here] = one
            second_new[here] = two
            total = step if total is None else total + step
        delta = mean_step(total, start, rate, decay)
        new_moment, new_weight = outer_step(start, delta, moment[at])
        delta_out[at] = delta
        moment_new[at] = new_moment
        master[at] = new_weight
        copy[at] = new_weight.astype(low_type)

    every = slice(None)
    for chunk, (begin, end) in enumerate(CHUNKS):
        for tile in range(begin, end):
            for kind in range(3):
                place = (2 * (tile - begin) + kind) if kind < 2 else (2 * (end - begin) + tile - begin)
                lanes = slice(place * LANES, (place + 1) * LANES)
                mine = [own[chunk * REPLICA_GROUPS + k][:, lanes] for k in range(REPLICA_GROUPS)]
                theirs = [other[chunk * REPLICA_GROUPS + k][:, lanes] for k in range(REPLICA_GROUPS)]
                for side in range(2):
                    grads = [
                        (jnp.where(near, a, b) if side == 0 else jnp.where(near, b, a)).astype(f32)
                        for a, b in zip(mine, theirs)
                    ]
                    at = slice(side * half + tile * LANES, side * half + (tile + 1) * LANES)
                    if kind < 2:
                        for k, grad in enumerate(grads):
                            gate_grads[k, :, kind, at] = grad
                    else:
                        update(
                            grads,
                            (every, at),
                            down_first,
                            down_second,
                            down_weight,
                            down_moment,
                            (down_first_new, down_second_new, down_delta, down_moment_new, down_master, down_copy),
                            inner_rates[4],
                            inner_decays[4],
                        )

    def some_rows(step, _):
        at = (pl.ds(step * PAIR_ROWS, PAIR_ROWS),)
        update(
            [gate_grads[(k,) + at] for k in range(REPLICA_GROUPS)],
            at,
            gate_first,
            gate_second,
            gate_weight,
            gate_moment,
            (gate_first_new, gate_second_new, gate_delta, gate_moment_new, gate_master, gate_copy),
            inner_rates[3],
            inner_decays[3],
        )
        return 0

    lax.fori_loop(0, down_weight.shape[0] // PAIR_ROWS, some_rows, 0)


def feed_update(place, own, other, gating, down):
    rows, _, hidden = gating[2].shape
    size = 32 if rows % 32 == 0 else 16
    steps = rows // size
    own_list = [value for chunk in own for value in chunk]
    other_list = [value for chunk in other for value in chunk]
    plane = pl.BlockSpec((size, hidden), lambda i, p: (i, 0))
    pair = pl.BlockSpec((size, 2, hidden), lambda i, p: (i, 0, 0))
    stack = pl.BlockSpec((REPLICA_GROUPS, size, hidden), lambda i, p: (0, i, 0))
    stack_pair = pl.BlockSpec((REPLICA_GROUPS, size, 2, hidden), lambda i, p: (0, i, 0, 0))
    shape = lambda value, dtype=f32: jax.ShapeDtypeStruct(value.shape, dtype)
    return pl.pallas_call(
        feed_update_kernel,
        grid_spec=pltpu.PrefetchScalarGridSpec(
            num_scalar_prefetch=1,
            grid=(steps,),
            in_specs=[
                pl.BlockSpec((size, value.shape[1]), lambda i, p: (i, 0)) for value in own_list + other_list
            ]
            + [stack_pair, stack_pair, pair, pair, stack, stack, plane, plane],
            out_specs=[stack_pair, stack_pair, pair, pair, pair, pair, stack, stack, plane, plane, plane, plane],
            scratch_shapes=[pltpu.VMEM((REPLICA_GROUPS, size, 2, hidden), f32)],
        ),
        out_shape=[
            shape(gating[0]),
            shape(gating[1]),
            shape(gating[2]),
            shape(gating[2]),
            shape(gating[2]),
            shape(gating[2], low_type),
            shape(down[0]),
            shape(down[1]),
            shape(down[2]),
            shape(down[2]),
            shape(down[2]),
            shape(down[2], low_type),
        ],
        compiler_params=params(),
        cost_estimate=cost(0, rows * hidden * 3 * 90),
        name="feed_update",
    )(place, *own_list, *other_list, *gating, *down)


def attention_update_kernel(place_ref, *refs):
    own, other, rest = refs[:REPLICA_GROUPS], refs[REPLICA_GROUPS : 2 * REPLICA_GROUPS], refs[2 * REPLICA_GROUPS :]
    left, right, states, outs = rest[0], rest[1], rest[2:10], rest[10:]
    near = place_ref[1] == 0
    flat = HEADS * HEAD_WIDTH
    for kind, (start, size) in enumerate(((0, PACK), (PACK, OUTPUT_PACK))):
        first, second, weight, moment = states[4 * kind : 4 * kind + 4]
        first_new, second_new, delta_out, moment_new, master, copy = outs[6 * kind : 6 * kind + 6]
        value = weight[...]
        total = None
        for slot in range(REPLICA_GROUPS):
            group = lax.rem(place_ref[2] + slot, REPLICA_GROUPS)
            mine, theirs = own[slot][:, start : start + size], other[slot][:, start : start + size]
            low, high = jnp.where(near, mine, theirs), jnp.where(near, theirs, mine)
            grad = dot(low, left[:size, :]) + dot(high, right[:size, :])
            one, two, step = adam_step(
                grad, first[group], second[group], lambda item: pl.reciprocal(item, approx=True)
            )
            first_new[group] = one
            second_new[group] = two
            total = step if total is None else total + step
        delta = mean_step(total, value, inner_rates[2 * kind], inner_decays[2 * kind])
        new_moment, new_weight = outer_step(value, delta, moment[...])
        delta_out[...] = delta
        moment_new[...] = new_moment
        master[...] = new_weight
        copy[...] = new_weight.astype(low_type)


def attention_update(place, own, other, query, output):
    rows, columns = query[2].shape
    flat = HEADS * HEAD_WIDTH
    size = math.gcd(rows, 160)
    table = np.zeros((2, PACK, columns), np.float32)
    for place_of in range(flat):
        table[0, place_of, place_of] = 1.0
        table[1, place_of, flat + place_of] = 1.0
    plane = pl.BlockSpec((size, columns), lambda i, p: (i, 0))
    stack = pl.BlockSpec((REPLICA_GROUPS, size, columns), lambda i, p: (0, i, 0))
    shape = lambda value, dtype=f32: jax.ShapeDtypeStruct(value.shape, dtype)
    shapes = []
    for state in (query, output):
        shapes += [shape(state[0]), shape(state[1])] + [shape(state[2])] * 3 + [shape(state[2], low_type)]
    return pl.pallas_call(
        attention_update_kernel,
        grid_spec=pltpu.PrefetchScalarGridSpec(
            num_scalar_prefetch=1,
            grid=(rows // size,),
            in_specs=[
                pl.BlockSpec((size, value.shape[1]), lambda i, p: (i, 0)) for value in (*own, *other)
            ]
            + [resident((PACK, columns))] * 2
            + [stack, stack, plane, plane] * 2,
            out_specs=[stack, stack, plane, plane, plane, plane] * 2,
        ),
        out_shape=shapes,
        compiler_params=params(),
        cost_estimate=cost(0, rows * columns * 2 * 90),
        name="attention_update",
    )(place, *own, *other, jnp.asarray(table[0], low_type), jnp.asarray(table[1], low_type), *query, *output)


def optimize(weight, grad, first, second, moment, rate, decay):
    first_new, second_new, step = adam_step(grad, first, second, lambda value: 1.0 / value)
    delta = mean_step(jnp.sum(step, axis=0), weight, rate, decay)
    moment_new, weight_new = outer_step(weight, delta, moment)
    return (first_new, second_new, delta, moment_new, weight_new, weight_new.astype(low_type))


def doc_layout(lengths, token_length):
    ends = jnp.cumsum(lengths)
    starts = ends - lengths
    places = jnp.arange(token_length, dtype=jnp.int32)
    segment = jnp.sum((places[:, None] >= ends[None, :]).astype(jnp.int32), axis=1)
    member = (segment[:, None] == jnp.arange(lengths.shape[0], dtype=jnp.int32)[None, :]).astype(
        jnp.int32
    )
    offset = jnp.sum(member * starts[None, :], axis=1)
    return offset, places - offset


def rope_tables(position):
    half = HEAD_WIDTH // 2
    frequency = rope_base ** (-2.0 * jnp.arange(half, dtype=f32) / HEAD_WIDTH)
    angle = position.astype(f32)[:, None] * frequency[None, :]
    cosine, sine = jnp.cos(angle), jnp.sin(angle)
    gap = jnp.zeros((angle.shape[0], HALF - half), f32)
    return (
        jnp.concatenate([cosine, gap, cosine, gap], axis=1),
        jnp.concatenate([-sine, gap, sine, gap], axis=1),
    )


def norm_inverse(value):
    return lax.rsqrt(jnp.mean(value * value, axis=-1, keepdims=True) + epsilon)


def norm_backward(value, inverse, gain, grad_normed):
    scaled = gain * grad_normed
    return inverse * scaled - value * inverse**3 * jnp.mean(scaled * value, axis=-1, keepdims=True)


def per_device(
    tokens,
    cotangent,
    doc_lengths,
    query_weight,
    keyvalue_weight_full,
    output_weight,
    gating_weight,
    down_weight,
    norm_gains,
    first_query,
    keyvalue_first_moment,
    first_output,
    first_gating,
    first_down,
    first_gains,
    second_query,
    keyvalue_second_moment,
    second_output,
    second_gating,
    second_down,
    second_gains,
    moment_query,
    keyvalue_outer_momentum,
    moment_output,
    moment_gating,
    moment_down,
    moment_gains,
):
    ring = lax.axis_size("ring")
    spot = lax.axis_index("ring")
    side = lax.axis_index("pair")
    near = side == 0
    rows = query_weight.shape[0]
    width = tokens.shape[1]
    local_rows = tokens.shape[0]
    sequence = local_rows * lax.axis_size("tensor")
    plane = ("pair", "tensor")
    per_group = ring // REPLICA_GROUPS
    direct = per_group == 1 and (2 * rows) % LANES == 0
    zero = jnp.zeros_like(spot)
    mine = side * lax.axis_size("tensor") + lax.axis_index("tensor")
    place = jnp.stack([spot if direct else zero, side, spot if direct else zero, mine])
    blocks = ring if direct else 1
    hops = [1, 3, 2]

    def swap(value):
        return lax.ppermute(value, "pair", [(0, 1), (1, 0)])

    def across(value, bit):
        count = lax.axis_size("tensor")
        return lax.ppermute(value, "tensor", [(i, i ^ bit) for i in range(count)])

    def add(left, right):
        return (left.astype(f32) + right.astype(f32)).astype(low_type)

    def core_stage(kept, sent):
        shape = (2, 2, local_rows, width)
        kept, other = kept.reshape(shape), across(sent, 1).reshape(shape)
        cut = local_rows // 2
        spans = [
            (slice(None), 0, slice(None, cut)),
            (slice(None), 1, slice(None, cut)),
            (0, slice(None), slice(cut, None)),
            (1, slice(None), slice(cut, None)),
        ]
        return [add(kept[span], other[span]) for span in spans]

    def chip_send(parts):
        return across(parts[1], 2), swap(parts[3])

    def chip_stage(parts, *earlier, came=None):
        by_x, by_y = after(came or chip_send(parts), *earlier)
        return add(parts[0], by_x), add(parts[2], by_y)

    def last_send(parts):
        return swap(parts[0][1]), across(parts[1][1], 2)

    def last_stage(parts, *earlier, came=None):
        one, two = parts
        by_y, by_x = after(came or last_send(parts), *earlier)
        return jnp.concatenate(
            [one[0].astype(f32) + by_y.astype(f32), two[0].astype(f32) + by_x.astype(f32)], axis=0
        )

    def hop(value, step):
        return lax.ppermute(value, "ring", [(i, (i + step) % ring) for i in range(ring)])

    def halves(kept, sent, other=None):
        other = swap(sent) if other is None else other
        return jnp.concatenate([jnp.where(near, kept, other), jnp.where(near, other, kept)], axis=0)

    def gather(shard):
        return lax.all_gather(shard, "ring", axis=0, tiled=True)

    def gather_hops(shard):
        if not direct:
            return [gather(shard)]
        found = [shard] + [None] * (ring - 1)
        for step in hops:
            found[step] = hop(shard, step)
        return found

    def relay(found):
        if not direct:
            return [gather(found[0])] if found[0].shape[0] == 2 * rows else found
        return found + [hop(found[-1], 1)]

    def gather_first(value):
        cut = local_rows // 2
        return value, across(value[:cut], 2), swap(value[cut:])

    def gather_second(parts):
        value, by_x, by_y = parts
        cut = local_rows // 2
        one = jnp.stack([value[:cut], by_x])
        two = jnp.stack([value[cut:], by_y])
        return one, two, swap(one), across(two, 2)

    def gather_pieces(parts):
        one, two, one_y, two_x = parts
        pieces = {(0, 0, 0): one[0], (0, 1, 0): one[1], (0, 0, 1): two[0], (1, 0, 1): two[1]}
        pieces |= {(1, 0, 0): one_y[0], (1, 1, 0): one_y[1], (0, 1, 1): two_x[0], (1, 1, 1): two_x[1]}
        early = across(jnp.concatenate([one, two], axis=0), 1)
        late_one, late_two = across(one_y, 1), across(two_x, 1)
        far = {(0, 0, 0): early[0], (0, 1, 0): early[1], (0, 0, 1): early[2], (1, 0, 1): early[3]}
        far |= {(1, 0, 0): late_one[0], (1, 1, 0): late_one[1], (0, 1, 1): late_two[0], (1, 1, 1): late_two[1]}
        found = []
        for by_y in range(2):
            for by_x in range(2):
                for group in (pieces, far):
                    found += [group[by_y, by_x, 0], group[by_y, by_x, 1]]
        return jnp.concatenate(found, axis=0)

    def gather_last(parts):
        one, two, one_y, two_x = parts
        ones = [one[0], one[1], one_y[0], one_y[1]]
        twos = [two[0], two_x[0], two[1], two_x[1]]
        mine = jnp.concatenate([half for pair in zip(ones, twos) for half in pair], axis=0)
        other = across(mine, 1)
        found = []
        for start in range(0, mine.shape[0], local_rows):
            found += [mine[start : start + local_rows], other[start : start + local_rows]]
        return jnp.concatenate(found, axis=0)

    def sides(grads):
        if direct:
            return grads[1::2], grads[0::2]
        whole = grads[0].reshape(ring, 2, rows, -1)
        return (lax.dynamic_index_in_dim(whole, 1 - side, 1, False), lax.dynamic_index_in_dim(whole, side, 1, False))

    def deliver(grads):
        if not direct:
            whole = lax.all_to_all(grads, "ring", split_axis=0, concat_axis=0, tiled=True).astype(f32)
            whole = whole.reshape((REPLICA_GROUPS, per_group) + whole.shape[1:])
            whole = jnp.sum(whole, axis=1).astype(low_type)
            return [whole[k] for k in range(REPLICA_GROUPS)]
        found = [grads[0]] + [None] * (ring - 1)
        for step in hops:
            found[step] = hop(grads[step], -step)
        return found

    def tensor_sum(value):
        count = lax.axis_size("tensor")
        bit = 1
        while bit < count:
            value = value + across(value, bit)
            bit *= 2
        return value

    tokens_all = lax.all_gather(tokens, plane, axis=0, tiled=True)

    flat = HEADS * HEAD_WIDTH
    query_halves = [query_weight[:, :flat], query_weight[:, flat:]]
    pair_halves = [
        keyvalue_weight_full[:, :, :HEAD_WIDTH].reshape(rows, 2 * HEAD_WIDTH),
        keyvalue_weight_full[:, :, HEAD_WIDTH:].reshape(rows, 2 * HEAD_WIDTH),
    ]
    gain_columns = jnp.concatenate(
        [norm_gains.T, jnp.zeros((rows, PACK - flat - 2 * HEAD_WIDTH - 2), f32)], axis=1
    )
    packed = [
        jnp.concatenate([q, p, gain_columns], axis=1).astype(low_type)
        for q, p in zip(query_halves, pair_halves)
    ]
    output_low = output_weight.astype(low_type)
    output_parts = [output_low[:, :flat], output_low[:, flat:]]
    pick = lambda parts: (jnp.where(near, parts[0], parts[1]), jnp.where(near, parts[1], parts[0]))
    attention_shard = halves(*pick(packed))
    attention_blocks = gather_hops(attention_shard)
    output_kept, output_sent = pick(output_parts)
    output_came = swap(after(output_sent, attention_shard))
    output_shard = halves(output_kept, output_sent, output_came)
    output_blocks = gather_hops(after(output_shard, attention_blocks[1:2]))

    feed_parts = pack_feed(after(place, attention_shard), gating_weight, down_weight)
    tokens_all = after(tokens_all, feed_parts)
    kept, sent = feed_parts[: len(CHUNKS)], feed_parts[len(CHUNKS) :]
    feed_shards, came = [], []
    last = output_came
    for a, b in zip(kept, sent):
        came.append(swap(after(b, last)))
        last = halves(a, b, came[-1])
        feed_shards.append(last)
    one = relay([after(feed_shards[0], attention_blocks)])
    cotangent_parts = gather_first(after(cotangent, tokens_all))

    other_lengths = swap(doc_lengths)
    lengths = [jnp.where(near, doc_lengths[0], other_lengths[0]), jnp.where(near, other_lengths[0], doc_lengths[0])]
    layouts = [doc_layout(value, sequence) for value in lengths]
    starts = jnp.broadcast_to(
        jnp.concatenate([value[0] for value in layouts])[None, :], (8, 2 * sequence)
    ).astype(jnp.int32)
    cosine, sine = rope_tables(jnp.concatenate([value[1] for value in layouts]))

    cosine = after(cosine, came[0])
    normed_one, heads, gains, wide = project(place, tokens_all, attention_blocks, cosine, sine)
    gain_one, gain_two = gains[0], gains[1]
    heads = after(heads, cotangent_parts)
    mixed, totals, *partial = attend(place, heads, starts, output_blocks, sequence)
    cotangent_parts = gather_second(cotangent_parts)
    partial = after(partial, cotangent_parts, one)
    one = relay(one)
    parts = after(core_stage(*partial), one)
    one = relay(one)
    cotangent_all = gather_last(after(cotangent_parts, parts))
    parts = after(chip_stage(parts, one), cotangent_all)
    two = relay([after(feed_shards[1], one)])
    attention = last_stage(parts, two)

    hidden = tokens.astype(f32)
    inverse_one = norm_inverse(hidden)
    hidden_one = hidden + attention
    inverse_two = norm_inverse(hidden_one)
    normed_two = (hidden_one * inverse_two * gain_two).astype(low_type)
    two = relay(two)
    normed_parts = after(gather_second(gather_first(normed_two)), two)
    two = relay(two)
    normed_two_all = gather_pieces(normed_parts)
    hid, grad_pair = feed(place, normed_two_all, cotangent_all, one)
    theirs, mine = sides(weight_grad(place, blocks, [(normed_two_all, grad_pair), (cotangent_all, hid)]))
    theirs_one = deliver(theirs)
    others_one = [swap(theirs_one[0])]
    normed_late = after(normed_two_all, theirs[0])
    hid_two, grad_pair_two = feed(place, normed_late, cotangent_all, two)
    partial = spread(place, after([grad_pair, grad_pair_two], others_one), [one, two], 0)
    partial = after(partial, theirs_one)
    others_one += [swap(after(value, partial)) for value in theirs_one[1:3]]
    parts = core_stage(*partial)
    mine_one = deliver(after(mine, partial))
    theirs, mine_later = sides(
        weight_grad(place, blocks, [(normed_two_all, after(grad_pair_two, *parts)), (cotangent_all, hid_two)])
    )
    parts = after(chip_stage(parts, theirs[0]), others_one, mine_one[1:2])
    theirs_two = deliver(theirs)
    feed_partial = spread(place, after([hid, hid_two], *parts), [one, two], 2)
    grad_normed_two = last_stage(parts, *feed_partial, theirs_two[1:2], theirs_two[3:])

    grad_hidden_one = cotangent.astype(f32) + norm_backward(
        hidden_one, inverse_two, gain_two, grad_normed_two
    )
    grad_gain_two = jnp.sum(grad_normed_two * hidden_one * inverse_two, axis=0)
    grad_hidden_all = lax.all_gather(grad_hidden_one.astype(low_type), plane, axis=0, tiled=True)
    feed_parts = chip_stage(core_stage(*after(feed_partial, grad_hidden_one)))
    feed_came = last_send(feed_parts)
    grad_hidden_all = after(grad_hidden_all, theirs_two, mine_one[3:], feed_came)
    mine_two = deliver(after(mine_later, grad_hidden_all))
    others_one.append(swap(after(theirs_one[3], grad_hidden_all)))
    others_two = [swap(after(value, grad_hidden_all)) for value in theirs_two[:2]]

    grad_query, grad_pair = attend_grad(
        place, grad_hidden_all, heads, totals, starts, cosine, sine, output_blocks, sequence
    )
    grad_heads = jnp.concatenate([grad_query, grad_pair], axis=1)
    *partial, gain_sums = project_grad(place, grad_heads, tokens_all, wide)
    grad_gains = jnp.stack([jnp.sum(gain_sums, axis=0), grad_gain_two], axis=0)
    grad_gains = jnp.concatenate([grad_gains, jnp.zeros((6, width), f32)], axis=0).astype(low_type)
    partial = after(partial, mine_one, others_one, others_two, mine_two[1:2])
    parts = core_stage(*partial)
    others_two += [swap(after(value, partial)) for value in theirs_two[2:]]
    theirs, mine = sides(
        weight_grad(
            place,
            blocks,
            [
                (normed_one, after(grad_heads, *parts)),
                (grad_gains, jnp.asarray(gains_selector(), low_type)),
                (grad_hidden_all, mixed),
            ],
            gradient_selectors(),
        )
    )
    parts = after(chip_stage(parts, theirs[0]), mine_two, others_two[:3])
    theirs_last = deliver(theirs)
    came = last_send(parts)
    grad_normed_one = last_stage(parts, came=came)
    mine_one, others_one, mine_two, others_two, theirs_last = after(
        (mine_one, others_one, mine_two, others_two, theirs_last), came
    )
    mine_last = deliver(after(mine, theirs_last))
    others_last = [swap(theirs_last[0]), swap(jnp.stack(theirs_last[1:]))]
    block_output = (hidden_one + last_stage(feed_parts, came=feed_came)).astype(low_type)

    token_grad = (
        grad_hidden_one + norm_backward(hidden, inverse_one, gain_one, grad_normed_one)
    ).astype(low_type)

    updated = feed_update(
        place,
        [mine_one, mine_two],
        [others_one, others_two],
        (first_gating, second_gating, gating_weight, moment_gating),
        (first_down, second_down, down_weight, moment_down),
    )
    mine_last = after(mine_last, updated[0])
    others_last = [others_last[0]] + [others_last[1][k] for k in range(REPLICA_GROUPS - 1)]
    attention_updated = attention_update(
        place,
        mine_last,
        others_last,
        (first_query, second_query, query_weight, moment_query),
        (first_output, second_output, output_weight, moment_output),
    )
    qry, out = attention_updated[:6], attention_updated[6:]
    columns = slice(flat, flat + 2 * HEAD_WIDTH + 2)
    both = [jnp.stack([value[:, columns] for value in part]) for part in (mine_last, others_last)]
    both = [jnp.where(near, both[0], both[1]), jnp.where(near, both[1], both[0])]
    if direct:
        both = [jnp.roll(value, spot, axis=0) for value in both]
    both = [value.astype(f32) for value in both]
    pair_total = jnp.concatenate(
        [value[..., : 2 * HEAD_WIDTH].reshape(REPLICA_GROUPS, rows, 2, HEAD_WIDTH) for value in both], axis=-1
    )
    gains_total = jnp.swapaxes(both[0][..., 2 * HEAD_WIDTH :] + both[1][..., 2 * HEAD_WIDTH :], 1, 2)
    gains_total = tensor_sum(gains_total)
    kvl = optimize(
        keyvalue_weight_full,
        pair_total,
        keyvalue_first_moment,
        keyvalue_second_moment,
        keyvalue_outer_momentum,
        inner_rates[1],
        inner_decays[1],
    )
    gns = optimize(
        norm_gains, gains_total, first_gains, second_gains, moment_gains, inner_rates[5], inner_decays[5]
    )
    gat = updated[:6]
    dwn = updated[6:]
    return (block_output, token_grad, *qry, *kvl, *out, *gat, *dwn, *gns)


def solution(mesh):
    shape = (mesh.shape["dp"] // 2, 2, mesh.shape["tensor"])
    mesh = Mesh(mesh.devices.reshape(shape), ("ring", "pair", "tensor"))
    dp = ("ring", "pair")
    matrix = P(dp, "tensor")
    pair = P(dp, None, "tensor")
    stack = P(None, dp, "tensor")
    stack_pair = P(None, dp, None, "tensor")
    tokens = P(("ring", "pair", "tensor"), None)
    gains = P(None, dp)
    stack_gains = P(None, None, dp)
    weights = (matrix, pair, matrix, pair, matrix, gains)
    states = (stack, stack_pair, stack, stack_pair, stack, stack_gains)
    outs = []
    for weight, state in zip(weights, states):
        outs += [state, state, weight, weight, weight, weight]
    return jax.shard_map(
        per_device,
        mesh=mesh,
        in_specs=(tokens, tokens, P(dp, None), *weights, *states, *states, *weights),
        out_specs=(tokens, tokens, *outs),
        check_vma=False,
    )
```

```python
import functools
import math

import jax
import jax.numpy as jnp
import numpy as np
from jax import lax
from jax.experimental import pallas as pl
from jax.experimental.pallas import tpu as pltpu
from jax.sharding import Mesh, PartitionSpec as P

HEAD_WIDTH = 80
REPLICA_GROUPS = 4
STEP = 8
LANES = 128
HEADS = 4
TILE = 256
PACK = 512
WIDE = 768
HALF = 64
VMEM_BYTES = 58 * 2**20

epsilon = 1e-05
rope_base = 1000000.0
beta_one = 0.9
beta_two = 0.95
adam_epsilon = 1e-08
outer_mu = 0.9
outer_rate = 0.7
inner_rates = (0.05, 0.05, 0.2, 0.05, 0.05, 0.5)
inner_decays = (0.1, 0.1, 0.1, 0.1, 0.1, 0.0)
correct_one = 1.0 - beta_one**STEP
correct_two = 1.0 - beta_two**STEP

low_type = jnp.bfloat16
f32 = jnp.float32

NN = (((1,), (0,)), ((), ()))
NT = (((1,), (1,)), ((), ()))
TN = (((0,), (0,)), ((), ()))

CHUNKS = ((0, 3), (3, 7))


def after(value, *earlier):
    return lax.optimization_barrier((value, earlier))[0]


def dot(left, right, dims=NN):
    return lax.dot_general(left, right, dims, preferred_element_type=f32)


def params(**kwargs):
    return pltpu.CompilerParams(vmem_limit_bytes=VMEM_BYTES, **kwargs)


COST_SHARE = 1.0


def cost(flops, size):
    return pl.CostEstimate(
        flops=int(COST_SHARE * flops), bytes_accessed=int(COST_SHARE * size), transcendentals=0
    )


SHORT = pl.CostEstimate(flops=1, bytes_accessed=1, transcendentals=0)


def resident(shape):
    zeros = (0,) * len(shape)
    return pl.BlockSpec(shape, lambda *_: zeros, pipeline_mode=pl.Buffered(1))


def projection_selector():
    table = np.zeros((PACK, WIDE), np.float32)
    for head in range(HEADS + 1):
        for place in range(HEAD_WIDTH):
            half, rest = divmod(place, HEAD_WIDTH // 2)
            table[head * HEAD_WIDTH + place, head * LANES + half * HALF + rest] = 1.0
    for place in range(HEAD_WIDTH):
        table[(HEADS + 1) * HEAD_WIDTH + place, (HEADS + 1) * LANES + place] = 1.0
    return table


def output_selector():
    table = np.zeros((HEADS * HEAD_WIDTH, HEADS * LANES), np.float32)
    for head in range(HEADS):
        for place in range(HEAD_WIDTH):
            table[head * HEAD_WIDTH + place, head * LANES + place] = 1.0
    return table


OUTPUT_PACK = 384


def gradient_selectors():
    project, output = projection_selector(), output_selector()
    padded = np.zeros((OUTPUT_PACK, HEADS * LANES), np.float32)
    padded[: output.shape[0]] = output
    return ((0, project), (0, None), (1, padded))


def gains_selector():
    table = np.zeros((8, PACK), np.float32)
    table[0, (HEADS + 2) * HEAD_WIDTH] = 1.0
    table[1, (HEADS + 2) * HEAD_WIDTH + 1] = 1.0
    return table


def seen_from(place_ref, piece):
    return lax.bitwise_xor(piece, place_ref[3])


def piece_specs(width, piece):
    return [pl.BlockSpec((TILE, width), lambda *at: (lax.shift_right_logical(piece(*at), 1), 0))] * 2


def piece_shapes(total, width):
    return [jax.ShapeDtypeStruct((total // 2, width), low_type)] * 2


def write_piece(piece, kept, sent, value):
    odd = lax.bitwise_and(piece, 1)

    @pl.when(odd == 0)
    def _():
        kept[...] = value

    @pl.when(odd == 1)
    def _():
        sent[...] = value


def first_row(place, step, blocks, rows):
    return pl.multiple_of(lax.rem(place - step + blocks, blocks) * rows, LANES if blocks > 1 else rows)


def assemble(place, blocks, target):
    rows = blocks[0].shape[0]
    for step, block in enumerate(blocks):
        target[pl.ds(first_row(place, step, len(blocks), rows), rows), :] = block[...]


def projection_kernel(count, place_ref, tokens, *refs):
    blocks, (select, pick, cosine, sine, normed, heads, gains, wide) = refs[:count], refs[count:]

    @pl.when(pl.program_id(0) == 0)
    def _():
        rows = blocks[0].shape[0]
        for step, block in enumerate(blocks):
            start = first_row(place_ref[0], step, count, rows)
            value = block[...]
            wide[pl.ds(start, rows), :] = dot(value, select[...]).astype(low_type)
            gains[:, pl.ds(start, rows)] = dot(pick[...], value, NT)

    value = tokens[...].astype(f32)
    inverse = lax.rsqrt(jnp.mean(value * value, axis=-1, keepdims=True) + epsilon)
    low = (value * inverse * gains[0:1, :]).astype(low_type)
    normed[...] = low
    result = dot(low, wide[...])
    cos_tile = cosine[...]
    sin_tile = sine[...]
    for head in range(HEADS + 1):
        part = result[:, head * LANES : (head + 1) * LANES]
        turned = part * cos_tile + pltpu.roll(part, HALF, 1) * sin_tile
        heads[:, head * LANES : (head + 1) * LANES] = turned.astype(low_type)
    heads[:, (HEADS + 1) * LANES :] = result[:, (HEADS + 1) * LANES :].astype(low_type)


def project(place, tokens, blocks, cosine, sine):
    total, width = tokens.shape
    tile = lambda columns: pl.BlockSpec((TILE, columns), lambda i, p: (i, 0))
    return pl.pallas_call(
        functools.partial(projection_kernel, len(blocks)),
        grid_spec=pltpu.PrefetchScalarGridSpec(
            num_scalar_prefetch=1,
            grid=(total // TILE,),
            in_specs=[tile(width)]
            + [resident(block.shape) for block in blocks]
            + [
                resident((PACK, WIDE)),
                resident((8, PACK)),
                tile(LANES),
                tile(LANES),
            ],
            out_specs=[
                tile(width),
                tile(WIDE),
                pl.BlockSpec((8, width), lambda *_: (0, 0)),
                pl.BlockSpec((width, WIDE), lambda *_: (0, 0)),
            ],
        ),
        out_shape=[
            jax.ShapeDtypeStruct((total, width), low_type),
            jax.ShapeDtypeStruct((total, WIDE), low_type),
            jax.ShapeDtypeStruct((8, width), f32),
            jax.ShapeDtypeStruct((width, WIDE), low_type),
        ],
        compiler_params=params(),
        cost_estimate=cost(2 * total * width * WIDE, 4 * total * width + 3 * width * WIDE * 2),
        name="projection",
    )(
        place,
        tokens,
        *blocks,
        jnp.asarray(projection_selector(), low_type),
        jnp.asarray(gains_selector(), low_type),
        cosine,
        sine,
    )


SCORE_SCALE = math.log2(math.e) / math.sqrt(HEAD_WIDTH)
GRAD_SCALE = 1.0 / math.sqrt(HEAD_WIDTH)


def allowed_pairs(block, width, starts):
    key_index = lax.broadcasted_iota(jnp.int32, (width, TILE), 0)
    row_index = block * TILE + lax.broadcasted_iota(jnp.int32, (1, TILE), 1)
    return (key_index >= starts) & (key_index <= row_index)


def widen_output(place_ref, blocks, select, wide):
    @pl.when((pl.program_id(0) == 0) & (pl.program_id(1) == 0))
    def _():
        rows = blocks[0].shape[0]
        for step, block in enumerate(blocks):
            start = first_row(place_ref[0], step, len(blocks), rows)
            wide[pl.ds(start, rows), :] = dot(block[...], select[...]).astype(low_type)


def attention_kernel(count, blocks_per, place_ref, query, key, value, starts, *refs):
    blocks, (select, mixed, totals, kept, sent, wide) = refs[:count], refs[count:]
    widen_output(place_ref, blocks, select, wide)

    for block in range(blocks_per):

        @pl.when(pl.program_id(1) == block)
        def _(block=block):
            width = (block + 1) * TILE
            allowed = allowed_pairs(block, width, starts[0:1, :])
            keys = key[0:width, :]
            values = value[0:width, :]
            for head in range(HEADS):
                lanes = slice(head * LANES, (head + 1) * LANES)
                scores = dot(keys, query[:, lanes], NT) * SCORE_SCALE
                scores = jnp.where(allowed, scores, -1e30)
                top = jnp.max(scores, axis=0, keepdims=True)
                expo = jnp.exp2(scores - top)
                total = jnp.sum(expo, axis=0, keepdims=True)
                out = dot(values, expo.astype(low_type), TN) * (1.0 / total)
                mixed[:, lanes] = out.T.astype(low_type)
                totals[head : head + 1, :] = top + jnp.log2(total)

    piece = pl.program_id(0) * blocks_per + pl.program_id(1)
    value = dot(mixed[...], wide[...], NT).astype(low_type)
    write_piece(seen_from(place_ref, piece), kept, sent, value)


def attend(place, heads, starts, blocks, sequence):
    total = heads.shape[0]
    width = blocks[0].shape[0] * len(blocks)
    per = sequence // TILE
    tile = lambda size, column: pl.BlockSpec((TILE, size), lambda s, i, *_: (s * per + i, column))
    full = lambda column: pl.BlockSpec((sequence, LANES), lambda s, i, *_: (s, column))
    line = pl.BlockSpec((8, TILE), lambda s, i, *_: (0, s * per + i))
    return pl.pallas_call(
        functools.partial(attention_kernel, len(blocks), per),
        grid_spec=pltpu.PrefetchScalarGridSpec(
            num_scalar_prefetch=1,
            grid=(total // sequence, per),
            in_specs=[
                tile(HEADS * LANES, 0),
                full(HEADS),
                full(HEADS + 1),
                line,
            ]
            + [resident(block.shape) for block in blocks]
            + [resident((HEADS * HEAD_WIDTH, HEADS * LANES))],
            out_specs=[tile(HEADS * LANES, 0), line]
            + piece_specs(width, lambda s, i, p: seen_from(p, s * per + i)),
            scratch_shapes=[pltpu.VMEM((width, HEADS * LANES), low_type)],
        ),
        out_shape=[
            jax.ShapeDtypeStruct((total, HEADS * LANES), low_type),
            jax.ShapeDtypeStruct((8, total), f32),
        ]
        + piece_shapes(total, width),
        compiler_params=params(),
        cost_estimate=cost(20e9, 4 * total * width),
        name="attention",
    )(place, heads, heads, heads, starts, *blocks, jnp.asarray(output_selector(), low_type))


def attention_grad_kernel(
    count,
    blocks_per,
    place_ref,
    grad_hidden,
    query,
    key,
    value,
    totals,
    starts,
    cosine,
    sine,
    cos_all,
    sin_all,
    *refs,
):
    blocks, (select, grad_query, grad_pair, wide, key_sum, value_sum) = refs[:count], refs[count:]
    widen_output(place_ref, blocks, select, wide)

    @pl.when(pl.program_id(1) == 0)
    def _():
        key_sum[...] = jnp.zeros_like(key_sum)
        value_sum[...] = jnp.zeros_like(value_sum)

    grad_mixed = dot(grad_hidden[...], wide[...]).astype(low_type)
    cos_tile = cosine[...]
    sin_tile = sine[...]
    for block in range(blocks_per):

        @pl.when(pl.program_id(1) == block)
        def _(block=block):
            width = (block + 1) * TILE
            allowed = allowed_pairs(block, width, starts[0:1, :])
            keys = key[0:width, :]
            values = value[0:width, :]
            key_part = jnp.zeros((width, LANES), f32)
            value_part = jnp.zeros((width, LANES), f32)
            for head in range(HEADS):
                lanes = slice(head * LANES, (head + 1) * LANES)
                queries = query[:, lanes]
                grads = grad_mixed[:, lanes]
                scores = dot(keys, queries, NT) * SCORE_SCALE
                scores = jnp.where(allowed, scores, -1e30)
                prob = jnp.exp2(scores - totals[head : head + 1, :])
                grad_prob = dot(values, grads, NT)
                inner = jnp.sum(prob * grad_prob, axis=0, keepdims=True)
                grad_scores = (prob * (grad_prob - inner)).astype(low_type)
                key_part = key_part + dot(grad_scores, queries)
                value_part = value_part + dot(prob.astype(low_type), grads)
                turned = dot(keys, grad_scores, TN).T * GRAD_SCALE
                turned = turned * cos_tile - pltpu.roll(turned, HALF, 1) * sin_tile
                grad_query[:, lanes] = turned.astype(low_type)
            key_sum[0:width, :] += key_part
            value_sum[0:width, :] += value_part

    @pl.when(pl.program_id(1) == blocks_per - 1)
    def _():
        grad_key = key_sum[...] * GRAD_SCALE
        grad_key = grad_key * cos_all[...] - pltpu.roll(grad_key, HALF, 1) * sin_all[...]
        grad_pair[:, :LANES] = grad_key.astype(low_type)
        grad_pair[:, LANES:] = value_sum[...].astype(low_type)


def attend_grad(place, grad_hidden, heads, totals, starts, cosine, sine, blocks, sequence):
    total, width = grad_hidden.shape
    per = sequence // TILE
    tile = lambda size, column: pl.BlockSpec((TILE, size), lambda s, i, p: (s * per + i, column))
    full = lambda size, column: pl.BlockSpec((sequence, size), lambda s, i, p: (s, column))
    line = pl.BlockSpec((8, TILE), lambda s, i, p: (0, s * per + i))
    return pl.pallas_call(
        functools.partial(attention_grad_kernel, len(blocks), per),
        grid_spec=pltpu.PrefetchScalarGridSpec(
            num_scalar_prefetch=1,
            grid=(total // sequence, per),
            in_specs=[
                tile(width, 0),
                tile(HEADS * LANES, 0),
                full(LANES, HEADS),
                full(LANES, HEADS + 1),
                line,
                line,
                tile(LANES, 0),
                tile(LANES, 0),
                full(LANES, 0),
                full(LANES, 0),
            ]
            + [resident(block.shape) for block in blocks]
            + [resident((HEADS * HEAD_WIDTH, HEADS * LANES))],
            out_specs=[tile(HEADS * LANES, 0), full(2 * LANES, 0)],
            scratch_shapes=[
                pltpu.VMEM((width, HEADS * LANES), low_type),
                pltpu.VMEM((sequence, LANES), f32),
                pltpu.VMEM((sequence, LANES), f32),
            ],
        ),
        out_shape=[
            jax.ShapeDtypeStruct((total, HEADS * LANES), low_type),
            jax.ShapeDtypeStruct((total, 2 * LANES), low_type),
        ],
        compiler_params=params(),
        cost_estimate=cost(30e9, 4 * total * width),
        name="attention_grad",
    )(
        place,
        grad_hidden,
        heads,
        heads,
        heads,
        totals,
        starts,
        cosine,
        sine,
        cosine,
        sine,
        *blocks,
        jnp.asarray(output_selector(), low_type),
    )


def projection_grad_kernel(place_ref, grad_heads, tokens, wide, kept, sent, gain_sums):
    grad = dot(grad_heads[...], wide[...], NT)
    write_piece(seen_from(place_ref, pl.program_id(0)), kept, sent, grad.astype(low_type))
    value = tokens[...].astype(f32)
    inverse = lax.rsqrt(jnp.mean(value * value, axis=-1, keepdims=True) + epsilon)
    product = grad * (value * inverse)
    sums = jnp.sum(product.reshape(TILE // 8, 8, product.shape[1]), axis=0)

    @pl.when(pl.program_id(0) == 0)
    def _():
        gain_sums[...] = sums

    @pl.when(pl.program_id(0) != 0)
    def _():
        gain_sums[...] += sums


def project_grad(place, grad_heads, tokens, wide):
    total, width = tokens.shape
    tile = lambda columns: pl.BlockSpec((TILE, columns), lambda i, *_: (i, 0))
    return pl.pallas_call(
        projection_grad_kernel,
        grid_spec=pltpu.PrefetchScalarGridSpec(
            num_scalar_prefetch=1,
            grid=(total // TILE,),
            in_specs=[
                tile(WIDE),
                tile(width),
                resident((width, WIDE)),
            ],
            out_specs=piece_specs(width, lambda i, p: seen_from(p, i)) + [pl.BlockSpec((8, width), lambda i, *_: (0, 0))],
        ),
        out_shape=piece_shapes(total, width) + [jax.ShapeDtypeStruct((8, width), f32)],
        compiler_params=params(),
        cost_estimate=SHORT,
        name="projection_grad",
    )(place, grad_heads, tokens, wide)


def pack_kernel(place_ref, gating, down, *outs):
    kept, sent = outs[: len(CHUNKS)], outs[len(CHUNKS) :]

    def write(targets):
        for (first, last), target in zip(CHUNKS, targets):
            count = last - first
            for tile in range(first, last):
                lanes = slice(tile * LANES, (tile + 1) * LANES)
                place = (tile - first) * 2 * LANES
                target[:, place : place + LANES] = gating[:, 0, lanes].astype(low_type)
                target[:, place + LANES : place + 2 * LANES] = gating[:, 1, lanes].astype(low_type)
                place = (2 * count + tile - first) * LANES
                target[:, place : place + LANES] = down[:, lanes].astype(low_type)

    @pl.when(pl.program_id(0) == 0)
    def _():
        write(sent)

    @pl.when(pl.program_id(0) == 1)
    def _():
        write(kept)


def pack_feed(place, gating, down):
    rows, _, hidden = gating.shape
    half = hidden // 2
    side = lambda i, place_ref: jnp.where(i == 0, 1 - place_ref[1], place_ref[1])
    shapes = [(rows, 3 * LANES * (last - first)) for first, last in CHUNKS] * 2
    return pl.pallas_call(
        pack_kernel,
        grid_spec=pltpu.PrefetchScalarGridSpec(
            num_scalar_prefetch=1,
            grid=(2,),
            in_specs=[
                pl.BlockSpec((rows, 2, half), lambda i, p: (0, 0, side(i, p))),
                pl.BlockSpec((rows, half), lambda i, p: (0, side(i, p))),
            ],
            out_specs=[pl.BlockSpec(shape, lambda *_: (0, 0)) for shape in shapes],
        ),
        out_shape=[jax.ShapeDtypeStruct(shape, low_type) for shape in shapes],
        compiler_params=params(),
        cost_estimate=cost(0, 18 * rows * hidden),
        name="pack_feed",
    )(place, gating, down)


def feed_kernel(count, tiles, place_ref, normed, grad_out, *refs):
    blocks, (hidden, grad_pair, weights) = refs[:count], refs[count:]

    @pl.when(pl.program_id(0) == 0)
    def _():
        assemble(place_ref[0], blocks, weights)

    pair = dot(normed[...], weights[:, : 2 * tiles * LANES])
    grad_hidden = dot(grad_out[...], weights[:, 2 * tiles * LANES :])
    for tile in range(tiles):
        place = 2 * tile * LANES
        gate = pair[:, place : place + LANES]
        up = pair[:, place + LANES : place + 2 * LANES]
        grad = grad_hidden[:, tile * LANES : (tile + 1) * LANES]
        sigma = 1.0 / (1.0 + jnp.exp(-gate))
        silu = gate * sigma
        hidden[:, tile * LANES : (tile + 1) * LANES] = (silu * up).astype(low_type)
        grad_gate = grad * up * sigma * (1.0 + gate * (1.0 - sigma))
        grad_pair[:, place : place + LANES] = grad_gate.astype(low_type)
        grad_pair[:, place + LANES : place + 2 * LANES] = (grad * silu).astype(low_type)


def feed(place, normed, grad_out, blocks):
    total, width = normed.shape
    rows, columns = blocks[0].shape
    tiles = columns // (3 * LANES)
    tile = lambda size: pl.BlockSpec((TILE, size), lambda i, p: (i, 0))
    return pl.pallas_call(
        functools.partial(feed_kernel, len(blocks), tiles),
        grid_spec=pltpu.PrefetchScalarGridSpec(
            num_scalar_prefetch=1,
            grid=(total // TILE,),
            in_specs=[tile(width), tile(width)] + [resident(block.shape) for block in blocks],
            out_specs=[tile(tiles * LANES), tile(2 * tiles * LANES)],
            scratch_shapes=[pltpu.VMEM((width, columns), low_type)],
        ),
        out_shape=[
            jax.ShapeDtypeStruct((total, tiles * LANES), low_type),
            jax.ShapeDtypeStruct((total, 2 * tiles * LANES), low_type),
        ],
        compiler_params=params(),
        cost_estimate=cost(2 * total * width * columns, 4 * total * width + 2 * width * columns),
        name="feed",
    )(place, normed, grad_out, *blocks)


def spread_kernel(counts, place_ref, *refs):
    parts = len(counts)
    values, rest = refs[:parts], refs[parts:]
    chunks = []
    for count in counts:
        chunks.append(rest[:count])
        rest = rest[count:]
    kept, sent, wholes = rest[0], rest[1], rest[2:]

    @pl.when(pl.program_id(0) == 0)
    def _():
        for blocks, whole in zip(chunks, wholes):
            assemble(place_ref[0], blocks, whole)

    total = dot(values[0][...], wholes[0][...], NT)
    for value, whole in zip(values[1:], wholes[1:]):
        total = total + dot(value[...], whole[...], NT)
    write_piece(pl.program_id(0), kept, sent, total.astype(low_type))


def spread(place, values, chunks, column):
    total = values[0].shape[0]
    width = chunks[0][0].shape[0] * len(chunks[0])
    tile = lambda size: pl.BlockSpec((TILE, size), lambda i, p: (i, 0))
    return pl.pallas_call(
        functools.partial(spread_kernel, tuple(len(blocks) for blocks in chunks)),
        grid_spec=pltpu.PrefetchScalarGridSpec(
            num_scalar_prefetch=1,
            grid=(total // TILE,),
            in_specs=[tile(value.shape[1]) for value in values]
            + [
                pl.BlockSpec(
                    (block.shape[0], value.shape[1]), lambda *_: (0, column), pipeline_mode=pl.Buffered(1)
                )
                for value, blocks in zip(values, chunks)
                for block in blocks
            ],
            out_specs=piece_specs(width, lambda i, p: i),
            scratch_shapes=[pltpu.VMEM((width, value.shape[1]), low_type) for value in values],
        ),
        out_shape=piece_shapes(total, width),
        compiler_params=params(),
        cost_estimate=SHORT,
        name="spread",
    )(place, *values, *[block for blocks in chunks for block in blocks])


ROW_TILE = 640


def weight_grad_kernel(spans, selected, split, place_ref, *refs):
    parts = len(spans)
    lefts, rights, rest = refs[:parts], refs[parts : 2 * parts], refs[2 * parts :]
    outs = rest[sum(selected) :]
    selects = [rest[sum(selected[:place])] if chosen else None for place, chosen in enumerate(selected)]

    def write(targets, value, columns, again):
        size = targets[0].shape[0]
        for place, target in enumerate(targets):
            rows = value[place * size : (place + 1) * size]
            if again:
                rows = rows + target[:, columns].astype(f32)
            target[:, columns] = rows.astype(low_type)

    for block in range(len(outs) // split):
        targets = outs[block * split : (block + 1) * split]

        @pl.when(pl.program_id(0) == block)
        def _(targets=targets):
            for place, (left, right) in enumerate(zip(lefts, rights)):
                value = dot(left[...], right[...], TN).astype(low_type)
                if selects[place] is not None:
                    value = dot(value, selects[place][...], NT)
                columns = slice(*spans[place])
                again = place and spans[place] == spans[place - 1]
                if split == 1:
                    write(targets, value, columns, again)
                    continue

                @pl.when(place_ref[1] == 0)
                def _(value=value, columns=columns, again=again):
                    write(targets, value, columns, again)

                @pl.when(place_ref[1] != 0)
                def _(value=value, columns=columns, again=again):
                    write(targets[::-1], value, columns, again)


def weight_grad(place, blocks, pairs, selects=()):
    total, width = pairs[0][0].shape
    rows = width // blocks
    split = 1 if blocks == 1 else 2
    row_tile = math.gcd(rows, ROW_TILE)
    row_tiles = rows // row_tile
    spans, end = [], 0
    for index, (_, right) in enumerate(pairs):
        if selects and index and selects[index][0] == selects[index - 1][0]:
            spans.append(spans[-1])
            continue
        size = selects[index][1].shape[0] if selects else right.shape[1]
        spans.append((end, end + size))
        end += size
    first = lambda b, r, p: lax.rem(p[0] - b + blocks, blocks) * row_tiles + r
    selected = [table is not None for _, table in selects] or [False] * len(pairs)
    extra = [jnp.asarray(table, low_type) for _, table in selects if table is not None]
    return pl.pallas_call(
        functools.partial(weight_grad_kernel, spans, selected, split),
        grid_spec=pltpu.PrefetchScalarGridSpec(
            num_scalar_prefetch=1,
            grid=(blocks, row_tiles),
            in_specs=[
                pl.BlockSpec((left.shape[0], row_tile), lambda b, r, p: (0, first(b, r, p))) for left, _ in pairs
            ]
            + [resident(right.shape) for _, right in pairs]
            + [resident(value.shape) for value in extra],
            out_specs=[pl.BlockSpec((row_tile // split, end), lambda b, r, p: (r, 0))] * (blocks * split),
        ),
        out_shape=[jax.ShapeDtypeStruct((rows // split, end), low_type)] * (blocks * split),
        compiler_params=params(),
        cost_estimate=cost(2 * total * width * end, 2 * total * (end + width * len(pairs))),
        name="weight_grad",
    )(place, *[left for left, _ in pairs], *[right for _, right in pairs], *extra)


ROOT_TWO = math.sqrt(correct_two)


def adam_step(grad, first, second, reciprocal):
    first_new = beta_one * first + (1.0 - beta_one) * grad
    second_new = beta_two * second + ((1.0 - beta_two) * grad) * grad
    root = second_new * lax.rsqrt(jnp.maximum(second_new, 1e-30)) + adam_epsilon * ROOT_TWO
    return first_new, second_new, first_new * reciprocal(root)


def mean_step(total, weight, rate, decay):
    return (rate * ROOT_TWO / correct_one / REPLICA_GROUPS) * total + (rate * decay) * weight


def outer_step(weight, delta, moment):
    moment_new = outer_mu * moment + delta
    return moment_new, weight - outer_rate * (delta + outer_mu * moment_new)


PAIR_ROWS = 4


def feed_update_kernel(place_ref, *refs):
    slots = REPLICA_GROUPS * len(CHUNKS)
    own, other, rest = refs[:slots], refs[slots : 2 * slots], refs[2 * slots :]
    (
        gate_first,
        gate_second,
        gate_weight,
        gate_moment,
        down_first,
        down_second,
        down_weight,
        down_moment,
        gate_first_new,
        gate_second_new,
        gate_delta,
        gate_moment_new,
        gate_master,
        gate_copy,
        down_first_new,
        down_second_new,
        down_delta,
        down_moment_new,
        down_master,
        down_copy,
        gate_grads,
    ) = rest
    near = place_ref[1] == 0
    quick = lambda value: pl.reciprocal(value, approx=True)
    half = down_weight.shape[1] // 2
    groups = [lax.rem(place_ref[2] + k, REPLICA_GROUPS) for k in range(REPLICA_GROUPS)]

    def update(grads, at, first, second, weight, moment, outs, rate, decay):
        first_new, second_new, delta_out, moment_new, master, copy = outs
        start = weight[at]
        total = None
        for group, grad in zip(groups, grads):
            here = (group,) + at
            one, two, step = adam_step(grad, first[here], second[here], quick)
            first_new[here] = one
            second_new[here] = two
            total = step if total is None else total + step
        delta = mean_step(total, start, rate, decay)
        new_moment, new_weight = outer_step(start, delta, moment[at])
        delta_out[at] = delta
        moment_new[at] = new_moment
        master[at] = new_weight
        copy[at] = new_weight.astype(low_type)

    every = slice(None)
    for chunk, (begin, end) in enumerate(CHUNKS):
        for tile in range(begin, end):
            for kind in range(3):
                place = (2 * (tile - begin) + kind) if kind < 2 else (2 * (end - begin) + tile - begin)
                lanes = slice(place * LANES, (place + 1) * LANES)
                mine = [own[chunk * REPLICA_GROUPS + k][:, lanes] for k in range(REPLICA_GROUPS)]
                theirs = [other[chunk * REPLICA_GROUPS + k][:, lanes] for k in range(REPLICA_GROUPS)]
                for side in range(2):
                    grads = [
                        (jnp.where(near, a, b) if side == 0 else jnp.where(near, b, a)).astype(f32)
                        for a, b in zip(mine, theirs)
                    ]
                    at = slice(side * half + tile * LANES, side * half + (tile + 1) * LANES)
                    if kind < 2:
                        for k, grad in enumerate(grads):
                            gate_grads[k, :, kind, at] = grad
                    else:
                        update(
                            grads,
                            (every, at),
                            down_first,
                            down_second,
                            down_weight,
                            down_moment,
                            (down_first_new, down_second_new, down_delta, down_moment_new, down_master, down_copy),
                            inner_rates[4],
                            inner_decays[4],
                        )

    def some_rows(step, _):
        at = (pl.ds(step * PAIR_ROWS, PAIR_ROWS),)
        update(
            [gate_grads[(k,) + at] for k in range(REPLICA_GROUPS)],
            at,
            gate_first,
            gate_second,
            gate_weight,
            gate_moment,
            (gate_first_new, gate_second_new, gate_delta, gate_moment_new, gate_master, gate_copy),
            inner_rates[3],
            inner_decays[3],
        )
        return 0

    lax.fori_loop(0, down_weight.shape[0] // PAIR_ROWS, some_rows, 0)


def feed_update(place, own, other, gating, down):
    rows, _, hidden = gating[2].shape
    size = 32 if rows % 32 == 0 else 16
    steps = rows // size
    own_list = [value for chunk in own for value in chunk]
    other_list = [value for chunk in other for value in chunk]
    plane = pl.BlockSpec((size, hidden), lambda i, p: (i, 0))
    pair = pl.BlockSpec((size, 2, hidden), lambda i, p: (i, 0, 0))
    stack = pl.BlockSpec((REPLICA_GROUPS, size, hidden), lambda i, p: (0, i, 0))
    stack_pair = pl.BlockSpec((REPLICA_GROUPS, size, 2, hidden), lambda i, p: (0, i, 0, 0))
    shape = lambda value, dtype=f32: jax.ShapeDtypeStruct(value.shape, dtype)
    return pl.pallas_call(
        feed_update_kernel,
        grid_spec=pltpu.PrefetchScalarGridSpec(
            num_scalar_prefetch=1,
            grid=(steps,),
            in_specs=[
                pl.BlockSpec((size, value.shape[1]), lambda i, p: (i, 0)) for value in own_list + other_list
            ]
            + [stack_pair, stack_pair, pair, pair, stack, stack, plane, plane],
            out_specs=[stack_pair, stack_pair, pair, pair, pair, pair, stack, stack, plane, plane, plane, plane],
            scratch_shapes=[pltpu.VMEM((REPLICA_GROUPS, size, 2, hidden), f32)],
        ),
        out_shape=[
            shape(gating[0]),
            shape(gating[1]),
            shape(gating[2]),
            shape(gating[2]),
            shape(gating[2]),
            shape(gating[2], low_type),
            shape(down[0]),
            shape(down[1]),
            shape(down[2]),
            shape(down[2]),
            shape(down[2]),
            shape(down[2], low_type),
        ],
        compiler_params=params(),
        cost_estimate=cost(0, rows * hidden * 3 * 90),
        name="feed_update",
    )(place, *own_list, *other_list, *gating, *down)


def attention_update_kernel(place_ref, *refs):
    own, other, rest = refs[:REPLICA_GROUPS], refs[REPLICA_GROUPS : 2 * REPLICA_GROUPS], refs[2 * REPLICA_GROUPS :]
    left, right, states, outs = rest[0], rest[1], rest[2:10], rest[10:]
    near = place_ref[1] == 0
    flat = HEADS * HEAD_WIDTH
    for kind, (start, size) in enumerate(((0, PACK), (PACK, OUTPUT_PACK))):
        first, second, weight, moment = states[4 * kind : 4 * kind + 4]
        first_new, second_new, delta_out, moment_new, master, copy = outs[6 * kind : 6 * kind + 6]
        value = weight[...]
        total = None
        for slot in range(REPLICA_GROUPS):
            group = lax.rem(place_ref[2] + slot, REPLICA_GROUPS)
            mine, theirs = own[slot][:, start : start + size], other[slot][:, start : start + size]
            low, high = jnp.where(near, mine, theirs), jnp.where(near, theirs, mine)
            grad = dot(low, left[:size, :]) + dot(high, right[:size, :])
            one, two, step = adam_step(
                grad, first[group], second[group], lambda item: pl.reciprocal(item, approx=True)
            )
            first_new[group] = one
            second_new[group] = two
            total = step if total is None else total + step
        delta = mean_step(total, value, inner_rates[2 * kind], inner_decays[2 * kind])
        new_moment, new_weight = outer_step(value, delta, moment[...])
        delta_out[...] = delta
        moment_new[...] = new_moment
        master[...] = new_weight
        copy[...] = new_weight.astype(low_type)


def attention_update(place, own, other, query, output):
    rows, columns = query[2].shape
    flat = HEADS * HEAD_WIDTH
    size = math.gcd(rows, 160)
    table = np.zeros((2, PACK, columns), np.float32)
    for place_of in range(flat):
        table[0, place_of, place_of] = 1.0
        table[1, place_of, flat + place_of] = 1.0
    plane = pl.BlockSpec((size, columns), lambda i, p: (i, 0))
    stack = pl.BlockSpec((REPLICA_GROUPS, size, columns), lambda i, p: (0, i, 0))
    shape = lambda value, dtype=f32: jax.ShapeDtypeStruct(value.shape, dtype)
    shapes = []
    for state in (query, output):
        shapes += [shape(state[0]), shape(state[1])] + [shape(state[2])] * 3 + [shape(state[2], low_type)]
    return pl.pallas_call(
        attention_update_kernel,
        grid_spec=pltpu.PrefetchScalarGridSpec(
            num_scalar_prefetch=1,
            grid=(rows // size,),
            in_specs=[
                pl.BlockSpec((size, value.shape[1]), lambda i, p: (i, 0)) for value in (*own, other[0])
            ]
            + [
                pl.BlockSpec((None, size, other[1].shape[2]), lambda i, p, k=k: (k, i, 0))
                for k in range(REPLICA_GROUPS - 1)
            ]
            + [resident((PACK, columns))] * 2
            + [stack, stack, plane, plane] * 2,
            out_specs=[stack, stack, plane, plane, plane, plane] * 2,
        ),
        out_shape=shapes,
        compiler_params=params(),
        cost_estimate=cost(0, rows * columns * 2 * 90),
        name="attention_update",
    )(place, *own, other[0], *[other[1]] * (REPLICA_GROUPS - 1), jnp.asarray(table[0], low_type), jnp.asarray(table[1], low_type), *query, *output)


def keyvalue_update_kernel(place_ref, *refs):
    own, other, rest = refs[:REPLICA_GROUPS], refs[REPLICA_GROUPS : 2 * REPLICA_GROUPS], refs[2 * REPLICA_GROUPS :]
    left, right, pick, first, second, weight, moment = rest[:7]
    first_new, second_new, delta_out, moment_new, master, copy, gains = rest[7:]
    near = place_ref[1] == 0
    value = weight[...]
    total = None
    for slot in range(REPLICA_GROUPS):
        group = lax.rem(place_ref[2] + slot, REPLICA_GROUPS)
        mine, theirs = own[slot][...], other[slot][...]
        low, high = jnp.where(near, mine, theirs), jnp.where(near, theirs, mine)
        gains[group] = dot(pick[...], low, NT) + dot(pick[...], high, NT)
        grad = dot(left[...], low, NT) + dot(right[...], high, NT)
        one, two, step = adam_step(
            grad, first[group], second[group], lambda item: pl.reciprocal(item, approx=True)
        )
        first_new[group] = one
        second_new[group] = two
        total = step if total is None else total + step
    delta = mean_step(total, value, inner_rates[1], inner_decays[1])
    new_moment, new_weight = outer_step(value, delta, moment[...])
    delta_out[...] = delta
    moment_new[...] = new_moment
    master[...] = new_weight
    copy[...] = new_weight.astype(low_type)


def keyvalue_update(place, own, other, first, second, weight, moment):
    rows, kinds, columns = weight.shape
    flat = kinds * columns
    size = math.gcd(flat, 80)
    table = np.zeros((2, flat, PACK), np.float32)
    for half in range(2):
        for kind in range(kinds):
            for spot in range(HEAD_WIDTH):
                table[half, kind * columns + half * HEAD_WIDTH + spot, (HEADS + kind) * HEAD_WIDTH + spot] = 1.0
    turn = lambda value: jnp.moveaxis(value, -3, -1).reshape(value.shape[:-3] + (flat, rows))
    back = lambda value: jnp.moveaxis(value.reshape(value.shape[:-2] + (kinds, columns, rows)), -1, -3)
    states = [turn(value) for value in (first, second, weight, moment)]
    plane = pl.BlockSpec((size, rows), lambda i, p: (i, 0))
    stack = pl.BlockSpec((REPLICA_GROUPS, size, rows), lambda i, p: (0, i, 0))
    pick = pl.BlockSpec((size, PACK), lambda i, p: (i, 0))
    wide = jax.ShapeDtypeStruct((REPLICA_GROUPS, flat, rows), f32)
    flat_shape = lambda dtype: jax.ShapeDtypeStruct((flat, rows), dtype)
    *outs, gains = pl.pallas_call(
        keyvalue_update_kernel,
        grid_spec=pltpu.PrefetchScalarGridSpec(
            num_scalar_prefetch=1,
            grid=(flat // size,),
            in_specs=[resident((rows, PACK))] * (REPLICA_GROUPS + 1)
            + [
                pl.BlockSpec((None, rows, PACK), lambda i, p, k=k: (k, 0, 0), pipeline_mode=pl.Buffered(1))
                for k in range(REPLICA_GROUPS - 1)
            ]
            + [pick, pick, resident((8, PACK)), stack, stack, plane, plane],
            out_specs=[stack, stack, plane, plane, plane, plane]
            + [pl.BlockSpec((REPLICA_GROUPS, 8, rows), lambda i, p: (0, 0, 0))],
        ),
        out_shape=[wide, wide, flat_shape(f32), flat_shape(f32), flat_shape(f32), flat_shape(low_type)]
        + [jax.ShapeDtypeStruct((REPLICA_GROUPS, 8, rows), f32)],
        compiler_params=params(),
        cost_estimate=cost(0, rows * flat * 90),
        name="keyvalue_update",
    )(
        place,
        *own,
        other[0],
        *[other[1]] * (REPLICA_GROUPS - 1),
        jnp.asarray(table[0], low_type),
        jnp.asarray(table[1], low_type),
        jnp.asarray(gains_selector(), low_type),
        *states,
    )
    return [back(value) for value in outs], gains[:, :2]


def optimize(weight, grad, first, second, moment, rate, decay):
    first_new, second_new, step = adam_step(grad, first, second, lambda value: 1.0 / value)
    delta = mean_step(jnp.sum(step, axis=0), weight, rate, decay)
    moment_new, weight_new = outer_step(weight, delta, moment)
    return (first_new, second_new, delta, moment_new, weight_new, weight_new.astype(low_type))


def doc_layout(lengths, token_length):
    ends = jnp.cumsum(lengths)
    starts = ends - lengths
    places = jnp.arange(token_length, dtype=jnp.int32)
    segment = jnp.sum((places[:, None] >= ends[None, :]).astype(jnp.int32), axis=1)
    member = (segment[:, None] == jnp.arange(lengths.shape[0], dtype=jnp.int32)[None, :]).astype(
        jnp.int32
    )
    offset = jnp.sum(member * starts[None, :], axis=1)
    return offset, places - offset


def rope_tables(position):
    half = HEAD_WIDTH // 2
    frequency = rope_base ** (-2.0 * jnp.arange(half, dtype=f32) / HEAD_WIDTH)
    angle = position.astype(f32)[:, None] * frequency[None, :]
    cosine, sine = jnp.cos(angle), jnp.sin(angle)
    gap = jnp.zeros((angle.shape[0], HALF - half), f32)
    return (
        jnp.concatenate([cosine, gap, cosine, gap], axis=1),
        jnp.concatenate([-sine, gap, sine, gap], axis=1),
    )


def norm_inverse(value):
    return lax.rsqrt(jnp.mean(value * value, axis=-1, keepdims=True) + epsilon)


def norm_backward(value, inverse, gain, grad_normed):
    scaled = gain * grad_normed
    return inverse * scaled - value * inverse**3 * jnp.mean(scaled * value, axis=-1, keepdims=True)


def per_device(
    tokens,
    cotangent,
    doc_lengths,
    query_weight,
    keyvalue_weight_full,
    output_weight,
    gating_weight,
    down_weight,
    norm_gains,
    first_query,
    keyvalue_first_moment,
    first_output,
    first_gating,
    first_down,
    first_gains,
    second_query,
    keyvalue_second_moment,
    second_output,
    second_gating,
    second_down,
    second_gains,
    moment_query,
    keyvalue_outer_momentum,
    moment_output,
    moment_gating,
    moment_down,
    moment_gains,
):
    ring = lax.axis_size("ring")
    spot = lax.axis_index("ring")
    side = lax.axis_index("pair")
    near = side == 0
    rows = query_weight.shape[0]
    width = tokens.shape[1]
    local_rows = tokens.shape[0]
    sequence = local_rows * lax.axis_size("tensor")
    plane = ("pair", "tensor")
    per_group = ring // REPLICA_GROUPS
    direct = per_group == 1 and (2 * rows) % LANES == 0
    zero = jnp.zeros_like(spot)
    mine = side * lax.axis_size("tensor") + lax.axis_index("tensor")
    place = jnp.stack([spot if direct else zero, side, spot if direct else zero, mine])
    blocks = ring if direct else 1
    hops = [1, 3, 2]

    def swap(value):
        return lax.ppermute(value, "pair", [(0, 1), (1, 0)])

    def across(value, bit):
        count = lax.axis_size("tensor")
        return lax.ppermute(value, "tensor", [(i, i ^ bit) for i in range(count)])

    def add(left, right):
        return (left.astype(f32) + right.astype(f32)).astype(low_type)

    def core_stage(kept, sent):
        shape = (2, 2, local_rows, width)
        kept, other = kept.reshape(shape), across(sent, 1).reshape(shape)
        cut = local_rows // 2
        spans = [
            (slice(None), 0, slice(None, cut)),
            (slice(None), 1, slice(None, cut)),
            (0, slice(None), slice(cut, None)),
            (1, slice(None), slice(cut, None)),
        ]
        return [add(kept[span], other[span]) for span in spans]

    def chip_send(parts):
        return across(parts[1], 2), swap(parts[3])

    def chip_stage(parts, *earlier, came=None):
        by_x, by_y = after(came or chip_send(parts), *earlier)
        return add(parts[0], by_x), add(parts[2], by_y)

    def last_send(parts):
        return swap(parts[0][1]), across(parts[1][1], 2)

    def last_stage(parts, *earlier, came=None):
        one, two = parts
        by_y, by_x = after(came or last_send(parts), *earlier)
        return jnp.concatenate(
            [one[0].astype(f32) + by_y.astype(f32), two[0].astype(f32) + by_x.astype(f32)], axis=0
        )

    def hop(value, step):
        return lax.ppermute(value, "ring", [(i, (i + step) % ring) for i in range(ring)])

    def halves(kept, sent, other=None):
        other = swap(sent) if other is None else other
        return jnp.concatenate([jnp.where(near, kept, other), jnp.where(near, other, kept)], axis=0)

    def gather(shard):
        return lax.all_gather(shard, "ring", axis=0, tiled=True)

    def gather_hops(shard):
        if not direct:
            return [gather(shard)]
        found = [shard] + [None] * (ring - 1)
        for step in hops:
            found[step] = hop(shard, step)
        return found

    def relay(found):
        if not direct:
            return [gather(found[0])] if found[0].shape[0] == 2 * rows else found
        return found + [hop(found[-1], 1)]

    def gather_first(value):
        cut = local_rows // 2
        return value, across(value[:cut], 2), swap(value[cut:])

    def gather_second(parts):
        value, by_x, by_y = parts
        cut = local_rows // 2
        one = jnp.stack([value[:cut], by_x])
        two = jnp.stack([value[cut:], by_y])
        return one, two, swap(one), across(two, 2)

    def gather_pieces(parts):
        one, two, one_y, two_x = parts
        pieces = {(0, 0, 0): one[0], (0, 1, 0): one[1], (0, 0, 1): two[0], (1, 0, 1): two[1]}
        pieces |= {(1, 0, 0): one_y[0], (1, 1, 0): one_y[1], (0, 1, 1): two_x[0], (1, 1, 1): two_x[1]}
        early = across(jnp.concatenate([one, two], axis=0), 1)
        late_one, late_two = across(one_y, 1), across(two_x, 1)
        far = {(0, 0, 0): early[0], (0, 1, 0): early[1], (0, 0, 1): early[2], (1, 0, 1): early[3]}
        far |= {(1, 0, 0): late_one[0], (1, 1, 0): late_one[1], (0, 1, 1): late_two[0], (1, 1, 1): late_two[1]}
        found = []
        for by_y in range(2):
            for by_x in range(2):
                for group in (pieces, far):
                    found += [group[by_y, by_x, 0], group[by_y, by_x, 1]]
        return jnp.concatenate(found, axis=0)

    def gather_last(parts):
        one, two, one_y, two_x = parts
        ones = [one[0], one[1], one_y[0], one_y[1]]
        twos = [two[0], two_x[0], two[1], two_x[1]]
        mine = jnp.concatenate([half for pair in zip(ones, twos) for half in pair], axis=0)
        other = across(mine, 1)
        found = []
        for start in range(0, mine.shape[0], local_rows):
            found += [mine[start : start + local_rows], other[start : start + local_rows]]
        return jnp.concatenate(found, axis=0)

    def sides(grads):
        if direct:
            return grads[1::2], grads[0::2]
        whole = grads[0].reshape(ring, 2, rows, -1)
        return (lax.dynamic_index_in_dim(whole, 1 - side, 1, False), lax.dynamic_index_in_dim(whole, side, 1, False))

    def deliver(grads):
        if not direct:
            whole = lax.all_to_all(grads, "ring", split_axis=0, concat_axis=0, tiled=True).astype(f32)
            whole = whole.reshape((REPLICA_GROUPS, per_group) + whole.shape[1:])
            whole = jnp.sum(whole, axis=1).astype(low_type)
            return [whole[k] for k in range(REPLICA_GROUPS)]
        found = [grads[0]] + [None] * (ring - 1)
        for step in hops:
            found[step] = hop(grads[step], -step)
        return found

    def tensor_sum(value):
        count = lax.axis_size("tensor")
        bit = 1
        while bit < count:
            value = value + across(value, bit)
            bit *= 2
        return value

    tokens_all = lax.all_gather(tokens, plane, axis=0, tiled=True)

    flat = HEADS * HEAD_WIDTH
    query_halves = [query_weight[:, :flat], query_weight[:, flat:]]
    pair_halves = [
        keyvalue_weight_full[:, :, :HEAD_WIDTH].reshape(rows, 2 * HEAD_WIDTH),
        keyvalue_weight_full[:, :, HEAD_WIDTH:].reshape(rows, 2 * HEAD_WIDTH),
    ]
    gain_columns = jnp.concatenate(
        [norm_gains.T, jnp.zeros((rows, PACK - flat - 2 * HEAD_WIDTH - 2), f32)], axis=1
    )
    packed = [
        jnp.concatenate([q, p, gain_columns], axis=1).astype(low_type)
        for q, p in zip(query_halves, pair_halves)
    ]
    output_low = output_weight.astype(low_type)
    output_parts = [output_low[:, :flat], output_low[:, flat:]]
    pick = lambda parts: (jnp.where(near, parts[0], parts[1]), jnp.where(near, parts[1], parts[0]))
    attention_shard = halves(*pick(packed))
    attention_blocks = gather_hops(attention_shard)
    output_kept, output_sent = pick(output_parts)
    output_came = swap(after(output_sent, attention_shard))
    output_shard = halves(output_kept, output_sent, output_came)
    output_blocks = gather_hops(after(output_shard, attention_blocks[1:2]))

    feed_parts = pack_feed(after(place, attention_shard), gating_weight, down_weight)
    tokens_all = after(tokens_all, feed_parts)
    kept, sent = feed_parts[: len(CHUNKS)], feed_parts[len(CHUNKS) :]
    feed_shards, came = [], []
    last = output_came
    for a, b in zip(kept, sent):
        came.append(swap(after(b, last)))
        last = halves(a, b, came[-1])
        feed_shards.append(last)
    one = relay([after(feed_shards[0], attention_blocks)])
    cotangent_parts = gather_first(after(cotangent, tokens_all))

    other_lengths = swap(doc_lengths)
    lengths = [jnp.where(near, doc_lengths[0], other_lengths[0]), jnp.where(near, other_lengths[0], doc_lengths[0])]
    layouts = [doc_layout(value, sequence) for value in lengths]
    starts = jnp.broadcast_to(
        jnp.concatenate([value[0] for value in layouts])[None, :], (8, 2 * sequence)
    ).astype(jnp.int32)
    cosine, sine = rope_tables(jnp.concatenate([value[1] for value in layouts]))

    cosine = after(cosine, came[0])
    normed_one, heads, gains, wide = project(place, tokens_all, attention_blocks, cosine, sine)
    gain_one, gain_two = gains[0], gains[1]
    heads = after(heads, cotangent_parts)
    mixed, totals, *partial = attend(place, heads, starts, output_blocks, sequence)
    cotangent_parts = gather_second(cotangent_parts)
    partial = after(partial, cotangent_parts, one)
    one = relay(one)
    parts = after(core_stage(*partial), one)
    one = relay(one)
    cotangent_all = gather_last(after(cotangent_parts, parts))
    parts = after(chip_stage(parts, one), cotangent_all)
    two = relay([after(feed_shards[1], one)])
    attention = last_stage(parts, two)

    hidden = tokens.astype(f32)
    inverse_one = norm_inverse(hidden)
    hidden_one = hidden + attention
    inverse_two = norm_inverse(hidden_one)
    normed_two = (hidden_one * inverse_two * gain_two).astype(low_type)
    two = relay(two)
    normed_parts = after(gather_second(gather_first(normed_two)), two)
    two = relay(two)
    normed_two_all = gather_pieces(normed_parts)
    hid, grad_pair = feed(place, normed_two_all, cotangent_all, one)
    theirs, mine = sides(weight_grad(place, blocks, [(normed_two_all, grad_pair), (cotangent_all, hid)]))
    theirs_one = deliver(theirs)
    others_one = [swap(theirs_one[0])]
    normed_late = after(normed_two_all, theirs[0])
    hid_two, grad_pair_two = feed(place, normed_late, cotangent_all, two)
    partial = spread(place, after([grad_pair, grad_pair_two], others_one), [one, two], 0)
    partial = after(partial, theirs_one)
    others_one += [swap(after(value, partial)) for value in theirs_one[1:3]]
    parts = core_stage(*partial)
    mine_one = deliver(after(mine, partial))
    theirs, mine_later = sides(
        weight_grad(place, blocks, [(normed_two_all, after(grad_pair_two, *parts)), (cotangent_all, hid_two)])
    )
    parts = after(chip_stage(parts, theirs[0]), others_one, mine_one[1:2])
    theirs_two = deliver(theirs)
    feed_partial = spread(place, after([hid, hid_two], *parts), [one, two], 2)
    grad_normed_two = last_stage(parts, *feed_partial)

    grad_hidden_one = cotangent.astype(f32) + norm_backward(
        hidden_one, inverse_two, gain_two, grad_normed_two
    )
    grad_gain_two = jnp.sum(grad_normed_two * hidden_one * inverse_two, axis=0)
    grad_hidden_all = lax.all_gather(grad_hidden_one.astype(low_type), plane, axis=0, tiled=True)
    feed_parts = chip_stage(core_stage(*after(feed_partial, grad_hidden_one)))
    feed_came = last_send(feed_parts)
    grad_hidden_all = after(grad_hidden_all, theirs_two, mine_one[3:], feed_came)
    mine_two = deliver(after(mine_later, grad_hidden_all))
    others_one.append(swap(after(theirs_one[3], grad_hidden_all)))
    others_two = [swap(after(value, grad_hidden_all)) for value in theirs_two[:2]]

    grad_query, grad_pair = attend_grad(
        place, grad_hidden_all, heads, totals, starts, cosine, sine, output_blocks, sequence
    )
    grad_heads = jnp.concatenate([grad_query, grad_pair], axis=1)
    *partial, gain_sums = project_grad(place, grad_heads, tokens_all, wide)
    grad_gains = jnp.stack([jnp.sum(gain_sums, axis=0), grad_gain_two], axis=0)
    grad_gains = jnp.concatenate([grad_gains, jnp.zeros((6, width), f32)], axis=0).astype(low_type)
    partial = after(partial, mine_one, others_one, others_two, mine_two[1:2])
    parts = core_stage(*partial)
    others_two += [swap(after(value, partial)) for value in theirs_two[2:]]
    theirs, mine = sides(
        weight_grad(
            place,
            blocks,
            [
                (normed_one, after(grad_heads, *parts)),
                (grad_gains, jnp.asarray(gains_selector(), low_type)),
                (grad_hidden_all, mixed),
            ],
            gradient_selectors(),
        )
    )
    parts = after(chip_stage(parts, theirs[0]), mine_two, others_two[:3])
    theirs_last = deliver(theirs)
    came = last_send(parts)
    grad_normed_one = last_stage(parts, came=came)
    mine_one, others_one, mine_two, others_two, theirs_last = after(
        (mine_one, others_one, mine_two, others_two, theirs_last), came
    )
    mine_last = deliver(after(mine, theirs_last))
    others_last = [swap(theirs_last[0]), swap(jnp.stack(theirs_last[1:]))]
    block_output = (hidden_one + last_stage(feed_parts, came=feed_came)).astype(low_type)

    token_grad = (
        grad_hidden_one + norm_backward(hidden, inverse_one, gain_one, grad_normed_one)
    ).astype(low_type)

    updated = feed_update(
        place,
        [mine_one, mine_two],
        [others_one, others_two],
        (first_gating, second_gating, gating_weight, moment_gating),
        (first_down, second_down, down_weight, moment_down),
    )
    mine_last = after(mine_last, updated[0])
    attention_updated = attention_update(
        place,
        mine_last,
        others_last,
        (first_query, second_query, query_weight, moment_query),
        (first_output, second_output, output_weight, moment_output),
    )
    qry, out = attention_updated[:6], attention_updated[6:]
    kvl, gains_total = keyvalue_update(
        place,
        mine_last,
        others_last,
        keyvalue_first_moment,
        keyvalue_second_moment,
        keyvalue_weight_full,
        keyvalue_outer_momentum,
    )
    gains_total = tensor_sum(gains_total)
    gns = optimize(
        norm_gains, gains_total, first_gains, second_gains, moment_gains, inner_rates[5], inner_decays[5]
    )
    gat = updated[:6]
    dwn = updated[6:]
    return (block_output, token_grad, *qry, *kvl, *out, *gat, *dwn, *gns)


def solution(mesh):
    shape = (mesh.shape["dp"] // 2, 2, mesh.shape["tensor"])
    mesh = Mesh(mesh.devices.reshape(shape), ("ring", "pair", "tensor"))
    dp = ("ring", "pair")
    matrix = P(dp, "tensor")
    pair = P(dp, None, "tensor")
    stack = P(None, dp, "tensor")
    stack_pair = P(None, dp, None, "tensor")
    tokens = P(("ring", "pair", "tensor"), None)
    gains = P(None, dp)
    stack_gains = P(None, None, dp)
    weights = (matrix, pair, matrix, pair, matrix, gains)
    states = (stack, stack_pair, stack, stack_pair, stack, stack_gains)
    outs = []
    for weight, state in zip(weights, states):
        outs += [state, state, weight, weight, weight, weight]
    return jax.shard_map(
        per_device,
        mesh=mesh,
        in_specs=(tokens, tokens, P(dp, None), *weights, *states, *states, *weights),
        out_specs=(tokens, tokens, *outs),
        check_vma=False,
    )
```
